256 devices in a mesh: ctx: 128 (over y, z, x_lo, core), head: 2 (over x_hi).
Axes of the slice: x: 4 (x_hi: 2, x_lo: 2; x = x_hi * 2 + x_lo), y: 4, z: 8, core: 2. Of those that a mesh axis runs over, the one named last changes fastest.
Arguments:
- hidden_in: bfloat16 [16384, 4096], P('ctx'), may hold values from -24 to 24
- queries: bfloat16 [16384, 2048], P('ctx', 'head'), may hold values from -32 to 32
- key_weight: bfloat16 [4096, 512], P('ctx', 'head'), may hold values from -0.09375 to 0.09375
- value_weight: bfloat16 [4096, 512], P('ctx', 'head'), may hold values from -0.09375 to 0.09375
- seg_ids: int32 [16384], replicated, may hold values from 0 to 31, never falling along the last dimension, each value on 1 to 4096 neighbouring positions
- grad_out: bfloat16 [16384, 2048], P('ctx', 'head'), may hold values from -6 to 6
Outputs:
- attended: bfloat16 [16384, 2048], P('ctx', 'head')
- grad_queries: bfloat16 [16384, 2048], P('ctx', 'head')
- grad_hidden: bfloat16 [16384, 4096], P('ctx')
- grad_key_weight: float32 [4096, 512], P('ctx', 'head')
- grad_value_weight: float32 [4096, 512], P('ctx', 'head')
The draws below stay inside these ranges and needn't reach their ends.
All inputs are finite; a program needn't handle non-finite values.
Results may differ from the reference program's by a relative error of at most 0.029.
Values may be sent and summed in bfloat16 or wider, within the bound.
A program may use at most 64 MiB of HBM per device.

```python
import math
import jax
import jax.numpy as jnp
import numpy as np
from jax import lax

D = 4096
HD = 128
QH = 16
KVH = 4
WINDOW = 2048
TOK_DEV = 128
SEQ = 16384
DOCS = 32
LONGEST = 4096


def draw_queries(key, part):
    key = jax.random.fold_in(key, 11)
    base = jax.random.normal(key, (SEQ, QH * HD), jnp.float32)
    return jnp.clip(base, -6.0, 6.0).astype(jnp.bfloat16)


def with_spikes(values, stream_key, source, target, blocks, factor):
    owner, partner = [(jnp.arange(values.shape[dim]) // (values.shape[dim] // blocks)).reshape([-1 if axis == dim else 1 for axis in range(values.ndim)]) for dim in (source, target)]
    chosen = jax.random.permutation(stream_key, blocks)[partner]
    strong = (owner == chosen) | (owner == (partner + blocks // 2) % blocks)
    return jnp.where(strong, factor * values, values)


def block_levels(own_key, extent, cuts, smallest, largest):
    loudness, own = 1.0, jax.random.fold_in(own_key, 6)
    for dim, parts in cuts:
        heights = jnp.exp(jax.random.uniform(jax.random.fold_in(own, dim), (parts,), jnp.float32, smallest / len(cuts), largest / len(cuts)))
        loudness = loudness * jnp.repeat(heights, extent[dim] // parts).reshape([-1 if axis == dim else 1 for axis in range(len(extent))])
    return loudness


def split_up(count, total, reach, lean):
    weights = [(1 << 20) // math.isqrt(rank ** lean) + 1 for rank in range(2, count + 1)]
    surplus, holding = total - reach - (count - 1), [1] * (count - 1)
    while surplus > 0:
        candidates = [i for i in range(count - 1) if holding[i] < reach]
        whole, remaining = sum([weights[i] for i in candidates]), surplus
        for i in candidates:
            more = min(reach - holding[i], max(1, remaining * weights[i] // whole), surplus)
            holding[i] = holding[i] + more
            surplus = surplus - more
    return np.array([reach] + holding)


def uneven_parts(key, amount, total, limit, slope):
    if amount == 2:
        one = jax.random.randint(key, (), max(1, total - limit), min(limit, total - 1) + 1)
        return jnp.stack([one, total - one])
    tallies = jnp.asarray(split_up(amount, total, limit, slope), jnp.int32)
    twos = (amount - 1) // 2
    giver, sink = tallies[1:1 + 2 * twos:2], tallies[2:2 + 2 * twos:2]
    room = jnp.minimum(giver - 1, limit - sink)
    moved = jax.random.randint(jax.random.fold_in(key, 1), (twos,), 0, 1 << 20) % (room + 1)
    tallies = tallies.at[1:1 + 2 * twos:2].set(giver - moved).at[2:2 + 2 * twos:2].set(sink + moved)
    return tallies[jax.random.permutation(jax.random.fold_in(key, 2), amount)]


def bell_draw(stream_key, shape, deviation, reach, shards=(), kind=jnp.bfloat16):
    array = jax.random.normal(stream_key, shape, jnp.float32) * deviation
    if len(shards) > 0:
        array = block_levels(stream_key, shape, shards, -0.22, 0.18) * array
    return jnp.clip(array, min=-reach, max=reach).astype(kind)


def noise_with(key, shape, deviation, limit, shards, heavy, kind=jnp.bfloat16):
    drawn = deviation * jax.random.normal(key, shape, jnp.float32)
    if shards:
        drawn = drawn * block_levels(key, shape, shards, -0.22, 0.18)
    return jnp.clip(with_spikes(drawn, jax.random.fold_in(key, 3), *heavy), -limit, limit).astype(kind)


def setup_inputs(seed: int = 0) -> dict:
    arg_keys = jax.random.split(jax.random.key(seed), 7)
    return {
        "hidden_in": noise_with(arg_keys[0], (SEQ, D), 1.0, 24.0, ((0, 128),), (0, 1, 128, 5.5)),
        "queries": draw_queries(jax.random.fold_in(arg_keys[6], 71), 0),
        "key_weight": bell_draw(arg_keys[2], (D, KVH * HD), D ** -0.5, 0.09375, ((0, 128), (1, 2))),
        "value_weight": bell_draw(arg_keys[3], (D, KVH * HD), D ** -0.5, 0.09375, ((0, 128), (1, 2))),
        "seg_ids": jnp.searchsorted(jnp.cumsum(uneven_parts(arg_keys[4], DOCS, SEQ, LONGEST, 2)), jnp.arange(SEQ), side="right").astype(jnp.int32),
        "grad_out": bell_draw(arg_keys[5], (SEQ, QH * HD), 1.0, 6.0, ((0, 128), (1, 2))),
    }


NEG = -1e+30

def rotary_tables(positions, head_width):
    halfway = head_width // 2
    frequency = 10000.0 ** (-(jnp.arange(halfway, dtype=jnp.float32) * 2.0 / head_width))
    angles = positions.astype(jnp.float32)[:, None] * frequency[None, :]
    return (jnp.cos(angles)[:, None, :], jnp.sin(angles)[:, None, :])

def rotate(vectors, cosine, sine_table):
    halfway = vectors.shape[-1] // 2
    lower_half = vectors[..., :halfway]
    upper_half = vectors[..., halfway:]
    return jnp.concatenate([lower_half * cosine - upper_half * sine_table, upper_half * cosine + lower_half * sine_table], axis=-1)

def unrotate(gradient, cosine, sine_table):
    halfway = gradient.shape[-1] // 2
    lower_half = gradient[..., :halfway]
    upper_half = gradient[..., halfway:]
    return jnp.concatenate([lower_half * cosine + upper_half * sine_table, upper_half * cosine - lower_half * sine_table], axis=-1)

def round_low(values_in):
    return lax.optimization_barrier(values_in.astype(jnp.bfloat16)).astype(jnp.float32)

def reference(hidden_in, queries, key_weight, value_weight, seg_ids, grad_out):
    seq_len = hidden_in.shape[0]
    group = QH // KVH
    scaling = 1.0 / math.sqrt(HD)
    positions = jnp.arange(seq_len, dtype=jnp.int32)
    cosine, sine_table = rotary_tables(positions, HD)
    key_raw = jnp.dot(hidden_in, key_weight, preferred_element_type=jnp.float32).reshape(seq_len, KVH, HD)
    key_rows = rotate(key_raw, cosine, sine_table).astype(jnp.bfloat16)
    value_rows = jnp.dot(hidden_in, value_weight, preferred_element_type=jnp.float32).astype(jnp.bfloat16).reshape(seq_len, KVH, HD)
    key_padded = jnp.pad(key_rows.astype(jnp.float32), ((WINDOW, 0), (0, 0), (0, 0)))
    value_padded = jnp.pad(value_rows.astype(jnp.float32), ((WINDOW, 0), (0, 0), (0, 0)))
    seg_padded = jnp.concatenate([jnp.full((WINDOW,), -1, jnp.int32), seg_ids.astype(jnp.int32)])
    span_len = WINDOW + TOK_DEV
    gap = jnp.arange(TOK_DEV, dtype=jnp.int32)[:, None] + WINDOW - jnp.arange(span_len, dtype=jnp.int32)[None, :]

    def one_block(carry, start):
        key_acc, value_acc = carry
        query_blk = lax.dynamic_slice_in_dim(queries, start, TOK_DEV, 0).astype(jnp.float32).reshape(TOK_DEV, KVH, group, HD)
        out_grad = lax.dynamic_slice_in_dim(grad_out, start, TOK_DEV, 0).astype(jnp.float32).reshape(TOK_DEV, KVH, group, HD)
        key_blk = lax.dynamic_slice_in_dim(key_padded, start, span_len, 0)
        value_blk = lax.dynamic_slice_in_dim(value_padded, start, span_len, 0)
        key_seg = lax.dynamic_slice_in_dim(seg_padded, start, span_len, 0)
        query_seg = lax.dynamic_slice_in_dim(seg_ids.astype(jnp.int32), start, TOK_DEV, 0)
        allowed = (query_seg[:, None] == key_seg[None, :]) & (gap >= 0) & (gap < WINDOW)
        scores = jnp.einsum('qkgd,lkd->kgql', query_blk, key_blk) * scaling
        scores = jnp.where(allowed[None, None], scores, NEG)
        row_max = lax.optimization_barrier(jnp.max(scores, axis=-1))
        expo = jnp.where(allowed[None, None], jnp.exp(scores - row_max[..., None]), 0.0)
        row_sum = lax.optimization_barrier(jnp.sum(expo, axis=-1))
        mixed = jnp.einsum('kgql,lkd->kgqd', round_low(expo), value_blk) / row_sum[..., None]
        mixed_low = mixed.astype(jnp.bfloat16)
        log_total = row_max + jnp.log(row_sum)
        delta = lax.optimization_barrier(jnp.sum(out_grad.transpose(1, 2, 0, 3) * mixed_low.astype(jnp.float32), axis=-1))
        probs = jnp.where(allowed[None, None], jnp.exp(scores - log_total[..., None]), 0.0)
        dprobs = jnp.einsum('qkgd,lkd->kgql', out_grad, value_blk)
        dscores = probs * (dprobs - delta[..., None])
        probs_low = round_low(probs)
        dscores_low = round_low(dscores)
        query_grad = jnp.einsum('kgql,lkd->kgqd', dscores_low, key_blk) * scaling
        key_part = jnp.einsum('kgql,qkgd->lkd', dscores_low, query_blk) * scaling
        value_part = jnp.einsum('kgql,qkgd->lkd', probs_low, out_grad)
        key_acc = lax.dynamic_update_slice_in_dim(key_acc, lax.dynamic_slice_in_dim(key_acc, start, span_len, 0) + key_part, start, 0)
        value_acc = lax.dynamic_update_slice_in_dim(value_acc, lax.dynamic_slice_in_dim(value_acc, start, span_len, 0) + value_part, start, 0)
        attended_blk = mixed_low.transpose(2, 0, 1, 3).reshape(TOK_DEV, QH * HD)
        query_grad_blk = query_grad.astype(jnp.bfloat16).transpose(2, 0, 1, 3).reshape(TOK_DEV, QH * HD)
        return ((key_acc, value_acc), (attended_blk, query_grad_blk))
    starts = jnp.arange(0, seq_len, TOK_DEV, dtype=jnp.int32)
    zero_acc = jnp.zeros((seq_len + WINDOW, KVH, HD), jnp.float32)
    (key_acc, value_acc), (attended_all, query_grads) = lax.scan(one_block, (zero_acc, zero_acc), starts)
    attended = attended_all.reshape(seq_len, QH * HD)
    grad_queries = query_grads.reshape(seq_len, QH * HD)
    key_grad = unrotate(key_acc[WINDOW:], cosine, sine_table).reshape(seq_len, KVH * HD).astype(jnp.bfloat16)
    value_grad = value_acc[WINDOW:].reshape(seq_len, KVH * HD).astype(jnp.bfloat16)
    grad_hidden = (jnp.dot(key_grad, key_weight.T, preferred_element_type=jnp.float32) + jnp.dot(value_grad, value_weight.T, preferred_element_type=jnp.float32)).astype(jnp.bfloat16)
    grad_key_weight = jnp.dot(hidden_in.T, key_grad, preferred_element_type=jnp.float32)
    grad_value_weight = jnp.dot(hidden_in.T, value_grad, preferred_element_type=jnp.float32)
    return (attended, grad_queries, grad_hidden, grad_key_weight, grad_value_weight)
```

```python
import functools
import math

import jax
import jax.numpy as jnp
from jax import lax
from jax.experimental import pallas as pl
from jax.experimental.pallas import tpu as pltpu
from jax.sharding import PartitionSpec as P

HD = 128
WINDOW = 2048
NEG = -1e30
MESH = pl.DeviceIdType.MESH
VM = pl.BlockSpec(memory_space=pltpu.VMEM)
ANY = pl.BlockSpec(memory_space=pl.ANY)
BF = jnp.bfloat16
F32 = jnp.float32
NY, NZ = 4, 8
DZ = (1, -1, 2, -2, 3, -3, 4)
DY = (1, -1, 2)


def coords():
    i = lax.axis_index("ctx")
    h = lax.axis_index("head")
    return i // 32, (i // 4) % 8, (i // 2) % 2, i % 2, h


def dev(y, z, x, c, h):
    return (((y % NY) * NZ + z % NZ) * 4 + x * 2 + c, h)


def plane_dev(p, x, c, h):
    return ((p % 32) * 4 + x * 2 + c, h)


def enter(partners):
    barrier = pltpu.get_barrier_semaphore()
    for partner in partners:
        pl.semaphore_signal(barrier, inc=1, device_id=partner, device_id_type=MESH)
    pl.semaphore_wait(barrier, len(partners))


def push(src, dst, send, recv, to):
    copy = pltpu.make_async_remote_copy(
        src_ref=src, dst_ref=dst, send_sem=send, recv_sem=recv, device_id=to, device_id_type=MESH
    )
    copy.start()
    return copy


def arrived(dst, send, recv, to):
    pltpu.make_async_remote_copy(
        src_ref=dst, dst_ref=dst, send_sem=send, recv_sem=recv, device_id=to, device_id_type=MESH
    ).wait_recv()


def params(cid):
    return pltpu.CompilerParams(
        collective_id=cid, has_side_effects=True, vmem_limit_bytes=56 * 2**20
    )


def gather_kernel(
    wk, wv, hid, q, do, w, hid2, q2, do2, loc, core_s, core_r, x_s, x_r, send, recv
):
    y, z, x, c, h = coords()
    other = dev(y, z, x, 1 - c, h)
    mate = dev(y, z, 1 - x, c, h)
    ys = [dev(y + d, z, x, c, h) for d in DY]
    zs = [dev(y, z + d, x, c, h) for d in DZ]
    enter([other, mate] + ys + zs)
    rows = pl.ds(c * 32, 32)
    theirs = pl.ds(pl.multiple_of((1 - c) * HD, HD), HD)
    mine = pl.ds(pl.multiple_of(c * HD, HD), HD)
    theirs_q = pl.ds(pl.multiple_of((1 - c) * 512, 512), 512)
    mine_q = pl.ds(pl.multiple_of(c * 512, 512), 512)
    toks = pl.ds(pl.multiple_of(c * 128, 128), 128)
    moves = [
        (wk.at[:, theirs], wk.at[:, mine], w.at[y, z, x, rows, pl.ds(0, HD)]),
        (wv.at[:, theirs], wv.at[:, mine], w.at[y, z, x, rows, pl.ds(HD, HD)]),
        (q.at[:, theirs_q], q.at[:, mine_q], q2.at[toks]),
        (do.at[:, theirs_q], do.at[:, mine_q], do2.at[toks]),
        (hid, hid, hid2.at[toks]),
    ]
    crossing, local = [], []
    for n, (out, own, dst) in enumerate(moves):
        crossing.append(push(out, dst, core_s.at[n], core_r.at[n], other))
        copy = pltpu.make_async_copy(own, dst, loc.at[n])
        copy.start()
        local.append(copy)
    for n in range(2):
        crossing[n].wait_recv()
        local[n].wait()
    pair = push(w.at[y, z, x], w.at[y, z, x], x_s, x_r, mate)
    pair.wait_recv()

    def slot(yy, zz):
        return recv.at[(yy % NY) * NZ + zz % NZ]

    def wait_plane(yy, zz):
        arrived(w.at[yy % NY, zz % NZ], send.at[0], slot(yy, zz), other)

    @pl.when(c == 0)
    def _():
        sent = []

        def go(yy, zz, to):
            ref = w.at[yy % NY, zz % NZ]
            sent.append(push(ref, ref, send.at[len(sent)], slot(yy, zz), to))

        for to in zs:
            go(y, z, to)
        for to in ys:
            go(y, z, to)
        for d in DZ:
            wait_plane(y, z + d)
            for to in ys:
                go(y, z + d, to)
        for d in (0,) + DZ:
            for e in DY:
                wait_plane(y + e, z + d)
        for copy in sent:
            copy.wait_send()

    @pl.when(c == 1)
    def _():
        sent = []

        def go(yy, zz, to):
            ref = w.at[yy % NY, zz % NZ]
            sent.append(push(ref, ref, send.at[len(sent)], slot(yy, zz), to))

        for to in ys:
            go(y, z, to)
        up, down = zs[0], zs[1]
        for s in range(4):
            for n, e in enumerate((0,) + DY):
                if s == 0:
                    if e:
                        wait_plane(y + e, z)
                    go(y + e, z, up)
                    go(y + e, z, down)
                    continue
                wait_plane(y + e, z - s)
                if s < 3 or n < 2:
                    go(y + e, z - s, up)
                wait_plane(y + e, z + s)
                if s < 3 or n >= 2:
                    go(y + e, z + s, down)
        for e in (0,) + DY:
            wait_plane(y + e, z + 4)
        for copy in sent:
            copy.wait_send()

    pair.wait_send()
    for n in range(5):
        crossing[n].wait_send()
        if n >= 2:
            crossing[n].wait_recv()
            local[n].wait()


def gather_weights(wk, wv, hid, q, do):
    dma = pltpu.SemaphoreType.DMA
    return pl.pallas_call(
        gather_kernel,
        out_shape=(
            jax.ShapeDtypeStruct((NY, NZ, 2, 64, 256), BF),
            jax.ShapeDtypeStruct((256, 4096), BF),
            jax.ShapeDtypeStruct((256, 512), BF),
            jax.ShapeDtypeStruct((256, 512), BF),
        ),
        in_specs=[VM, VM, ANY, ANY, ANY],
        out_specs=(VM, ANY, ANY, ANY),
        scratch_shapes=[dma((5,)), dma((5,)), dma((5,)), dma, dma, dma((31,)), dma((32,))],
        compiler_params=params(0),
        name="gather",
    )(wk, wv, hid, q, do)


def window_kernel(kv, w, win, wo, loc, core_s, core_r, z_s, z_r, x_s, x_r):
    y, z, x, c, h = coords()
    p = y * NZ + z
    other = dev(y, z, x, 1 - c, h)
    mate = dev(y, z, 1 - x, c, h)
    near = [plane_dev(p + d, x, c, h) for d in (1, -1, 2, -2, 4, -4)]
    enter([other, mate] + near)
    up1, up2, up4 = near[0], near[2], near[4]
    sent = [
        push(kv, win.at[3, x], z_s.at[0], z_r.at[3], up1),
        push(kv, win.at[2, x], z_s.at[1], z_r.at[2], up2),
        push(kv, win.at[0, x], z_s.at[2], z_r.at[0], up4),
    ]
    own = pltpu.make_async_copy(kv, win.at[4, x], loc)
    own.start()

    def across(k, src):
        j = 4 - x - k
        return push(src, win.at[k, x], x_s.at[j], x_r.at[j], mate)

    @pl.when(x == 0)
    def _():
        across(4, kv)

    weights = push(w, wo, core_s, core_r, other)

    def got(k):
        arrived(win.at[k, x], z_s.at[0], z_r.at[k], up1)

    got(3)
    across(3, win.at[3, x])
    got(2)
    sent.append(push(win.at[2, x], win.at[1, x], z_s.at[3], z_r.at[1], up1))
    across(2, win.at[2, x])
    got(0)

    @pl.when(x == 1)
    def _():
        across(0, win.at[0, x])

    got(1)
    across(1, win.at[1, x])
    for j in range(4):
        arrived(win.at[3 + x - j, 1 - x], x_s.at[j], x_r.at[j], mate)
    for copy in sent:
        copy.wait_send()
    for j in range(4):
        pltpu.make_async_remote_copy(
            src_ref=kv, dst_ref=win.at[4 - x - j, x], send_sem=x_s.at[j], recv_sem=x_r.at[j],
            device_id=mate, device_id_type=MESH,
        ).wait_send()
    own.wait()
    weights.wait()


def exchange_window(kv, w):
    dma = pltpu.SemaphoreType.DMA
    return pl.pallas_call(
        window_kernel,
        out_shape=(
            jax.ShapeDtypeStruct((5, 2, 256, 256), BF),
            jax.ShapeDtypeStruct(w.shape, BF),
        ),
        in_specs=[VM, ANY],
        out_specs=(VM, ANY),
        scratch_shapes=[dma, dma, dma, dma((4,)), dma((4,)), dma((4,)), dma((4,))],
        compiler_params=params(1),
        name="window",
    )(kv, w)


def attention_kernel(q2, do2, win, seg, att, gq, dkv, s_ref, acc):
    i = lax.axis_index("ctx")
    x = (i // 2) % 2
    chip = i // 2
    base = x * 256
    scaling = 1.0 / math.sqrt(HD)
    to2 = scaling * math.log2(math.e)
    acc[...] = jnp.zeros_like(acc)
    key_row = lax.broadcasted_iota(jnp.int32, (128, 128), 0)
    query_col = lax.broadcasted_iota(jnp.int32, (128, 128), 1)
    tilt = query_col - key_row
    nt = (((0,), (0,)), ((), ()))

    def dot(a, b):
        return jnp.dot(a, b, preferred_element_type=F32)

    for t in range(2):
        block = chip * 2 + t
        rows = pl.ds(t * 128, 128)
        q = jnp.concatenate([q2[rows, g * HD : (g + 1) * HD] for g in range(4)], axis=0)
        do = jnp.concatenate([do2[rows, g * HD : (g + 1) * HD] for g in range(4)], axis=0)
        q_t = q.T
        do_t = do.T
        seg_q = seg[pl.ds(block, 1), :]

        def keys_at(b):
            return pl.ds(pl.multiple_of(base + (b + t) * 128, 128), 128)

        def score(b, best):
            k = win[keys_at(b), 0:HD]
            index = block - 16 + b
            seg_k = seg[pl.ds(jnp.maximum(index, 0), 1), :]
            seg_k = jnp.where(index >= 0, seg_k, -1.0)
            seg_k = jnp.broadcast_to(seg_k, (128, 128)).T
            gap = tilt + (16 - b) * 128
            ok = (seg_k == seg_q) & (gap >= 0) & (gap < WINDOW)
            bias = jnp.where(ok, 0.0, NEG)
            s = dot(k, q_t) * to2 + jnp.concatenate([bias] * 4, axis=1)
            s_ref[pl.ds(pl.multiple_of(b * 128, 128), 128), :] = s
            return jnp.maximum(best, jnp.max(s, axis=0, keepdims=True))

        best = lax.fori_loop(0, 17, score, jnp.full((1, 512), NEG, F32))

        def mix(b, carry):
            total, out = carry
            where = pl.ds(pl.multiple_of(b * 128, 128), 128)
            e = jnp.exp2(s_ref[where, :] - best)
            s_ref[where, :] = e
            v = win[keys_at(b), HD : 2 * HD]
            out = out + lax.dot_general(v, e.astype(BF), nt, preferred_element_type=F32)
            return total + jnp.sum(e, axis=0, keepdims=True), out

        total, out = lax.fori_loop(
            0, 17, mix, (jnp.zeros((1, 512), F32), jnp.zeros((HD, 512), F32))
        )
        inverse = 1.0 / total
        low = (out * inverse).astype(BF)
        delta = jnp.sum(low.astype(F32) * do_t.astype(F32), axis=0, keepdims=True)
        for g in range(4):
            att[rows, g * HD : (g + 1) * HD] = low[:, g * HD : (g + 1) * HD].T

        def back(b, query_sum):
            where = pl.ds(pl.multiple_of(b * 128, 128), 128)
            k = win[keys_at(b), 0:HD]
            v = win[keys_at(b), HD : 2 * HD]
            probs = s_ref[where, :] * inverse
            dscores = probs * (dot(v, do_t) - delta)
            probs = probs.astype(BF)
            dscores = dscores.astype(BF)
            into = pl.ds(pl.multiple_of((b + t) * 128, 128), 128)
            acc[into, 0:HD] += dot(dscores, q)
            acc[into, HD : 2 * HD] += dot(probs, do)
            return query_sum + lax.dot_general(k, dscores, nt, preferred_element_type=F32)

        query_sum = lax.fori_loop(0, 17, back, jnp.zeros((HD, 512), F32))
        query_low = (query_sum * scaling).astype(BF)
        for g in range(4):
            gq[rows, g * HD : (g + 1) * HD] = query_low[:, g * HD : (g + 1) * HD].T

    def finish(b, _):
        src = pl.ds(pl.multiple_of(b * 128, 128), 128)
        dst = pl.ds(pl.multiple_of(base + b * 128, 128), 128)
        dkv[dst, 0:HD] = (acc[src, 0:HD] * scaling).astype(BF)
        dkv[dst, HD : 2 * HD] = acc[src, HD : 2 * HD].astype(BF)
        return 0

    lax.fori_loop(0, 18, finish, 0)


def attention(q2, do2, win, seg):
    return pl.pallas_call(
        attention_kernel,
        out_shape=(
            jax.ShapeDtypeStruct((256, 512), BF),
            jax.ShapeDtypeStruct((256, 512), BF),
            jax.ShapeDtypeStruct((2560, 256), BF),
        ),
        in_specs=[VM] * 4,
        out_specs=(VM,) * 3,
        scratch_shapes=[pltpu.VMEM((2176, 512), F32), pltpu.VMEM((2304, 256), F32)],
        compiler_params=pltpu.CompilerParams(vmem_limit_bytes=56 * 2**20),
        name="attention",
    )(q2, do2, win, seg)


def return_kernel(
    dkv, att2, gq2, cos, sin, kvg, kvo, att, gq,
    own, x_in, z_in, core_s, core_r, x_s, x_r, z_s, z_r, loc
):
    y, z, x, c, h = coords()
    p = y * NZ + z
    other = dev(y, z, x, 1 - c, h)
    mate = dev(y, z, 1 - x, c, h)
    near = [plane_dev(p + d, x, c, h) for d in (-1, 1, -2, 2, -4, 4)]
    enter([other, mate] + near)
    down1, down2, down4 = near[0], near[2], near[4]
    theirs = pl.ds(pl.multiple_of((1 - c) * 128, 128), 128)
    mine = pl.ds(pl.multiple_of(c * 128, 128), 128)
    cols = pl.ds(pl.multiple_of(c * 512, 512), 512)
    crossing = []
    for j in (3, 2, 1, 0):
        crossing.append(
            push(dkv.at[3 + x - j, 1 - x], x_in.at[j], x_s.at[j], x_r.at[j], mate)
        )
    waits = []
    for n, (src, dst) in enumerate(((att2, att), (gq2, gq))):
        waits.append(push(src.at[theirs], dst.at[:, cols], core_s.at[n], core_r.at[n], other))
        copy = pltpu.make_async_copy(src.at[mine], dst.at[:, cols], loc.at[n])
        copy.start()
        waits.append(copy)

    def merge(k, with_mate):
        if with_mate is None:
            own[k] = dkv[k, x]
        else:
            own[k] = (dkv[k, x].astype(F32) + x_in[with_mate].astype(F32)).astype(BF)

    @pl.when(x == 0)
    def _():
        merge(0, None)

    @pl.when(x == 1)
    def _():
        arrived(x_in.at[3], x_s.at[3], x_r.at[3], mate)
        merge(0, 3)

    sent = [push(own.at[0], z_in.at[0], z_s.at[0], z_r.at[0], down4)]
    for k in (1, 2, 3):
        j = 4 - x - k
        arrived(x_in.at[j], x_s.at[j], x_r.at[j], mate)
        merge(k, j)
        if k == 1:
            sent.append(push(own.at[1], z_in.at[1], z_s.at[1], z_r.at[1], down1))
        if k == 3:
            sent.append(push(own.at[3], z_in.at[3], z_s.at[3], z_r.at[3], down1))
    arrived(z_in.at[1], z_s.at[1], z_r.at[1], down1)
    own[2] = (own[2].astype(F32) + z_in[1].astype(F32)).astype(BF)
    sent.append(push(own.at[2], z_in.at[2], z_s.at[2], z_r.at[2], down2))

    @pl.when(x == 0)
    def _():
        arrived(x_in.at[0], x_s.at[0], x_r.at[0], mate)
        merge(4, 0)

    @pl.when(x == 1)
    def _():
        merge(4, None)

    for k in (3, 0, 2):
        arrived(z_in.at[k], z_s.at[k], z_r.at[k], down1)
    total = (
        own[4].astype(F32) + z_in[3].astype(F32) + z_in[0].astype(F32) + z_in[2].astype(F32)
    )
    keys = total[:, 0:HD]
    keys = keys * cos[...] + pltpu.roll(keys, 64, 1) * sin[...]
    kvg[:, 0:HD] = keys.astype(BF)
    kvg[:, HD : 2 * HD] = total[:, HD : 2 * HD].astype(BF)
    waits.append(push(kvg.at[theirs], kvo, core_s.at[2], core_r.at[2], other))
    for copy in crossing:
        copy.wait_send()
    for copy in sent:
        copy.wait_send()
    for copy in waits:
        copy.wait()


def return_gradients(dkv, att2, gq2, cos, sin):
    dma = pltpu.SemaphoreType.DMA
    return pl.pallas_call(
        return_kernel,
        out_shape=(
            jax.ShapeDtypeStruct((256, 256), BF),
            jax.ShapeDtypeStruct((128, 256), BF),
            jax.ShapeDtypeStruct((128, 1024), BF),
            jax.ShapeDtypeStruct((128, 1024), BF),
        ),
        in_specs=[VM, VM, VM, VM, VM],
        out_specs=(VM, VM, VM, VM),
        scratch_shapes=[
            pltpu.VMEM((5, 256, 256), BF),
            pltpu.VMEM((4, 256, 256), BF),
            pltpu.VMEM((4, 256, 256), BF),
            dma((3,)),
            dma((3,)),
            dma((4,)),
            dma((4,)),
            dma((4,)),
            dma((4,)),
            dma((2,)),
        ],
        compiler_params=params(2),
        name="returns",
    )(dkv, att2, gq2, cos, sin)


def sums_kernel(
    ph, wg, gh, gk, gv, h_in, buf0, acc0, zin0, buf1, acc1, yin1, part, x_in, chunk, c_in,
    h_s, h_r, a_s, a_r, b_s, b_r, x_s, x_r, c_s, c_r
):
    y, z, x, c, h = coords()
    other = dev(y, z, x, 1 - c, h)
    mate = dev(y, z, 1 - x, c, h)
    peer = dev(y, z, x, c, 1 - h)
    ys = [dev(y + d, z, x, c, h) for d in DY]
    zs = [dev(y, z + d, x, c, h) for d in DZ]
    enter([other, mate, peer] + ys + zs)
    hidden = push(ph, h_in, h_s, h_r, peer)

    @pl.when(c == 0)
    def _():
        first = [
            push(wg.at[(y + d) % NY], buf0.at[n], a_s.at[n], a_r.at[n], ys[n])
            for n, d in enumerate(DY)
        ]
        for copy in first:
            copy.wait_recv()

        def add(zz, _):
            acc0[zz] = (
                wg[y, zz].astype(F32)
                + buf0[0, zz].astype(F32)
                + buf0[1, zz].astype(F32)
                + buf0[2, zz].astype(F32)
            ).astype(BF)
            return 0

        lax.fori_loop(0, NZ, add, 0)
        second = [
            push(acc0.at[(z + d) % NZ], zin0.at[n], b_s.at[n], b_r.at[n], zs[n])
            for n, d in enumerate(DZ)
        ]
        total = acc0[z].astype(F32)
        for n, copy in enumerate(second):
            copy.wait_recv()
            total = total + zin0[n].astype(F32)
        part[...] = total
        for copy in first + second:
            copy.wait_send()

    @pl.when(c == 1)
    def _():
        first = [
            push(wg.at[:, (z + d) % NZ], buf1.at[n], a_s.at[n], a_r.at[n], zs[n])
            for n, d in enumerate(DZ)
        ]
        for copy in first:
            copy.wait_recv()

        def add(yy, _):
            total = wg[yy, z].astype(F32)
            for n in range(7):
                total = total + buf1[n, yy].astype(F32)
            acc1[yy] = total.astype(BF)
            return 0

        lax.fori_loop(0, NY, add, 0)
        second = [
            push(acc1.at[(y + d) % NY], yin1.at[n], b_s.at[n], b_r.at[n], ys[n])
            for n, d in enumerate(DY)
        ]
        total = acc1[y].astype(F32)
        for n, copy in enumerate(second):
            copy.wait_recv()
            total = total + yin1[n].astype(F32)
        part[...] = total
        for copy in first + second:
            copy.wait_send()

    pair = push(part.at[1 - x], x_in, x_s, x_r, mate)
    pair.wait_recv()
    chunk[...] = part[x] + x_in[...]
    last = push(chunk.at[pl.ds((1 - c) * 32, 32)], c_in, c_s, c_r, other)
    hidden.wait_recv()

    def add(n, _):
        cols = pl.ds(pl.multiple_of(n * 512, 512), 512)
        gh[:, cols] = (ph[:, cols].astype(F32) + h_in[:, cols].astype(F32)).astype(BF)
        return 0

    lax.fori_loop(0, 8, add, 0)
    last.wait_recv()

    @pl.when(c == 0)
    def _():
        gk[:, 0:HD] = chunk[0:32, 0:HD]
        gv[:, 0:HD] = chunk[0:32, HD : 2 * HD]
        gk[:, HD : 2 * HD] = c_in[:, 0:HD]
        gv[:, HD : 2 * HD] = c_in[:, HD : 2 * HD]

    @pl.when(c == 1)
    def _():
        gk[:, 0:HD] = c_in[:, 0:HD]
        gv[:, 0:HD] = c_in[:, HD : 2 * HD]
        gk[:, HD : 2 * HD] = chunk[32:64, 0:HD]
        gv[:, HD : 2 * HD] = chunk[32:64, HD : 2 * HD]

    last.wait_send()
    pair.wait_send()
    hidden.wait_send()


def sum_up(ph, wg):
    dma = pltpu.SemaphoreType.DMA
    return pl.pallas_call(
        sums_kernel,
        out_shape=(
            jax.ShapeDtypeStruct((128, 4096), BF),
            jax.ShapeDtypeStruct((32, 256), F32),
            jax.ShapeDtypeStruct((32, 256), F32),
        ),
        in_specs=[VM, VM],
        out_specs=(VM, VM, VM),
        scratch_shapes=[
            pltpu.VMEM((128, 4096), BF),
            pltpu.VMEM((3, NZ, 2, 64, 256), BF),
            pltpu.VMEM((NZ, 2, 64, 256), BF),
            pltpu.VMEM((7, 2, 64, 256), BF),
            pltpu.VMEM((7, NY, 2, 64, 256), BF),
            pltpu.VMEM((NY, 2, 64, 256), BF),
            pltpu.VMEM((3, 2, 64, 256), BF),
            pltpu.VMEM((2, 64, 256), F32),
            pltpu.VMEM((64, 256), F32),
            pltpu.VMEM((64, 256), F32),
            pltpu.VMEM((32, 256), F32),
            dma, dma, dma((7,)), dma((7,)), dma((7,)), dma((7,)), dma, dma, dma, dma,
        ],
        compiler_params=params(3),
        name="sums",
    )(ph, wg)


def body(hidden_in, queries, key_weight, value_weight, seg_ids, grad_out):
    i = lax.axis_index("ctx")
    c = i % 2
    w, hid2, q2, do2 = gather_weights(key_weight, value_weight, hidden_in, queries, grad_out)
    flat = w.reshape(4096, 256)
    kv = jnp.dot(hid2, flat, preferred_element_type=F32)
    positions = (i // 2) * 256 + jnp.arange(256, dtype=jnp.int32)
    frequency = 10000.0 ** (-(jnp.arange(64, dtype=F32) * 2.0 / HD))
    angles = positions.astype(F32)[:, None] * frequency[None, :]
    cosine, sine = jnp.cos(angles), jnp.sin(angles)
    cos2 = jnp.concatenate([cosine, cosine], axis=1)
    sin2 = jnp.concatenate([sine, -sine], axis=1)
    raw = kv[:, :HD]
    keys = raw * cos2 - jnp.concatenate([raw[:, 64:], raw[:, :64]], axis=1) * sin2
    kv = jnp.concatenate([keys, kv[:, HD:]], axis=1).astype(BF)
    win, wo = exchange_window(kv, w)
    seg = seg_ids.astype(F32).reshape(128, 128)
    att2, gq2, dkv = attention(q2, do2, win.reshape(2560, 256), seg)
    kvg, kvo, att, gq = return_gradients(dkv.reshape(5, 2, 256, 256), att2, gq2, cos2, sin2)
    own = lax.dynamic_slice_in_dim(kvg, c * 128, 128)
    nt = (((1,), (1,)), ((), ()))
    ph = lax.dot_general(own, flat, nt, preferred_element_type=F32) + lax.dot_general(
        kvo, wo.reshape(4096, 256), nt, preferred_element_type=F32
    )
    wg = lax.dot_general(hid2, kvg, (((0,), (0,)), ((), ())), preferred_element_type=F32)
    gh, gk, gv = sum_up(ph.astype(BF), wg.astype(BF).reshape(NY, NZ, 2, 64, 256))
    return att, gq, gh, gk, gv


def solution(mesh):
    placed = (
        P("ctx", None),
        P("ctx", "head"),
        P("ctx", "head"),
        P("ctx", "head"),
        P(),
        P("ctx", "head"),
    )
    return jax.shard_map(
        body,
        mesh=mesh,
        in_specs=placed,
        out_specs=(
            P("ctx", "head"),
            P("ctx", "head"),
            P("ctx", None),
            P("ctx", "head"),
            P("ctx", "head"),
        ),
        check_vma=False,
    )
```

```python
import math

import jax
import jax.numpy as jnp
from jax import lax
from jax.experimental import pallas as pl
from jax.experimental.pallas import tpu as pltpu
from jax.sharding import PartitionSpec as P

HD = 128
WINDOW = 2048
NEG = -1e30
MESH = pl.DeviceIdType.MESH
VM = pl.BlockSpec(memory_space=pltpu.VMEM)
BF = jnp.bfloat16
F32 = jnp.float32
NY, NZ = 4, 8
DZ = (1, -1, 2, -2, 3, -3, 4)
DY = (1, -1, 2)
FAR = (4, 3, -3, 2, -2, 1, -1)
SCALING = 1.0 / math.sqrt(HD)
TO_EXP2 = SCALING * math.log2(math.e)
LEFT = (((0,), (0,)), ((), ()))
RIGHT = (((1,), (1,)), ((), ()))


def coords():
    i = lax.axis_index("ctx")
    return i // 32, (i // 4) % 8, (i // 2) % 2, i % 2, lax.axis_index("head")


def dev(y, z, x, c, h):
    return (((y % NY) * NZ + z % NZ) * 4 + x * 2 + c, h)


def plane_dev(p, x, c, h):
    return ((p % 32) * 4 + x * 2 + c, h)


def remote(src, dst, send, recv, to):
    return pltpu.make_async_remote_copy(
        src_ref=src, dst_ref=dst, send_sem=send, recv_sem=recv, device_id=to, device_id_type=MESH
    )


def push(src, dst, send, recv, to):
    copy = remote(src, dst, send, recv, to)
    copy.start()
    return copy


def dot(a, b):
    return jnp.dot(a, b, preferred_element_type=F32)


def part(start, size):
    return pl.ds(pl.multiple_of(start, size), size)


def kernel(
    wk, wv, hid, q, do, seg, cos, sin,
    att, gq, gh, gk, gv,
    pw, w, wo, hs, hst, qx, dx, win, qa, da, qt, dt, s, dkv, att2, gq2,
    x_in, own, z_in, kvg, kvo, wg, ph, h_in,
    buf0, acc0, zin0, plus, minus, acc1, yin1, total, f_in,
    p_s, p_r, g_s, g_r, o_s, o_r, wo_s, wo_r, wz_s, wz_r, wx_s, wx_r,
    bx_s, bx_r, bz_s, bz_r, k_s, k_r, h_s, h_r, a_s, a_r, b_s, b_r, m_s, m_r, f_s, f_r, loc,
):
    y, z, x, c, h = coords()
    p = y * NZ + z
    chip = p * 2 + x
    other = dev(y, z, x, 1 - c, h)
    mate = dev(y, z, 1 - x, c, h)
    diag = dev(y, z, 1 - x, 1 - c, h)
    peer = dev(y, z, x, c, 1 - h)
    ys = [dev(y + d, z, x, c, h) for d in DY]
    zs = [dev(y, z + d, x, c, h) for d in DZ]
    up1, down1, up2, down2, up4, down4 = [
        plane_dev(p + d, x, c, h) for d in (1, -1, 2, -2, 4, -4)
    ]
    partners = [other, mate, diag, peer, up1, down1, up2, down2, up4, down4] + ys + zs
    barrier = pltpu.get_barrier_semaphore()
    for partner in partners:
        pl.semaphore_signal(barrier, inc=1, device_id=partner, device_id_type=MESH)
    for n in range(2):
        pw[n, :, 0:HD] = wk[:, n * HD : (n + 1) * HD]
        pw[n, :, HD : 2 * HD] = wv[:, n * HD : (n + 1) * HD]
    pl.semaphore_wait(barrier, len(partners))

    def plane(yy, zz):
        return part(((yy % NY) * NZ + zz % NZ) * 128, 128)

    def piece(xx, cc):
        return part(p * 128 + xx * 64 + cc * 32, 32)

    pieces = [
        push(pw.at[1 - c], w.at[piece(x, c)], p_s.at[0], p_r.at[0], other),
        push(pw.at[c], w.at[piece(x, c)], p_s.at[1], p_r.at[1], mate),
        push(pw.at[1 - c], w.at[piece(x, c)], p_s.at[2], p_r.at[2], diag),
    ]
    w[piece(x, c), :] = pw[c]
    theirs = part((1 - c) * 512, 512)
    mine = part(c * 512, 512)
    toks = part(c * 128, 128)
    trades = [
        push(q.at[:, theirs], qx, o_s.at[0], o_r.at[0], other),
        push(do.at[:, theirs], dx, o_s.at[1], o_r.at[1], other),
        push(hid, hs.at[toks], o_s.at[2], o_r.at[2], other),
    ]
    for copy in pieces:
        copy.wait_recv()

    def plane_sem(yy, zz):
        return g_r.at[(yy % NY) * NZ + zz % NZ]

    def wait_plane(yy, zz):
        ref = w.at[plane(yy, zz)]
        remote(ref, ref, g_s.at[0], plane_sem(yy, zz), other).wait_recv()

    def keep_own():
        def copy_rows(n, _):
            cols = part(n * 512, 512)
            hs[toks, cols] = hid[:, cols]
            return 0

        lax.fori_loop(0, 8, copy_rows, 0)

    @pl.when(c == 0)
    def _():
        sent = []

        def go(yy, zz, to):
            ref = w.at[plane(yy, zz)]
            sent.append(push(ref, ref, g_s.at[len(sent)], plane_sem(yy, zz), to))

        for n in range(4):
            go(y, z, zs[n])
        for to in ys:
            go(y, z, to)
        keep_own()
        for d in DZ:
            wait_plane(y, z + d)
            if d == 2:
                go(y, z + 2, zs[1])
            if d == -2:
                go(y, z - 2, zs[0])
                go(y, z - 2, zs[2])
            for to in ys:
                go(y, z + d, to)
        for d in (0,) + DZ:
            for e in DY:
                wait_plane(y + e, z + d)
        for copy in sent:
            copy.wait_send()

    @pl.when(c == 1)
    def _():
        sent = []

        def go(yy, zz, to):
            ref = w.at[plane(yy, zz)]
            sent.append(push(ref, ref, g_s.at[len(sent)], plane_sem(yy, zz), to))

        for to in ys:
            go(y, z, to)
        up, down = zs[0], zs[1]
        for d in range(4):
            for n, e in enumerate((0,) + DY):
                if d == 0:
                    if e:
                        wait_plane(y + e, z)
                    go(y + e, z, up)
                    go(y + e, z, down)
                    continue
                wait_plane(y + e, z - d)
                if d < 3 or n < 2:
                    go(y + e, z - d, up)
                wait_plane(y + e, z + d)
                if d < 3 or n >= 2:
                    go(y + e, z + d, down)
            if d == 0:
                keep_own()
        for e in (0,) + DY:
            wait_plane(y + e, z + 4)
        for copy in sent:
            copy.wait_send()

    for copy in trades:
        copy.wait_recv()
    weights = push(w, wo, wo_s, wo_r, other)

    def project(n, sums):
        span = part(n * 1024, 1024)
        return sums + dot(hs[:, span], w[span, :])

    raw = lax.fori_loop(0, 4, project, jnp.zeros((256, 256), F32))

    def win_rows(k, xx):
        return part((k * 2 + xx) * 256, 256)

    def win_half(k, xx, n):
        return part((k * 2 + xx) * 256 + n * 128, 128)

    keys = raw[:, 0:HD]
    win[win_rows(4, x), 0:HD] = (keys * cos[...] - pltpu.roll(keys, 64, 1) * sin[...]).astype(BF)
    win[win_rows(4, x), HD : 2 * HD] = raw[:, HD : 2 * HD].astype(BF)

    def window_up(k, n):
        return remote(
            win.at[win_half(k, x, n)], win.at[win_half(k - 1, x, n)],
            wz_s.at[k * 2 + n], wz_r.at[(k - 1) * 2 + n], up1,
        )

    def window_across(k, n):
        j = (4 - x - k) * 2 + n
        ref = win.at[win_half(k, x, n)]
        return remote(ref, ref, wx_s.at[j], wx_r.at[j], mate)

    for n in range(2):
        window_up(4, n).start()

    @pl.when(x == 0)
    def _():
        for n in range(2):
            window_across(4, n).start()

    for t in range(2):
        @pl.when(c == t)
        def _():
            for g in range(4):
                cols = pl.ds((t * 4 + g) * HD, HD)
                rows = pl.ds((t * 4 + g) * HD, HD)
                qa[rows, :] = q[:, cols]
                da[rows, :] = do[:, cols]

        @pl.when(c != t)
        def _():
            for g in range(4):
                rows = pl.ds((t * 4 + g) * HD, HD)
                qa[rows, :] = qx[:, g * HD : (g + 1) * HD]
                da[rows, :] = dx[:, g * HD : (g + 1) * HD]

    for n in range(8):
        block = slice(n * HD, (n + 1) * HD)
        qt[:, block] = qa[block, :].T
        dt[:, block] = da[block, :].T
    base = x * 256
    row = lax.broadcasted_iota(jnp.int32, (256, 128), 0)
    col = lax.broadcasted_iota(jnp.int32, (256, 128), 1)
    tilt = col - row

    def key_rows(b):
        return part(base + b * 256, 256)

    def score(b, best):
        seg_k = []
        for n in range(2):
            index = chip * 2 - 16 + b * 2 + n
            line = seg[pl.ds(jnp.maximum(index, 0), 1), :].astype(F32)
            line = jnp.where(index >= 0, line, -1.0)
            seg_k.append(jnp.broadcast_to(line, (128, 128)).T)
        seg_k = jnp.concatenate(seg_k, axis=0)
        bias = []
        for t in range(2):
            seg_q = seg[pl.ds(chip * 2 + t, 1), :].astype(F32)
            gap = tilt + (WINDOW + t * 128 - b * 256)
            ok = (seg_k == seg_q) & (gap >= 0) & (gap < WINDOW)
            bias += [jnp.where(ok, 0.0, NEG)] * 4
        k = win[key_rows(b), 0:HD]
        values = dot(k, qt[...]) * TO_EXP2 + jnp.concatenate(bias, axis=1)
        s[part(b * 256, 256), :] = values
        return jnp.maximum(best, jnp.max(values, axis=0, keepdims=True))

    best = score(8, jnp.full((1, 1024), NEG, F32))

    def turn_over(n, _):
        cols = part(n * 512, 512)
        hst[cols, :] = hs[:, cols].T
        return 0

    lax.fori_loop(0, 8, turn_over, 0)

    def inward(d, best):
        k = 4 - d
        for n in range(2):
            remote(
                win.at[win_half(k, x, n)], win.at[win_half(k, x, n)],
                wz_s.at[0], wz_r.at[k * 2 + n], up1,
            ).wait_recv()

            @pl.when(d < 4)
            def _():
                window_up(k, n).start()

            @pl.when((k >= 1) | (x == 1))
            def _():
                window_across(k, n).start()

        best = score(2 * k, best)
        for n in range(2):
            j = (d - 1) * 2 + n
            ref = win.at[win_half(4 + x - d, 1 - x, n)]
            remote(ref, ref, wx_s.at[j], wx_r.at[j], mate).wait_recv()
        return score(9 - 2 * d, best)

    best = lax.fori_loop(1, 5, inward, best)

    def mix(b, carry):
        sums, out = carry
        rows = part(b * 256, 256)
        e = jnp.exp2(s[rows, :] - best)
        s[rows, :] = e
        v = win[key_rows(b), HD : 2 * HD]
        out = out + lax.dot_general(v, e.astype(BF), LEFT, preferred_element_type=F32)
        return sums + jnp.sum(e, axis=0, keepdims=True), out

    sums, out = lax.fori_loop(
        0, 9, mix, (jnp.zeros((1, 1024), F32), jnp.zeros((HD, 1024), F32))
    )
    inverse = 1.0 / sums
    low = (out * inverse).astype(BF)
    delta = jnp.sum(low.astype(F32) * dt[...].astype(F32), axis=0, keepdims=True)
    for t in range(2):
        for g in range(4):
            n = t * 4 + g
            att2[t, :, g * HD : (g + 1) * HD] = low[:, n * HD : (n + 1) * HD].T
    trades.append(push(att2.at[1 - c], att.at[:, mine], o_s.at[3], o_r.at[3], other))
    keep_att = pltpu.make_async_copy(att2.at[c], att.at[:, mine], loc.at[0])
    keep_att.start()

    def give(b):
        j = (7 - b) // 2
        return remote(dkv.at[b], x_in.at[j], bx_s.at[j], bx_r.at[j], mate)

    def merge(k):
        j = 4 - x - k
        alone = (j < 0) | (j > 3)

        @pl.when(alone)
        def _():
            own[k] = dkv[2 * k]

        @pl.when(jnp.logical_not(alone))
        def _():
            remote(x_in.at[j], x_in.at[j], bx_s.at[0], bx_r.at[j], mate).wait_recv()
            own[k] = (dkv[2 * k].astype(F32) + x_in[j].astype(F32)).astype(BF)

    def give_back(k, to):
        return remote(own.at[k], z_in.at[k], bz_s.at[k], bz_r.at[k], to)

    def back(n, query_sum):
        b = jnp.where(n == 8, 8, n + 1 - 2 * (n % 2))
        rows = part(b * 256, 256)
        k = win[key_rows(b), 0:HD]
        v = win[key_rows(b), HD : 2 * HD]
        probs = s[rows, :] * inverse
        dscores = probs * (dot(v, dt[...]) - delta)
        probs = probs.astype(BF)
        dscores = dscores.astype(BF)
        dkv[b, :, 0:HD] = (dot(dscores, qa[...]) * SCALING).astype(BF)
        dkv[b, :, HD : 2 * HD] = dot(probs, da[...]).astype(BF)

        @pl.when((n % 2 == 0) & (n < 8))
        def _():
            give(b).start()

        @pl.when(n == 3)
        def _():
            merge(0)
            give_back(0, down4).start()

        @pl.when(n == 5)
        def _():
            merge(1)
            give_back(1, down1).start()

        return query_sum + lax.dot_general(k, dscores, LEFT, preferred_element_type=F32)

    query_sum = lax.fori_loop(0, 9, back, jnp.zeros((HD, 1024), F32))
    merge(3)
    give_back(3, down1).start()
    merge(2)
    remote(z_in.at[1], z_in.at[1], bz_s.at[1], bz_r.at[1], down1).wait_recv()
    own[2] = (own[2].astype(F32) + z_in[1].astype(F32)).astype(BF)
    give_back(2, down2).start()
    query_low = (query_sum * SCALING).astype(BF)
    for t in range(2):
        for g in range(4):
            n = t * 4 + g
            gq2[t, :, g * HD : (g + 1) * HD] = query_low[:, n * HD : (n + 1) * HD].T
    trades.append(push(gq2.at[1 - c], gq.at[:, mine], o_s.at[4], o_r.at[4], other))
    keep_gq = pltpu.make_async_copy(gq2.at[c], gq.at[:, mine], loc.at[1])
    keep_gq.start()
    merge(4)
    for k in (3, 0, 2):
        remote(z_in.at[k], z_in.at[k], bz_s.at[k], bz_r.at[k], down1).wait_recv()
    grads = (
        own[4].astype(F32) + z_in[3].astype(F32) + z_in[0].astype(F32) + z_in[2].astype(F32)
    )
    keys = grads[:, 0:HD]
    kvg[:, 0:HD] = (keys * cos[...] + pltpu.roll(keys, 64, 1) * sin[...]).astype(BF)
    kvg[:, HD : 2 * HD] = grads[:, HD : 2 * HD].astype(BF)
    crossing = push(kvg.at[part((1 - c) * 128, 128)], kvo, k_s, k_r, other)

    def outer(n, _):
        rows = part(n * 512, 512)
        wg[rows, :] = dot(hst[rows, :], kvg[...]).astype(BF)
        return 0

    lax.fori_loop(0, 8, outer, 0)

    @pl.when(c == 0)
    def _():
        for i, d in enumerate(FAR + (0,)):
            for n, e in enumerate(DY):
                push(
                    wg.at[plane(y + e, z + d)], buf0.at[i, n],
                    a_s.at[i * 3 + n], a_r.at[i * 3 + n], ys[n],
                )

    @pl.when(c == 1)
    def _():
        for n, e in enumerate((2, 1, -1, 0)):
            top = 4 if n < 2 else 3
            low = 3 if n < 2 else 4
            push(
                wg.at[plane(y + e, z + top)], plus.at[n, top - 1],
                a_s.at[n * 4 + top - 1], a_r.at[n * 4 + top - 1], zs[0],
            )
            push(
                wg.at[plane(y + e, z - low)], minus.at[n, low - 1],
                b_s.at[n * 4 + low - 1], b_r.at[n * 4 + low - 1], zs[1],
            )

    crossing.wait_recv()
    weights.wait_recv()

    def hidden(n, _):
        for m in range(2):
            span = part(n * 1024 + m * 512, 512)
            ph[n, :, m * 512 : (m + 1) * 512] = (
                lax.dot_general(kvg[toks, :], w[span, :], RIGHT, preferred_element_type=F32)
                + lax.dot_general(kvo[...], wo[span, :], RIGHT, preferred_element_type=F32)
            ).astype(BF)
        remote(ph.at[n], h_in.at[n], h_s.at[n], h_r.at[n], peer).start()
        return 0

    lax.fori_loop(0, 4, hidden, 0)

    @pl.when(c == 0)
    def _():
        for i, d in enumerate(FAR + (0,)):
            for n in range(3):
                ref = buf0.at[i, n]
                remote(ref, ref, a_s.at[0], a_r.at[i * 3 + n], other).wait_recv()
            value = (
                wg[plane(y, z + d), :].astype(F32)
                + buf0[i, 0].astype(F32)
                + buf0[i, 1].astype(F32)
                + buf0[i, 2].astype(F32)
            )
            if d:
                acc0[i] = value.astype(BF)
                push(acc0.at[i], zin0.at[i], b_s.at[i], b_r.at[i], zs[DZ.index(d)])
            else:
                total[...] = value
        for i in range(7):
            remote(zin0.at[i], zin0.at[i], b_s.at[0], b_r.at[i], other).wait_recv()
            total[...] += zin0[i].astype(F32)
        for i in range(8):
            for n in range(3):
                ref = buf0.at[i, n]
                remote(ref, ref, a_s.at[i * 3 + n], a_r.at[0], other).wait_send()
        for i in range(7):
            remote(zin0.at[i], zin0.at[i], b_s.at[i], b_r.at[0], other).wait_send()

    @pl.when(c == 1)
    def _():
        def step(ref, send, recv, n, m, e, sign, to):
            remote(ref.at[n, m], ref.at[n, m], send.at[0], recv.at[n * 4 + m], other).wait_recv()
            if m:
                ref[n, m] = (
                    ref[n, m].astype(F32) + wg[plane(y + e, z + sign * m), :].astype(F32)
                ).astype(BF)
                push(
                    ref.at[n, m], ref.at[n, m - 1],
                    send.at[n * 4 + m - 1], recv.at[n * 4 + m - 1], to,
                )

        for m in (3, 2, 1, 0):
            for n, e in enumerate((2, 1, -1, 0)):
                top = 4 if n < 2 else 3
                low = 3 if n < 2 else 4
                if m < top:
                    step(plus, a_s, a_r, n, m, e, 1, zs[0])
                if m < low:
                    step(minus, b_s, b_r, n, m, e, -1, zs[1])
                if m == 0:
                    value = (
                        wg[plane(y + e, z), :].astype(F32)
                        + plus[n, 0].astype(F32)
                        + minus[n, 0].astype(F32)
                    )
                    if e:
                        acc1[n] = value.astype(BF)
                        to = DY.index(e)
                        push(acc1.at[n], yin1.at[n], m_s.at[n], m_r.at[n], ys[to])
                    else:
                        total[...] = value
        for n in range(3):
            remote(yin1.at[n], yin1.at[n], m_s.at[0], m_r.at[n], other).wait_recv()
            total[...] += yin1[n].astype(F32)
        for n in range(4):
            top = 4 if n < 2 else 3
            low = 3 if n < 2 else 4
            for m in range(top):
                remote(
                    plus.at[n, m], plus.at[n, m], a_s.at[n * 4 + m], a_r.at[0], other
                ).wait_send()
            for m in range(low):
                remote(
                    minus.at[n, m], minus.at[n, m], b_s.at[n * 4 + m], b_r.at[0], other
                ).wait_send()
        for n in range(3):
            remote(yin1.at[n], yin1.at[n], m_s.at[n], m_r.at[0], other).wait_send()

    def rows_of(xx, cc):
        return part(xx * 64 + cc * 32, 32)

    finals = [
        push(total.at[rows_of(x, 1 - c)], f_in.at[0], f_s.at[0], f_r.at[0], other),
        push(total.at[rows_of(1 - x, c)], f_in.at[1], f_s.at[1], f_r.at[1], mate),
        push(total.at[rows_of(1 - x, 1 - c)], f_in.at[2], f_s.at[2], f_r.at[2], diag),
    ]

    def finish(n, _):
        remote(ph.at[n], h_in.at[n], h_s.at[n], h_r.at[n], peer).wait()
        cols = part(n * 1024, 1024)
        gh[:, cols] = (ph[n].astype(F32) + h_in[n].astype(F32)).astype(BF)
        return 0

    lax.fori_loop(0, 4, finish, 0)
    for copy in finals:
        copy.wait_recv()
    here = total[rows_of(x, c), :] + f_in[1]
    there = f_in[0] + f_in[2]
    for n in range(2):
        @pl.when(c == n)
        def _():
            for first, value in ((n, here), (1 - n, there)):
                gk[:, first * HD : (first + 1) * HD] = value[:, 0:HD]
                gv[:, first * HD : (first + 1) * HD] = value[:, HD : 2 * HD]

    for copy in pieces + trades[:3] + finals + [crossing, weights]:
        copy.wait_send()
    for copy in trades[3:]:
        copy.wait()
    keep_att.wait()
    keep_gq.wait()
    for n in range(2):
        for k in range(1, 5):
            window_up(k, n).wait_send()
        for j in range(4):
            ref = win.at[win_half(4 - x - j, x, n)]
            remote(ref, ref, wx_s.at[j * 2 + n], wx_r.at[0], mate).wait_send()
    for j in range(4):
        remote(x_in.at[j], x_in.at[j], bx_s.at[j], bx_r.at[0], mate).wait_send()
        remote(z_in.at[j], z_in.at[j], bz_s.at[j], bz_r.at[0], mate).wait_send()


def run(wk, wv, hid, q, do, seg, cos, sin):
    dma = pltpu.SemaphoreType.DMA
    shape = jax.ShapeDtypeStruct

    def bf(*dims):
        return pltpu.VMEM(dims, BF)

    def f32(*dims):
        return pltpu.VMEM(dims, F32)

    buffers = [
        bf(2, 32, 256), bf(4096, 256), bf(4096, 256), bf(256, 4096), bf(4096, 256),
        bf(128, 512), bf(128, 512), bf(2560, 256),
        bf(1024, 128), bf(1024, 128), bf(128, 1024), bf(128, 1024), f32(2304, 1024),
        bf(9, 256, 256), bf(2, 128, 512), bf(2, 128, 512),
        bf(4, 256, 256), bf(5, 256, 256), bf(4, 256, 256), bf(256, 256), bf(128, 256),
        bf(4096, 256), bf(4, 128, 1024), bf(4, 128, 1024),
        bf(8, 3, 128, 256), bf(7, 128, 256), bf(7, 128, 256),
        bf(4, 4, 128, 256), bf(4, 4, 128, 256), bf(3, 128, 256), bf(3, 128, 256),
        f32(128, 256), f32(3, 32, 256),
    ]
    counts = [3, 3, 31, 32, 5, 5, 0, 0, 10, 8, 8, 8, 4, 4, 4, 4, 0, 0, 4, 4, 24, 24, 16, 16, 3, 3, 3, 3, 2]
    return pl.pallas_call(
        kernel,
        out_shape=(
            shape((128, 1024), BF),
            shape((128, 1024), BF),
            shape((128, 4096), BF),
            shape((32, 256), F32),
            shape((32, 256), F32),
        ),
        in_specs=[VM] * 8,
        out_specs=(VM,) * 5,
        scratch_shapes=buffers + [dma((n,)) if n else dma for n in counts],
        compiler_params=pltpu.CompilerParams(
            collective_id=0, has_side_effects=True, vmem_limit_bytes=60 * 2**20
        ),
        name="layer",
    )(wk, wv, hid, q, do, seg, cos, sin)


def body(hidden_in, queries, key_weight, value_weight, seg_ids, grad_out):
    chip = lax.axis_index("ctx") // 2
    positions = chip * 256 + jnp.arange(256, dtype=jnp.int32)
    frequency = 10000.0 ** (-(jnp.arange(64, dtype=F32) * 2.0 / HD))
    angles = positions.astype(F32)[:, None] * frequency[None, :]
    cosine, sine = jnp.cos(angles), jnp.sin(angles)
    cos2 = jnp.concatenate([cosine, cosine], axis=1)
    sin2 = jnp.concatenate([sine, -sine], axis=1)
    seg = seg_ids.reshape(128, 128)
    return run(key_weight, value_weight, hidden_in, queries, grad_out, seg, cos2, sin2)


def solution(mesh):
    placed = (
        P("ctx", None),
        P("ctx", "head"),
        P("ctx", "head"),
        P("ctx", "head"),
        P(),
        P("ctx", "head"),
    )
    return jax.shard_map(
        body,
        mesh=mesh,
        in_specs=placed,
        out_specs=(
            P("ctx", "head"),
            P("ctx", "head"),
            P("ctx", None),
            P("ctx", "head"),
            P("ctx", "head"),
        ),
        check_vma=False,
    )
```

```python
import math

import jax
import jax.numpy as jnp
import numpy as np
from jax import lax
from jax.experimental import pallas as pl
from jax.experimental.pallas import tpu as pltpu
from jax.sharding import PartitionSpec as P

HD = 128
WINDOW = 2048
NEG = -1e30
MESH = pl.DeviceIdType.MESH
VM = pl.BlockSpec(memory_space=pltpu.VMEM)
ANY = pl.BlockSpec(memory_space=pl.ANY)
BF = jnp.bfloat16
F32 = jnp.float32
NY, NZ = 4, 8
DZ = (1, -1, 2, -2, 3, -3, 4)
DY = (1, -1, 2)
FAR = (4, 3, -3, 2, -2, 1, -1)
SCALING = 1.0 / math.sqrt(HD)
TO_EXP2 = SCALING * math.log2(math.e)
LEFT = (((0,), (0,)), ((), ()))
RIGHT = (((1,), (1,)), ((), ()))


def coords():
    i = lax.axis_index("ctx")
    return i // 32, (i // 4) % 8, (i // 2) % 2, i % 2, lax.axis_index("head")


def dev(y, z, x, c, h):
    return (((y % NY) * NZ + z % NZ) * 4 + x * 2 + c, h)


def plane_dev(p, x, c, h):
    return ((p % 32) * 4 + x * 2 + c, h)


def remote(src, dst, send, recv, to):
    return pltpu.make_async_remote_copy(
        src_ref=src, dst_ref=dst, send_sem=send, recv_sem=recv, device_id=to, device_id_type=MESH
    )


def push(src, dst, send, recv, to):
    copy = remote(src, dst, send, recv, to)
    copy.start()
    return copy


def dot(a, b):
    return jnp.dot(a, b, preferred_element_type=F32)


def part(start, size):
    return pl.ds(pl.multiple_of(start, size), size)


def kernel(
    wk, wv, hid, q, do, seg, table,
    att, gq, ph_out, h_in, own_out, f_in,
    cos, sin, top, pw, w, wo, hs, hst, q_own, d_own, qx, dx, win, qa, da, qt, dt, s, dkv, att2, gq2,
    x_in, own, z_in, kvg, kvo, wg, ph,
    buf0, acc0, zin0, plus, minus, acc1, yin1, total,
    p_s, p_r, g_s, g_r, o_s, o_r, wo_s, wo_r, wz_s, wz_r, wx_s, wx_r,
    bx_s, bx_r, bz_s, bz_r, k_s, k_r, h_s, h_r, a_s, a_r, b_s, b_r, m_s, m_r, f_s, f_r, loc, out_sem,
):
    y, z, x, c, h = coords()
    p = y * NZ + z
    chip = p * 2 + x
    other = dev(y, z, x, 1 - c, h)
    mate = dev(y, z, 1 - x, c, h)
    diag = dev(y, z, 1 - x, 1 - c, h)
    peer = dev(y, z, x, c, 1 - h)
    ys = [dev(y + d, z, x, c, h) for d in DY]
    zs = [dev(y, z + d, x, c, h) for d in DZ]
    up1, down1, up2, down2, up4, down4 = [
        plane_dev(p + d, x, c, h) for d in (1, -1, 2, -2, 4, -4)
    ]
    partners = [other, mate, diag, peer, up1, down1, up2, down2, up4, down4] + ys + zs
    barrier = pltpu.get_barrier_semaphore()
    for partner in partners:
        pl.semaphore_signal(barrier, inc=1, device_id=partner, device_id_type=MESH)
    for n in range(2):
        pw[n, :, 0:HD] = wk[:, n * HD : (n + 1) * HD]
        pw[n, :, HD : 2 * HD] = wv[:, n * HD : (n + 1) * HD]
    theirs = part((1 - c) * 512, 512)
    mine = part(c * 512, 512)
    toks = part(c * 128, 128)
    staged = [
        pltpu.make_async_copy(q.at[:, mine], q_own, loc.at[0]),
        pltpu.make_async_copy(do.at[:, mine], d_own, loc.at[1]),
        pltpu.make_async_copy(hid, hs.at[toks], loc.at[2]),
    ]
    for copy in staged:
        copy.start()
    cos_a, sin_a = table[pl.ds(chip, 1), :], table[pl.ds(64 + chip, 1), :]
    cos_b, sin_b = table[128:384, :], table[384:640, :]
    cos[...] = cos_a * cos_b - sin_a * sin_b
    lane = lax.broadcasted_iota(jnp.int32, (256, HD), 1)
    angle_sin = sin_a * cos_b + cos_a * sin_b
    sin[...] = jnp.where(lane < 64, angle_sin, -angle_sin)
    pl.semaphore_wait(barrier, len(partners))

    def plane(yy, zz):
        return part(((yy % NY) * NZ + zz % NZ) * 128, 128)

    def piece(xx, cc):
        return part(p * 128 + xx * 64 + cc * 32, 32)

    pieces = [
        push(pw.at[1 - c], w.at[piece(x, c)], p_s.at[0], p_r.at[0], other),
        push(pw.at[c], w.at[piece(x, c)], p_s.at[1], p_r.at[1], mate),
        push(pw.at[1 - c], w.at[piece(x, c)], p_s.at[2], p_r.at[2], diag),
    ]
    w[piece(x, c), :] = pw[c]
    trades = [
        push(q.at[:, theirs], qx, o_s.at[0], o_r.at[0], other),
        push(do.at[:, theirs], dx, o_s.at[1], o_r.at[1], other),
        push(hid, hs.at[toks], o_s.at[2], o_r.at[2], other),
    ]
    for copy in pieces:
        copy.wait_recv()

    def plane_sem(yy, zz):
        return g_r.at[(yy % NY) * NZ + zz % NZ]

    def wait_plane(yy, zz):
        ref = w.at[plane(yy, zz)]
        remote(ref, ref, g_s.at[0], plane_sem(yy, zz), other).wait_recv()

    @pl.when(c == 0)
    def _():
        sent = []

        def go(yy, zz, to):
            ref = w.at[plane(yy, zz)]
            sent.append(push(ref, ref, g_s.at[len(sent)], plane_sem(yy, zz), to))

        for n in range(4):
            go(y, z, zs[n])
        for to in ys:
            go(y, z, to)
        for d in DZ:
            wait_plane(y, z + d)
            if d == 2:
                go(y, z + 2, zs[1])
            if d == -2:
                go(y, z - 2, zs[0])
                go(y, z - 2, zs[2])
            for to in ys:
                go(y, z + d, to)
        for d in (0,) + DZ:
            for e in DY:
                wait_plane(y + e, z + d)
        for copy in sent:
            copy.wait_send()

    @pl.when(c == 1)
    def _():
        sent = []

        def go(yy, zz, to):
            ref = w.at[plane(yy, zz)]
            sent.append(push(ref, ref, g_s.at[len(sent)], plane_sem(yy, zz), to))

        for to in ys:
            go(y, z, to)
        up, down = zs[0], zs[1]
        for d in range(4):
            for n, e in enumerate((0,) + DY):
                if d == 0:
                    if e:
                        wait_plane(y + e, z)
                    go(y + e, z, up)
                    go(y + e, z, down)
                    continue
                wait_plane(y + e, z - d)
                if d < 3 or n < 1:
                    go(y + e, z - d, up)
                wait_plane(y + e, z + d)
                if d < 3 or n >= 1:
                    go(y + e, z + d, down)
        for e in (0,) + DY:
            wait_plane(y + e, z + 4)
        for copy in sent:
            copy.wait_send()

    for copy in trades:
        copy.wait_recv()
    for copy in staged:
        copy.wait()
    weights = push(w, wo, wo_s, wo_r, other)

    def project(n, sums):
        span = part(n * 1024, 1024)
        return sums + dot(hs[:, span], w[span, :])

    raw = lax.fori_loop(0, 4, project, jnp.zeros((256, 256), F32))

    def win_rows(k, xx):
        return part((k * 2 + xx) * 256, 256)

    def win_piece(k, xx, n):
        return win.at[n // 2, part((k * 2 + xx) * 256 + (n % 2) * 128, 128)]

    keys = raw[:, 0:HD]
    win[0, win_rows(4, x), :] = (keys * cos[...] - pltpu.roll(keys, 64, 1) * sin[...]).astype(BF)
    win[1, win_rows(4, x), :] = raw[:, HD : 2 * HD].astype(BF)

    def window_up(k, n):
        return remote(
            win_piece(k, x, n), win_piece(k - 1, x, n),
            wz_s.at[k * 4 + n], wz_r.at[(k - 1) * 4 + n], up1,
        )

    def window_across(k, n):
        j = (4 - x - k) * 4 + n
        ref = win_piece(k, x, n)
        return remote(ref, ref, wx_s.at[j], wx_r.at[j], mate)

    for n in range(4):
        window_up(4, n).start()

    @pl.when(x == 0)
    def _():
        for n in range(4):
            window_across(4, n).start()

    for t in range(2):
        @pl.when(c == t)
        def _():
            for g in range(4):
                cols = pl.ds(g * HD, HD)
                rows = pl.ds((t * 4 + g) * HD, HD)
                qa[rows, :] = q_own[:, cols]
                da[rows, :] = d_own[:, cols]

        @pl.when(c != t)
        def _():
            for g in range(4):
                rows = pl.ds((t * 4 + g) * HD, HD)
                qa[rows, :] = qx[:, g * HD : (g + 1) * HD]
                da[rows, :] = dx[:, g * HD : (g + 1) * HD]

    for n in range(8):
        block = slice(n * HD, (n + 1) * HD)
        qt[:, block] = qa[block, :].T
        dt[:, block] = da[block, :].T
    base = x * 256
    row = lax.broadcasted_iota(jnp.int32, (256, 128), 0)
    col = lax.broadcasted_iota(jnp.int32, (256, 128), 1)
    tilt = col - row

    def key_rows(b):
        return part(base + b * 256, 256)

    def forward(b, carry):
        best, sums, out = carry
        seg_k = []
        for n in range(2):
            index = chip * 2 - 16 + b * 2 + n
            line = seg[pl.ds(jnp.maximum(index, 0), 1), :].astype(F32)
            line = jnp.where(index >= 0, line, -1.0)
            seg_k.append(jnp.broadcast_to(line, (128, 128)).T)
        seg_k = jnp.concatenate(seg_k, axis=0)
        bias = []
        for t in range(2):
            seg_q = seg[pl.ds(chip * 2 + t, 1), :].astype(F32)
            gap = tilt + (WINDOW + t * 128 - b * 256)
            ok = (seg_k == seg_q) & (gap >= 0) & (gap < WINDOW)
            bias += [jnp.where(ok, 0.0, NEG)] * 4
        values = dot(win[0, key_rows(b), :], qt[...]) * TO_EXP2 + jnp.concatenate(bias, axis=1)
        higher = jnp.maximum(best, jnp.max(values, axis=0, keepdims=True))
        e = jnp.exp2(values - higher)
        s[part(b * 256, 256), :] = e
        top[pl.ds(b, 1), :] = higher
        shrink = jnp.exp2(best - higher)
        mixed = lax.dot_general(
            win[1, key_rows(b), :], e.astype(BF), LEFT, preferred_element_type=F32
        )
        return higher, sums * shrink + jnp.sum(e, axis=0, keepdims=True), out * shrink + mixed

    def turn_over(n, _):
        cols = part(n * 512, 512)
        hst[cols, :] = hs[:, cols].T
        return 0

    lax.fori_loop(0, 8, turn_over, 0)

    def wait_mate(d):
        for n in range(4):
            j = (d - 1) * 4 + n
            ref = win_piece(4 + x - d, 1 - x, n)
            remote(ref, ref, wx_s.at[j], wx_r.at[j], mate).wait_recv()

    def inward(d, carry):
        k = 4 - d
        for n in range(4):
            ref = win_piece(k, x, n)
            remote(ref, ref, wz_s.at[0], wz_r.at[k * 4 + n], up1).wait_recv()

            @pl.when(d < 4)
            def _():
                window_up(k, n).start()

            @pl.when((k >= 1) | (x == 1))
            def _():
                window_across(k, n).start()

        @pl.when(d > 1)
        def _():
            wait_mate(d - 1)

        carry = forward(jnp.where(d == 1, 8, 11 - 2 * d), carry)
        return forward(2 * k, carry)

    carry = (
        jnp.full((1, 1024), NEG, F32), jnp.zeros((1, 1024), F32), jnp.zeros((HD, 1024), F32)
    )
    carry = lax.fori_loop(1, 5, inward, carry)
    wait_mate(4)
    best, sums, out = forward(1, carry)
    inverse = 1.0 / sums
    low = (out * inverse).astype(BF)
    delta = jnp.sum(low.astype(F32) * dt[...].astype(F32), axis=0, keepdims=True)
    for t in range(2):
        for g in range(4):
            n = t * 4 + g
            att2[t, :, g * HD : (g + 1) * HD] = low[:, n * HD : (n + 1) * HD].T
    trades.append(push(att2.at[1 - c], att.at[:, mine], o_s.at[3], o_r.at[3], other))
    keep_att = pltpu.make_async_copy(att2.at[c], att.at[:, mine], out_sem.at[0])
    keep_att.start()

    def give(b):
        j = (7 - b) // 2
        return remote(dkv.at[b], x_in.at[j], bx_s.at[j], bx_r.at[j], mate)

    def merge(k):
        j = 4 - x - k
        alone = (j < 0) | (j > 3)

        @pl.when(alone)
        def _():
            own[k] = dkv[2 * k]

        @pl.when(jnp.logical_not(alone))
        def _():
            remote(x_in.at[j], x_in.at[j], bx_s.at[0], bx_r.at[j], mate).wait_recv()
            own[k] = (dkv[2 * k].astype(F32) + x_in[j].astype(F32)).astype(BF)

    def give_back(k, to):
        return remote(own.at[k], z_in.at[k], bz_s.at[k], bz_r.at[k], to)

    def back(n, query_sum):
        b = jnp.where(n == 8, 8, n + 1 - 2 * (n % 2))
        rows = part(b * 256, 256)
        k = win[0, key_rows(b), :]
        v = win[1, key_rows(b), :]
        probs = s[rows, :] * (inverse * jnp.exp2(top[pl.ds(b, 1), :] - best))
        dscores = probs * (dot(v, dt[...]) - delta)
        probs = probs.astype(BF)
        dscores = dscores.astype(BF)
        dkv[b, :, 0:HD] = (dot(dscores, qa[...]) * SCALING).astype(BF)
        dkv[b, :, HD : 2 * HD] = dot(probs, da[...]).astype(BF)

        @pl.when((n % 2 == 0) & (n < 8))
        def _():
            give(b).start()

        @pl.when(n == 3)
        def _():
            merge(0)
            give_back(0, down4).start()

        @pl.when(n == 5)
        def _():
            merge(1)
            give_back(1, down1).start()

        return query_sum + lax.dot_general(k, dscores, LEFT, preferred_element_type=F32)

    query_sum = lax.fori_loop(0, 9, back, jnp.zeros((HD, 1024), F32))
    merge(3)
    give_back(3, down1).start()
    merge(2)
    remote(z_in.at[1], z_in.at[1], bz_s.at[1], bz_r.at[1], down1).wait_recv()
    own[2] = (own[2].astype(F32) + z_in[1].astype(F32)).astype(BF)
    give_back(2, down2).start()
    query_low = (query_sum * SCALING).astype(BF)
    for t in range(2):
        for g in range(4):
            n = t * 4 + g
            gq2[t, :, g * HD : (g + 1) * HD] = query_low[:, n * HD : (n + 1) * HD].T
    trades.append(push(gq2.at[1 - c], gq.at[:, mine], o_s.at[4], o_r.at[4], other))
    keep_gq = pltpu.make_async_copy(gq2.at[c], gq.at[:, mine], out_sem.at[1])
    keep_gq.start()
    merge(4)
    for n in range(4):
        for k in range(1, 5):
            window_up(k, n).wait_send()
        for j in range(4):
            ref = win_piece(4 - x - j, x, n)
            remote(ref, ref, wx_s.at[j * 4 + n], wx_r.at[0], mate).wait_send()
    for copy in pieces + trades[:3] + [weights]:
        copy.wait_send()
    for copy in trades[3:]:
        copy.wait()
    keep_att.wait()
    keep_gq.wait()
    for k in (3, 0, 2):
        remote(z_in.at[k], z_in.at[k], bz_s.at[k], bz_r.at[k], down1).wait_recv()
    grads = (
        own[4].astype(F32) + z_in[3].astype(F32) + z_in[0].astype(F32) + z_in[2].astype(F32)
    )
    keys = grads[:, 0:HD]
    kvg[:, 0:HD] = (keys * cos[...] + pltpu.roll(keys, 64, 1) * sin[...]).astype(BF)
    kvg[:, HD : 2 * HD] = grads[:, HD : 2 * HD].astype(BF)
    crossing = push(kvg.at[part((1 - c) * 128, 128)], kvo, k_s, k_r, other)

    def outer(n, _):
        rows = part(n * 512, 512)
        wg[rows, :] = dot(hst[rows, :], kvg[...]).astype(BF)
        return 0

    lax.fori_loop(0, 8, outer, 0)

    @pl.when(c == 0)
    def _():
        for i, d in enumerate(FAR + (0,)):
            for n, e in enumerate(DY):
                push(
                    wg.at[plane(y + e, z + d)], buf0.at[i, n],
                    a_s.at[i * 3 + n], a_r.at[i * 3 + n], ys[n],
                )

    @pl.when(c == 1)
    def _():
        for n, e in enumerate((2, 1, -1, 0)):
            top = 4 if n < 2 else 3
            low = 3 if n < 2 else 4
            push(
                wg.at[plane(y + e, z + top)], plus.at[n, top - 1],
                a_s.at[n * 4 + top - 1], a_r.at[n * 4 + top - 1], zs[0],
            )
            push(
                wg.at[plane(y + e, z - low)], minus.at[n, low - 1],
                b_s.at[n * 4 + low - 1], b_r.at[n * 4 + low - 1], zs[1],
            )

    crossing.wait_recv()
    weights.wait_recv()

    def hidden(n, _):
        for m in range(2):
            span = part(n * 1024 + m * 512, 512)
            ph[n, :, m * 512 : (m + 1) * 512] = (
                lax.dot_general(kvg[toks, :], w[span, :], RIGHT, preferred_element_type=F32)
                + lax.dot_general(kvo[...], wo[span, :], RIGHT, preferred_element_type=F32)
            ).astype(BF)
        remote(ph.at[n], h_in.at[n], h_s.at[n], h_r.at[n], peer).start()
        pltpu.make_async_copy(ph.at[n], ph_out.at[n], out_sem.at[2 + n]).start()
        return 0

    lax.fori_loop(0, 4, hidden, 0)

    @pl.when(c == 0)
    def _():
        for i, d in enumerate(FAR + (0,)):
            for n in range(3):
                ref = buf0.at[i, n]
                remote(ref, ref, a_s.at[0], a_r.at[i * 3 + n], other).wait_recv()
            value = (
                wg[plane(y, z + d), :].astype(F32)
                + buf0[i, 0].astype(F32)
                + buf0[i, 1].astype(F32)
                + buf0[i, 2].astype(F32)
            )
            if d:
                acc0[i] = value.astype(BF)
                push(acc0.at[i], zin0.at[i], b_s.at[i], b_r.at[i], zs[DZ.index(d)])
            else:
                total[...] = value
        for i in range(7):
            remote(zin0.at[i], zin0.at[i], b_s.at[0], b_r.at[i], other).wait_recv()
            total[...] += zin0[i].astype(F32)

    @pl.when(c == 1)
    def _():
        def step(ref, send, recv, n, m, e, sign, to):
            remote(ref.at[n, m], ref.at[n, m], send.at[0], recv.at[n * 4 + m], other).wait_recv()
            if m:
                ref[n, m] = (
                    ref[n, m].astype(F32) + wg[plane(y + e, z + sign * m), :].astype(F32)
                ).astype(BF)
                push(
                    ref.at[n, m], ref.at[n, m - 1],
                    send.at[n * 4 + m - 1], recv.at[n * 4 + m - 1], to,
                )

        for m in (3, 2, 1, 0):
            for n, e in enumerate((2, 1, -1, 0)):
                top = 4 if n < 2 else 3
                low = 3 if n < 2 else 4
                if m < top:
                    step(plus, a_s, a_r, n, m, e, 1, zs[0])
                if m < low:
                    step(minus, b_s, b_r, n, m, e, -1, zs[1])
                if m == 0:
                    value = (
                        wg[plane(y + e, z), :].astype(F32)
                        + plus[n, 0].astype(F32)
                        + minus[n, 0].astype(F32)
                    )
                    if e:
                        acc1[n] = value.astype(BF)
                        to = DY.index(e)
                        push(acc1.at[n], yin1.at[n], m_s.at[n], m_r.at[n], ys[to])
                    else:
                        total[...] = value
        for n in range(3):
            remote(yin1.at[n], yin1.at[n], m_s.at[0], m_r.at[n], other).wait_recv()
            total[...] += yin1[n].astype(F32)

    def rows_of(xx, cc):
        return part(xx * 64 + cc * 32, 32)

    finals = [
        push(total.at[rows_of(x, 1 - c)], f_in.at[0], f_s.at[0], f_r.at[0], other),
        push(total.at[rows_of(1 - x, c)], f_in.at[1], f_s.at[1], f_r.at[1], mate),
        push(total.at[rows_of(1 - x, 1 - c)], f_in.at[2], f_s.at[2], f_r.at[2], diag),
    ]

    keep_own = pltpu.make_async_copy(total.at[rows_of(x, c)], own_out, out_sem.at[6])
    keep_own.start()
    crossing.wait_send()
    for j in range(4):
        remote(x_in.at[j], x_in.at[j], bx_s.at[j], bx_r.at[0], mate).wait_send()
        remote(z_in.at[j], z_in.at[j], bz_s.at[j], bz_r.at[0], mate).wait_send()

    @pl.when(c == 0)
    def _():
        for i in range(8):
            for n in range(3):
                ref = buf0.at[i, n]
                remote(ref, ref, a_s.at[i * 3 + n], a_r.at[0], other).wait_send()
        for i in range(7):
            remote(zin0.at[i], zin0.at[i], b_s.at[i], b_r.at[0], other).wait_send()

    @pl.when(c == 1)
    def _():
        for n in range(4):
            top = 4 if n < 2 else 3
            low = 3 if n < 2 else 4
            for m in range(top):
                remote(
                    plus.at[n, m], plus.at[n, m], a_s.at[n * 4 + m], a_r.at[0], other
                ).wait_send()
            for m in range(low):
                remote(
                    minus.at[n, m], minus.at[n, m], b_s.at[n * 4 + m], b_r.at[0], other
                ).wait_send()
        for n in range(3):
            remote(yin1.at[n], yin1.at[n], m_s.at[n], m_r.at[0], other).wait_send()

    for copy in finals:
        copy.wait()
    keep_own.wait()
    for n in range(4):
        remote(ph.at[n], h_in.at[n], h_s.at[n], h_r.at[n], peer).wait()
        pltpu.make_async_copy(ph.at[n], ph_out.at[n], out_sem.at[2 + n]).wait()


def run(wk, wv, hid, q, do, seg, table):
    dma = pltpu.SemaphoreType.DMA
    shape = jax.ShapeDtypeStruct

    def bf(*dims):
        return pltpu.VMEM(dims, BF)

    def f32(*dims):
        return pltpu.VMEM(dims, F32)

    buffers = [
        f32(256, 128), f32(256, 128), f32(16, 1024),
        bf(2, 32, 256), bf(4096, 256), bf(4096, 256), bf(256, 4096), bf(4096, 256),
        bf(128, 512), bf(128, 512), bf(128, 512), bf(128, 512), bf(2, 2560, 128),
        bf(1024, 128), bf(1024, 128), bf(128, 1024), bf(128, 1024), f32(2304, 1024),
        bf(9, 256, 256), bf(2, 128, 512), bf(2, 128, 512),
        bf(4, 256, 256), bf(5, 256, 256), bf(4, 256, 256), bf(256, 256), bf(128, 256),
        bf(4096, 256), bf(4, 128, 1024),
        bf(8, 3, 128, 256), bf(7, 128, 256), bf(7, 128, 256),
        bf(4, 4, 128, 256), bf(4, 4, 128, 256), bf(3, 128, 256), bf(3, 128, 256),
        f32(128, 256),
    ]
    counts = [3, 3, 31, 32, 5, 5, 0, 0, 20, 16, 16, 16, 4, 4, 4, 4, 0, 0, 4, 4, 24, 24, 16, 16, 3, 3, 3, 3, 3, 7]
    return pl.pallas_call(
        kernel,
        out_shape=(
            shape((128, 1024), BF),
            shape((128, 1024), BF),
            shape((4, 128, 1024), BF),
            shape((4, 128, 1024), BF),
            shape((32, 256), F32),
            shape((3, 32, 256), F32),
        ),
        in_specs=[VM, VM, ANY, ANY, ANY, VM, VM],
        out_specs=(ANY,) * 6,
        scratch_shapes=buffers + [dma((n,)) if n else dma for n in counts],
        compiler_params=pltpu.CompilerParams(
            collective_id=0, has_side_effects=True, vmem_limit_bytes=60 * 2**20
        ),
        name="layer",
    )(wk, wv, hid, q, do, seg, table)


def last_kernel(att_in, gq_in, ph, h_in, own, f_in, att, gq, gh, gk, gv):
    att[...] = att_in[...]
    gq[...] = gq_in[...]
    c = lax.axis_index("ctx") % 2
    here = own[...] + f_in[1]
    there = f_in[0] + f_in[2]
    for n in range(2):
        @pl.when(c == n)
        def _():
            for first, value in ((n, here), (1 - n, there)):
                gk[:, first * HD : (first + 1) * HD] = value[:, 0:HD]
                gv[:, first * HD : (first + 1) * HD] = value[:, HD : 2 * HD]

    for n in range(4):
        gh[:, n * 1024 : (n + 1) * 1024] = (
            ph[n].astype(F32) + h_in[n].astype(F32)
        ).astype(BF)


def last(*parts):
    shape = jax.ShapeDtypeStruct
    return pl.pallas_call(
        last_kernel,
        out_shape=(
            shape((128, 1024), BF),
            shape((128, 1024), BF),
            shape((128, 4096), BF),
            shape((32, 256), F32),
            shape((32, 256), F32),
        ),
        in_specs=[VM] * 6,
        out_specs=(VM,) * 5,
        compiler_params=pltpu.CompilerParams(vmem_limit_bytes=32 * 2**20),
        name="last",
    )(*parts)


def tables():
    frequency = 10000.0 ** (-(np.arange(64) * 2.0 / HD))
    first = (np.arange(64) * 256)[:, None] * frequency[None, :]
    within = np.arange(256)[:, None] * frequency[None, :]
    both = np.concatenate([np.cos(first), np.sin(first), np.cos(within), np.sin(within)])
    return jnp.asarray(np.concatenate([both, both], axis=1), F32)


def body(hidden_in, queries, key_weight, value_weight, seg_ids, grad_out):
    seg = seg_ids.reshape(128, 128)
    return last(*run(key_weight, value_weight, hidden_in, queries, grad_out, seg, tables()))


def solution(mesh):
    placed = (
        P("ctx", None),
        P("ctx", "head"),
        P("ctx", "head"),
        P("ctx", "head"),
        P(),
        P("ctx", "head"),
    )
    return jax.shard_map(
        body,
        mesh=mesh,
        in_specs=placed,
        out_specs=(
            P("ctx", "head"),
            P("ctx", "head"),
            P("ctx", None),
            P("ctx", "head"),
            P("ctx", "head"),
        ),
        check_vma=False,
    )
```

```python
import math

import jax
import jax.numpy as jnp
import numpy as np
from jax import lax
from jax.experimental import pallas as pl
from jax.experimental.pallas import tpu as pltpu
from jax.sharding import PartitionSpec as P

HD = 128
WINDOW = 2048
NEG = -1e30
MESH = pl.DeviceIdType.MESH
VM = pl.BlockSpec(memory_space=pltpu.VMEM)
ANY = pl.BlockSpec(memory_space=pl.ANY)
BF = jnp.bfloat16
F32 = jnp.float32
NY, NZ = 4, 8
DZ = (1, -1, 2, -2, 3, -3, 4)
DY = (1, -1, 2)
FAR = (4, 3, -3, 2, -2, 1, -1)
SCALING = 1.0 / math.sqrt(HD)
TO_EXP2 = SCALING * math.log2(math.e)
LEFT = (((0,), (0,)), ((), ()))
RIGHT = (((1,), (1,)), ((), ()))


def coords():
    i = lax.axis_index("ctx")
    return i // 32, (i // 4) % 8, (i // 2) % 2, i % 2, lax.axis_index("head")


def dev(y, z, x, c, h):
    return (((y % NY) * NZ + z % NZ) * 4 + x * 2 + c, h)


def plane_dev(p, x, c, h):
    return ((p % 32) * 4 + x * 2 + c, h)


def remote(src, dst, send, recv, to):
    return pltpu.make_async_remote_copy(
        src_ref=src, dst_ref=dst, send_sem=send, recv_sem=recv, device_id=to, device_id_type=MESH
    )


def push(src, dst, send, recv, to):
    copy = remote(src, dst, send, recv, to)
    copy.start()
    return copy


def dot(a, b):
    return jnp.dot(a, b, preferred_element_type=F32)


def part(start, size):
    return pl.ds(pl.multiple_of(start, size), size)


def kernel(
    wk, wv, hid, q, do, seg, table,
    att, gq, ph_out, h_in, own_out, f_in,
    cos, sin, top, pw, w, wo, hs, hst, q_own, d_own, qx, dx, win, qa, da, qt, dt, s, dkv, att2, gq2,
    x_in, own, z_in, kvg, kvo, wg, ph,
    buf0, acc0, zin0, plus, minus, acc1, yin1, total,
    p_s, p_r, g_s, g_r, o_s, o_r, wo_s, wo_r, wz_s, wz_r, wx_s, wx_r,
    bx_s, bx_r, bz_s, bz_r, k_s, k_r, h_s, h_r, a_s, a_r, b_s, b_r, m_s, m_r, f_s, f_r, loc, out_sem,
):
    y, z, x, c, h = coords()
    p = y * NZ + z
    chip = p * 2 + x
    other = dev(y, z, x, 1 - c, h)
    mate = dev(y, z, 1 - x, c, h)
    diag = dev(y, z, 1 - x, 1 - c, h)
    peer = dev(y, z, x, c, 1 - h)
    ys = [dev(y + d, z, x, c, h) for d in DY]
    zs = [dev(y, z + d, x, c, h) for d in DZ]
    up1, down1, up2, down2, up4, down4 = [
        plane_dev(p + d, x, c, h) for d in (1, -1, 2, -2, 4, -4)
    ]
    partners = [other, mate, diag, peer, up1, down1, up2, down2, up4, down4] + ys + zs
    barrier = pltpu.get_barrier_semaphore()
    for partner in partners:
        pl.semaphore_signal(barrier, inc=1, device_id=partner, device_id_type=MESH)
    for n in range(2):
        pw[n, :, 0:HD] = wk[:, n * HD : (n + 1) * HD]
        pw[n, :, HD : 2 * HD] = wv[:, n * HD : (n + 1) * HD]
    theirs = part((1 - c) * 512, 512)
    mine = part(c * 512, 512)
    toks = part(c * 128, 128)
    staged = [
        pltpu.make_async_copy(q.at[:, mine], q_own, loc.at[0]),
        pltpu.make_async_copy(do.at[:, mine], d_own, loc.at[1]),
        pltpu.make_async_copy(hid, hs.at[toks], loc.at[2]),
    ]
    for copy in staged:
        copy.start()
    cos_a, sin_a = table[pl.ds(chip, 1), :], table[pl.ds(64 + chip, 1), :]
    cos_b, sin_b = table[128:384, :], table[384:640, :]
    cos[...] = cos_a * cos_b - sin_a * sin_b
    lane = lax.broadcasted_iota(jnp.int32, (256, HD), 1)
    angle_sin = sin_a * cos_b + cos_a * sin_b
    sin[...] = jnp.where(lane < 64, angle_sin, -angle_sin)
    pl.semaphore_wait(barrier, len(partners))

    def plane(yy, zz):
        return part(((yy % NY) * NZ + zz % NZ) * 128, 128)

    def piece(xx, cc):
        return part(p * 128 + xx * 64 + cc * 32, 32)

    pieces = [
        push(pw.at[1 - c], w.at[piece(x, c)], p_s.at[0], p_r.at[0], other),
        push(pw.at[c], w.at[piece(x, c)], p_s.at[1], p_r.at[1], mate),
        push(pw.at[1 - c], w.at[piece(x, c)], p_s.at[2], p_r.at[2], diag),
    ]
    w[piece(x, c), :] = pw[c]
    trades = [
        push(q.at[:, theirs], qx, o_s.at[0], o_r.at[0], other),
        push(do.at[:, theirs], dx, o_s.at[1], o_r.at[1], other),
        push(hid, hs.at[toks], o_s.at[2], o_r.at[2], other),
    ]
    for copy in pieces:
        copy.wait_recv()

    def plane_sem(yy, zz):
        return g_r.at[(yy % NY) * NZ + zz % NZ]

    def wait_plane(yy, zz):
        ref = w.at[plane(yy, zz)]
        remote(ref, ref, g_s.at[0], plane_sem(yy, zz), other).wait_recv()

    @pl.when(c == 0)
    def _():
        sent = []

        def go(yy, zz, to):
            ref = w.at[plane(yy, zz)]
            sent.append(push(ref, ref, g_s.at[len(sent)], plane_sem(yy, zz), to))

        for n in range(4):
            go(y, z, zs[n])
        for to in ys:
            go(y, z, to)
        for d in DZ:
            wait_plane(y, z + d)
            if d == 2:
                go(y, z + 2, zs[1])
            if d == -2:
                go(y, z - 2, zs[0])
                go(y, z - 2, zs[2])
            for to in ys:
                go(y, z + d, to)
        for d in (0,) + DZ:
            for e in DY:
                wait_plane(y + e, z + d)
        for copy in sent:
            copy.wait_send()

    @pl.when(c == 1)
    def _():
        sent = []

        def go(yy, zz, to):
            ref = w.at[plane(yy, zz)]
            sent.append(push(ref, ref, g_s.at[len(sent)], plane_sem(yy, zz), to))

        for to in ys:
            go(y, z, to)
        up, down = zs[0], zs[1]
        for d in range(4):
            for n, e in enumerate((0,) + DY):
                if d == 0:
                    if e:
                        wait_plane(y + e, z)
                    go(y + e, z, up)
                    go(y + e, z, down)
                    continue
                wait_plane(y + e, z - d)
                if d < 3 or n < 1:
                    go(y + e, z - d, up)
                wait_plane(y + e, z + d)
                if d < 3 or n >= 1:
                    go(y + e, z + d, down)
        for e in (0,) + DY:
            wait_plane(y + e, z + 4)
        for copy in sent:
            copy.wait_send()

    for copy in trades:
        copy.wait_recv()
    for copy in staged:
        copy.wait()
    weights = push(w, wo, wo_s, wo_r, other)

    def project(n, sums):
        span = part(n * 1024, 1024)
        return sums + dot(hs[:, span], w[span, :])

    raw = lax.fori_loop(0, 4, project, jnp.zeros((256, 256), F32))

    def win_rows(k, xx):
        return part((k * 2 + xx) * 256, 256)

    def win_piece(k, xx, n):
        return win.at[n // 2, part((k * 2 + xx) * 256 + (n % 2) * 128, 128)]

    keys = raw[:, 0:HD]
    win[0, win_rows(4, x), :] = (keys * cos[...] - pltpu.roll(keys, 64, 1) * sin[...]).astype(BF)
    win[1, win_rows(4, x), :] = raw[:, HD : 2 * HD].astype(BF)

    def window_up(k, n):
        return remote(
            win_piece(k, x, n), win_piece(k - 1, x, n),
            wz_s.at[k * 4 + n], wz_r.at[(k - 1) * 4 + n], up1,
        )

    def window_across(k, n):
        j = (4 - x - k) * 4 + n
        ref = win_piece(k, x, n)
        return remote(ref, ref, wx_s.at[j], wx_r.at[j], mate)

    for n in range(4):
        window_up(4, n).start()

    @pl.when(x == 0)
    def _():
        for n in range(4):
            window_across(4, n).start()

    for t in range(2):
        @pl.when(c == t)
        def _():
            for g in range(4):
                cols = pl.ds(g * HD, HD)
                rows = pl.ds((t * 4 + g) * HD, HD)
                qa[rows, :] = q_own[:, cols]
                da[rows, :] = d_own[:, cols]

        @pl.when(c != t)
        def _():
            for g in range(4):
                rows = pl.ds((t * 4 + g) * HD, HD)
                qa[rows, :] = qx[:, g * HD : (g + 1) * HD]
                da[rows, :] = dx[:, g * HD : (g + 1) * HD]

    for n in range(8):
        block = slice(n * HD, (n + 1) * HD)
        qt[:, block] = qa[block, :].T
        dt[:, block] = da[block, :].T
    base = x * 256
    row = lax.broadcasted_iota(jnp.int32, (256, 128), 0)
    col = lax.broadcasted_iota(jnp.int32, (256, 128), 1)
    tilt = col - row

    def key_rows(b):
        return part(base + b * 256, 256)

    def forward(b, carry):
        best, sums, out = carry
        seg_k = []
        for n in range(2):
            index = chip * 2 - 16 + b * 2 + n
            line = seg[pl.ds(jnp.maximum(index, 0), 1), :].astype(F32)
            line = jnp.where(index >= 0, line, -1.0)
            seg_k.append(jnp.broadcast_to(line, (128, 128)).T)
        seg_k = jnp.concatenate(seg_k, axis=0)
        bias = []
        for t in range(2):
            seg_q = seg[pl.ds(chip * 2 + t, 1), :].astype(F32)
            gap = tilt + (WINDOW + t * 128 - b * 256)
            ok = (seg_k == seg_q) & (gap >= 0) & (gap < WINDOW)
            bias += [jnp.where(ok, 0.0, NEG)] * 4
        values = dot(win[0, key_rows(b), :], qt[...]) * TO_EXP2 + jnp.concatenate(bias, axis=1)
        higher = jnp.maximum(best, jnp.max(values, axis=0, keepdims=True))
        e = jnp.exp2(values - higher)
        s[part(b * 256, 256), :] = e
        top[pl.ds(b, 1), :] = higher
        shrink = jnp.exp2(best - higher)
        mixed = lax.dot_general(
            win[1, key_rows(b), :], e.astype(BF), LEFT, preferred_element_type=F32
        )
        return higher, sums * shrink + jnp.sum(e, axis=0, keepdims=True), out * shrink + mixed

    def turn_over(n, _):
        cols = part(n * 512, 512)
        hst[cols, :] = hs[:, cols].T
        return 0

    lax.fori_loop(0, 8, turn_over, 0)

    def wait_mate(d):
        for n in range(4):
            j = (d - 1) * 4 + n
            ref = win_piece(4 + x - d, 1 - x, n)
            remote(ref, ref, wx_s.at[j], wx_r.at[j], mate).wait_recv()

    def inward(d, carry):
        k = 4 - d
        for n in range(4):
            ref = win_piece(k, x, n)
            remote(ref, ref, wz_s.at[0], wz_r.at[k * 4 + n], up1).wait_recv()

            @pl.when(d < 4)
            def _():
                window_up(k, n).start()

            @pl.when((k >= 1) | (x == 1))
            def _():
                window_across(k, n).start()

        @pl.when(d > 1)
        def _():
            wait_mate(d - 1)

        carry = forward(jnp.where(d == 1, 8, 11 - 2 * d), carry)
        return forward(2 * k, carry)

    carry = (
        jnp.full((1, 1024), NEG, F32), jnp.zeros((1, 1024), F32), jnp.zeros((HD, 1024), F32)
    )
    carry = lax.fori_loop(1, 5, inward, carry)
    wait_mate(4)
    best, sums, out = forward(1, carry)
    inverse = 1.0 / sums
    low = (out * inverse).astype(BF)
    delta = jnp.sum(low.astype(F32) * dt[...].astype(F32), axis=0, keepdims=True)
    for t in range(2):
        for g in range(4):
            n = t * 4 + g
            att2[t, :, g * HD : (g + 1) * HD] = low[:, n * HD : (n + 1) * HD].T
    trades.append(push(att2.at[1 - c], att.at[:, mine], o_s.at[3], o_r.at[3], other))
    keep_att = pltpu.make_async_copy(att2.at[c], att.at[:, mine], out_sem.at[0])
    keep_att.start()

    def rows_half(n):
        return pl.ds(n * 128, 128)

    def give(b, n):
        j = (7 - b) // 2
        return remote(
            dkv.at[b, rows_half(n)], x_in.at[j, rows_half(n)],
            bx_s.at[j * 2 + n], bx_r.at[j * 2 + n], mate,
        )

    def pass_on(k, n):
        return remote(
            own.at[k, rows_half(n)], z_in.at[k + 1, rows_half(n)],
            bz_s.at[k * 2 + n], bz_r.at[k * 2 + n], down1,
        )

    straight = remote(own.at[0], z_in.at[0], bz_s.at[0], bz_r.at[0], down4)

    def merge(k, j, n, chain):
        rows = rows_half(n)
        value = dkv[2 * k, rows, :].astype(F32)
        if j is not None:
            ref = x_in.at[j, rows]
            remote(ref, ref, bx_s.at[0], bx_r.at[j * 2 + n], mate).wait_recv()
            value = value + x_in[j, rows, :].astype(F32)
        if chain:
            ref = z_in.at[k, rows]
            remote(ref, ref, bz_s.at[0], bz_r.at[(k - 1) * 2 + n], down1).wait_recv()
            value = value + z_in[k, rows, :].astype(F32)
        own[k, rows, :] = value.astype(BF)

    def back(n, query_sum):
        odd = n % 2
        b = jnp.where(n < 4, jnp.where(odd == 1, 3 - n, jnp.where(x == 0, 3 - n, n + 1)), n + 1 - 2 * odd)
        b = jnp.where(n == 8, 8, b)
        rows = part(b * 256, 256)
        k = win[0, key_rows(b), :]
        v = win[1, key_rows(b), :]
        probs = s[rows, :] * (inverse * jnp.exp2(top[pl.ds(b, 1), :] - best))
        dscores = probs * (dot(v, dt[...]) - delta)
        probs = probs.astype(BF)
        dscores = dscores.astype(BF)
        dkv[b, :, 0:HD] = (dot(dscores, qa[...]) * SCALING).astype(BF)
        dkv[b, :, HD : 2 * HD] = dot(probs, da[...]).astype(BF)

        @pl.when((odd == 0) & (n < 8))
        def _():
            for half in range(2):
                give(b, half).start()

        @pl.when((n == 3) & (x == 0))
        def _():
            for half in range(2):
                merge(0, None, half, False)
            straight.start()

        @pl.when(n == 5)
        def _():
            for half in range(2):
                merge(1, 3 - x, half, False)
                pass_on(1, half).start()

        return query_sum + lax.dot_general(k, dscores, LEFT, preferred_element_type=F32)

    query_sum = lax.fori_loop(0, 9, back, jnp.zeros((HD, 1024), F32))

    @pl.when(x == 1)
    def _():
        for n in range(2):
            merge(0, 3, n, False)
        straight.start()

    for k in (2, 3):
        for n in range(2):
            merge(k, 4 - x - k, n, True)
            pass_on(k, n).start()
    query_low = (query_sum * SCALING).astype(BF)
    for t in range(2):
        for g in range(4):
            n = t * 4 + g
            gq2[t, :, g * HD : (g + 1) * HD] = query_low[:, n * HD : (n + 1) * HD].T
    trades.append(push(gq2.at[1 - c], gq.at[:, mine], o_s.at[4], o_r.at[4], other))
    keep_gq = pltpu.make_async_copy(gq2.at[c], gq.at[:, mine], out_sem.at[1])
    keep_gq.start()

    for n in range(4):
        for k in range(1, 5):
            window_up(k, n).wait_send()
        for j in range(4):
            ref = win_piece(4 - x - j, x, n)
            remote(ref, ref, wx_s.at[j * 4 + n], wx_r.at[0], mate).wait_send()
    for copy in pieces + trades[:3] + [weights]:
        copy.wait_send()
    for copy in trades[3:]:
        copy.wait()
    keep_att.wait()
    keep_gq.wait()
    for n in range(2):
        @pl.when(x == 0)
        def _():
            merge(4, 0, n, True)

        @pl.when(x == 1)
        def _():
            merge(4, None, n, True)

    straight.wait_recv()
    grads = own[4].astype(F32) + z_in[0].astype(F32)
    keys = grads[:, 0:HD]
    kvg[:, 0:HD] = (keys * cos[...] + pltpu.roll(keys, 64, 1) * sin[...]).astype(BF)
    kvg[:, HD : 2 * HD] = grads[:, HD : 2 * HD].astype(BF)
    crossing = push(kvg.at[part((1 - c) * 128, 128)], kvo, k_s, k_r, other)

    def outer(n, _):
        rows = part(n * 512, 512)
        wg[rows, :] = dot(hst[rows, :], kvg[...]).astype(BF)
        return 0

    lax.fori_loop(0, 8, outer, 0)

    @pl.when(c == 0)
    def _():
        for i, d in enumerate(FAR + (0,)):
            for n, e in enumerate(DY):
                push(
                    wg.at[plane(y + e, z + d)], buf0.at[i, n],
                    a_s.at[i * 3 + n], a_r.at[i * 3 + n], ys[n],
                )

    @pl.when(c == 1)
    def _():
        for n, e in enumerate((2, 1, -1, 0)):
            top = 4 if n < 2 else 3
            low = 3 if n < 2 else 4
            push(
                wg.at[plane(y + e, z + top)], plus.at[n, top - 1],
                a_s.at[n * 4 + top - 1], a_r.at[n * 4 + top - 1], zs[0],
            )
            push(
                wg.at[plane(y + e, z - low)], minus.at[n, low - 1],
                b_s.at[n * 4 + low - 1], b_r.at[n * 4 + low - 1], zs[1],
            )

    crossing.wait_recv()
    weights.wait_recv()

    def hidden(n, _):
        for m in range(2):
            span = part(n * 1024 + m * 512, 512)
            ph[n, :, m * 512 : (m + 1) * 512] = (
                lax.dot_general(kvg[toks, :], w[span, :], RIGHT, preferred_element_type=F32)
                + lax.dot_general(kvo[...], wo[span, :], RIGHT, preferred_element_type=F32)
            ).astype(BF)
        remote(ph.at[n], h_in.at[n], h_s.at[n], h_r.at[n], peer).start()
        pltpu.make_async_copy(ph.at[n], ph_out.at[n], out_sem.at[2 + n]).start()
        return 0

    lax.fori_loop(0, 4, hidden, 0)

    @pl.when(c == 0)
    def _():
        ready = {4: (0, 1, 2, 3, 4), 5: (5,), 6: (6,)}
        for i, d in enumerate(FAR + (0,)):
            for n in range(3):
                ref = buf0.at[i, n]
                remote(ref, ref, a_s.at[0], a_r.at[i * 3 + n], other).wait_recv()
            value = (
                wg[plane(y, z + d), :].astype(F32)
                + buf0[i, 0].astype(F32)
                + buf0[i, 1].astype(F32)
                + buf0[i, 2].astype(F32)
            )
            if d:
                acc0[i] = value.astype(BF)
                for m in ready.get(i, ()):
                    push(acc0.at[m], zin0.at[m], b_s.at[m], b_r.at[m], zs[DZ.index(FAR[m])])
            else:
                total[...] = value
        for i in range(7):
            remote(zin0.at[i], zin0.at[i], b_s.at[0], b_r.at[i], other).wait_recv()
            total[...] += zin0[i].astype(F32)

    @pl.when(c == 1)
    def _():
        def step(ref, send, recv, n, m, e, sign, to):
            remote(ref.at[n, m], ref.at[n, m], send.at[0], recv.at[n * 4 + m], other).wait_recv()
            if m:
                ref[n, m] = (
                    ref[n, m].astype(F32) + wg[plane(y + e, z + sign * m), :].astype(F32)
                ).astype(BF)
                push(
                    ref.at[n, m], ref.at[n, m - 1],
                    send.at[n * 4 + m - 1], recv.at[n * 4 + m - 1], to,
                )

        for m in (3, 2, 1, 0):
            for n, e in enumerate((2, 1, -1, 0)):
                top = 4 if n < 2 else 3
                low = 3 if n < 2 else 4
                if m < top:
                    step(plus, a_s, a_r, n, m, e, 1, zs[0])
                if m < low:
                    step(minus, b_s, b_r, n, m, e, -1, zs[1])
                if m == 0:
                    value = (
                        wg[plane(y + e, z), :].astype(F32)
                        + plus[n, 0].astype(F32)
                        + minus[n, 0].astype(F32)
                    )
                    if e:
                        acc1[n] = value.astype(BF)
                        to = DY.index(e)
                        push(acc1.at[n], yin1.at[n], m_s.at[n], m_r.at[n], ys[to])
                    else:
                        total[...] = value
        for n in range(3):
            remote(yin1.at[n], yin1.at[n], m_s.at[0], m_r.at[n], other).wait_recv()
            total[...] += yin1[n].astype(F32)

    def rows_of(xx, cc):
        return part(xx * 64 + cc * 32, 32)

    finals = [
        push(total.at[rows_of(x, 1 - c)], f_in.at[0], f_s.at[0], f_r.at[0], other),
        push(total.at[rows_of(1 - x, c)], f_in.at[1], f_s.at[1], f_r.at[1], mate),
        push(total.at[rows_of(1 - x, 1 - c)], f_in.at[2], f_s.at[2], f_r.at[2], diag),
    ]

    keep_own = pltpu.make_async_copy(total.at[rows_of(x, c)], own_out, out_sem.at[6])
    keep_own.start()
    crossing.wait_send()
    for j in range(4):
        for n in range(2):
            give(7 - 2 * j, n).wait_send()
    for k in range(1, 4):
        for n in range(2):
            pass_on(k, n).wait_send()
    straight.wait_send()

    @pl.when(c == 0)
    def _():
        for i in range(8):
            for n in range(3):
                ref = buf0.at[i, n]
                remote(ref, ref, a_s.at[i * 3 + n], a_r.at[0], other).wait_send()
        for i in range(7):
            remote(zin0.at[i], zin0.at[i], b_s.at[i], b_r.at[0], other).wait_send()

    @pl.when(c == 1)
    def _():
        for n in range(4):
            top = 4 if n < 2 else 3
            low = 3 if n < 2 else 4
            for m in range(top):
                remote(
                    plus.at[n, m], plus.at[n, m], a_s.at[n * 4 + m], a_r.at[0], other
                ).wait_send()
            for m in range(low):
                remote(
                    minus.at[n, m], minus.at[n, m], b_s.at[n * 4 + m], b_r.at[0], other
                ).wait_send()
        for n in range(3):
            remote(yin1.at[n], yin1.at[n], m_s.at[n], m_r.at[0], other).wait_send()

    for copy in finals:
        copy.wait()
    keep_own.wait()
    for n in range(4):
        remote(ph.at[n], h_in.at[n], h_s.at[n], h_r.at[n], peer).wait()
        pltpu.make_async_copy(ph.at[n], ph_out.at[n], out_sem.at[2 + n]).wait()


def run(wk, wv, hid, q, do, seg, table):
    dma = pltpu.SemaphoreType.DMA
    shape = jax.ShapeDtypeStruct

    def bf(*dims):
        return pltpu.VMEM(dims, BF)

    def f32(*dims):
        return pltpu.VMEM(dims, F32)

    buffers = [
        f32(256, 128), f32(256, 128), f32(16, 1024),
        bf(2, 32, 256), bf(4096, 256), bf(4096, 256), bf(256, 4096), bf(4096, 256),
        bf(128, 512), bf(128, 512), bf(128, 512), bf(128, 512), bf(2, 2560, 128),
        bf(1024, 128), bf(1024, 128), bf(128, 1024), bf(128, 1024), f32(2304, 1024),
        bf(9, 256, 256), bf(2, 128, 512), bf(2, 128, 512),
        bf(4, 256, 256), bf(5, 256, 256), bf(5, 256, 256), bf(256, 256), bf(128, 256),
        bf(4096, 256), bf(4, 128, 1024),
        bf(8, 3, 128, 256), bf(7, 128, 256), bf(7, 128, 256),
        bf(4, 4, 128, 256), bf(4, 4, 128, 256), bf(3, 128, 256), bf(3, 128, 256),
        f32(128, 256),
    ]
    counts = [3, 3, 31, 32, 5, 5, 0, 0, 20, 16, 16, 16, 8, 8, 8, 8, 0, 0, 4, 4, 24, 24, 16, 16, 3, 3, 3, 3, 3, 7]
    return pl.pallas_call(
        kernel,
        out_shape=(
            shape((128, 1024), BF),
            shape((128, 1024), BF),
            shape((4, 128, 1024), BF),
            shape((4, 128, 1024), BF),
            shape((32, 256), F32),
            shape((3, 32, 256), F32),
        ),
        in_specs=[VM, VM, ANY, ANY, ANY, VM, VM],
        out_specs=(ANY,) * 6,
        scratch_shapes=buffers + [dma((n,)) if n else dma for n in counts],
        compiler_params=pltpu.CompilerParams(
            collective_id=0, has_side_effects=True, vmem_limit_bytes=60 * 2**20
        ),
        name="layer",
    )(wk, wv, hid, q, do, seg, table)


def last_kernel(
    att_in, gq_in, ph_in, h_in, own_in, f_in, att, gq, gh, gk, gv,
    ph, hb, at, qt, own, f, gsum, gkb, gvb, sem_in, sem_out
):
    def load(src, dst, n):
        copy = pltpu.make_async_copy(src, dst, sem_in.at[n])
        copy.start()
        return copy

    def store(src, dst, n):
        copy = pltpu.make_async_copy(src, dst, sem_out.at[n])
        copy.start()
        return copy

    parts = [
        (load(ph_in.at[n], ph.at[n], n), load(h_in.at[n], hb.at[n], 4 + n)) for n in range(4)
    ]
    small = [load(own_in, own, 8), load(f_in, f, 9)]
    whole = [load(att_in, at, 10), load(gq_in, qt, 11)]
    stores = []
    for n in range(4):
        for copy in parts[n]:
            copy.wait()
        gsum[:, n * 1024 : (n + 1) * 1024] = (ph[n].astype(F32) + hb[n].astype(F32)).astype(BF)
        cols = pl.ds(n * 1024, 1024)
        stores.append(store(gsum.at[:, cols], gh.at[:, cols], n))
    for n, (copy, src, dst) in enumerate(((whole[0], at, att), (whole[1], qt, gq))):
        copy.wait()
        stores.append(store(src, dst, 4 + n))
    for copy in small:
        copy.wait()
    c = lax.axis_index("ctx") % 2
    here = own[...] + f[1]
    there = f[0] + f[2]
    for n in range(2):
        @pl.when(c == n)
        def _():
            for first, value in ((n, here), (1 - n, there)):
                gkb[:, first * HD : (first + 1) * HD] = value[:, 0:HD]
                gvb[:, first * HD : (first + 1) * HD] = value[:, HD : 2 * HD]

    stores += [store(gkb, gk, 6), store(gvb, gv, 7)]
    for copy in stores:
        copy.wait()


def last(*parts):
    dma = pltpu.SemaphoreType.DMA
    results = (
        jax.ShapeDtypeStruct((128, 1024), BF),
        jax.ShapeDtypeStruct((128, 1024), BF),
        jax.ShapeDtypeStruct((128, 4096), BF),
        jax.ShapeDtypeStruct((32, 256), F32),
        jax.ShapeDtypeStruct((32, 256), F32),
    )
    return pl.pallas_call(
        last_kernel,
        out_shape=results,
        in_specs=[ANY] * 6,
        out_specs=(ANY,) * 5,
        scratch_shapes=[
            pltpu.VMEM((4, 128, 1024), BF),
            pltpu.VMEM((4, 128, 1024), BF),
            pltpu.VMEM((128, 1024), BF),
            pltpu.VMEM((128, 1024), BF),
            pltpu.VMEM((32, 256), F32),
            pltpu.VMEM((3, 32, 256), F32),
            pltpu.VMEM((128, 4096), BF),
            pltpu.VMEM((32, 256), F32),
            pltpu.VMEM((32, 256), F32),
            dma((12,)),
            dma((8,)),
        ],
        compiler_params=pltpu.CompilerParams(vmem_limit_bytes=60 * 2**20),
        name="last",
    )(*parts)


def tables():
    frequency = 10000.0 ** (-(np.arange(64) * 2.0 / HD))
    first = (np.arange(64) * 256)[:, None] * frequency[None, :]
    within = np.arange(256)[:, None] * frequency[None, :]
    both = np.concatenate([np.cos(first), np.sin(first), np.cos(within), np.sin(within)])
    return jnp.asarray(np.concatenate([both, both], axis=1), F32)


def body(hidden_in, queries, key_weight, value_weight, seg_ids, grad_out):
    seg = seg_ids.reshape(128, 128)
    return last(*run(key_weight, value_weight, hidden_in, queries, grad_out, seg, tables()))


def solution(mesh):
    placed = (
        P("ctx", None),
        P("ctx", "head"),
        P("ctx", "head"),
        P("ctx", "head"),
        P(),
        P("ctx", "head"),
    )
    return jax.shard_map(
        body,
        mesh=mesh,
        in_specs=placed,
        out_specs=(
            P("ctx", "head"),
            P("ctx", "head"),
            P("ctx", None),
            P("ctx", "head"),
            P("ctx", "head"),
        ),
        check_vma=False,
    )
```

```python
import math

import jax
import jax.numpy as jnp
import numpy as np
from jax import lax
from jax.experimental import pallas as pl
from jax.experimental.pallas import tpu as pltpu
from jax.sharding import PartitionSpec as P

HD = 128
WINDOW = 2048
NEG = -1e30
MESH = pl.DeviceIdType.MESH
VM = pl.BlockSpec(memory_space=pltpu.VMEM)
ANY = pl.BlockSpec(memory_space=pl.ANY)
BF = jnp.bfloat16
F32 = jnp.float32
NY, NZ = 4, 8
DZ = (1, -1, 2, -2, 3, -3, 4)
DY = (1, -1, 2)
FAR = (4, 3, -3, 2, -2, 1, -1)
SCALING = 1.0 / math.sqrt(HD)
TO_EXP2 = SCALING * math.log2(math.e)
LEFT = (((0,), (0,)), ((), ()))
RIGHT = (((1,), (1,)), ((), ()))


def coords():
    i = lax.axis_index("ctx")
    return i // 32, (i // 4) % 8, (i // 2) % 2, i % 2, lax.axis_index("head")


def dev(y, z, x, c, h):
    return (((y % NY) * NZ + z % NZ) * 4 + x * 2 + c, h)


def plane_dev(p, x, c, h):
    return ((p % 32) * 4 + x * 2 + c, h)


def remote(src, dst, send, recv, to):
    return pltpu.make_async_remote_copy(
        src_ref=src, dst_ref=dst, send_sem=send, recv_sem=recv, device_id=to, device_id_type=MESH
    )


def push(src, dst, send, recv, to):
    copy = remote(src, dst, send, recv, to)
    copy.start()
    return copy


def all_sent(ref, sem, to):
    remote(ref, ref, sem, sem, to).wait_send()


def dot(a, b):
    return jnp.dot(a, b, preferred_element_type=F32)


def part(start, size):
    return pl.ds(pl.multiple_of(start, size), size)


def kernel(
    wk, wv, hid, q, do, seg, table,
    att, gq, ph_out, h_in, own_out, f_in,
    cos, sin, top, pw, w, wo, hs, hst, q_own, d_own, qx, dx, win, qa, da, qt, dt, s, dkv, att2, gq2,
    x_in, own, z_in, kvg, kvo, wg, ph,
    relay, buf0, acc0, zin0, plus, minus, acc1, yin1, total,
    p_s, p_r, g_s, g_r, v_s, v_r, o_s, o_r, wo_s, wo_r, wz_s, wz_r, wx_s, wx_r,
    bx_s, bx_r, bz_s, bz_r, k_s, k_r, h_s, h_r, l_r, a_s, a_r, b_s, b_r, m_s, m_r, f_s, f_r, loc, out_sem,
):
    y, z, x, c, h = coords()
    p = y * NZ + z
    chip = p * 2 + x
    other = dev(y, z, x, 1 - c, h)
    mate = dev(y, z, 1 - x, c, h)
    diag = dev(y, z, 1 - x, 1 - c, h)
    peer = dev(y, z, x, c, 1 - h)
    ys = [dev(y + d, z, x, c, h) for d in DY]
    zs = [dev(y, z + d, x, c, h) for d in DZ]
    up1, down1 = plane_dev(p + 1, x, c, h), plane_dev(p - 1, x, c, h)
    partners = [other, mate, diag, peer, up1, down1] + ys + zs
    barrier = pltpu.get_barrier_semaphore()
    for partner in partners:
        pl.semaphore_signal(barrier, inc=1, device_id=partner, device_id_type=MESH)
    for n in range(2):
        pw[n, :, 0:HD] = wk[:, n * HD : (n + 1) * HD]
        pw[n, :, HD : 2 * HD] = wv[:, n * HD : (n + 1) * HD]
    theirs = part((1 - c) * 512, 512)
    mine = part(c * 512, 512)
    toks = part(c * 128, 128)
    staged = [
        pltpu.make_async_copy(q.at[:, mine], q_own, loc.at[0]),
        pltpu.make_async_copy(do.at[:, mine], d_own, loc.at[1]),
        pltpu.make_async_copy(hid, hs.at[toks], loc.at[2]),
    ]
    for copy in staged:
        copy.start()
    cos_a, sin_a = table[pl.ds(chip, 1), :], table[pl.ds(64 + chip, 1), :]
    cos_b, sin_b = table[128:384, :], table[384:640, :]
    cos[...] = cos_a * cos_b - sin_a * sin_b
    lane = lax.broadcasted_iota(jnp.int32, (256, HD), 1)
    angle_sin = sin_a * cos_b + cos_a * sin_b
    sin[...] = jnp.where(lane < 64, angle_sin, -angle_sin)
    pl.semaphore_wait(barrier, len(partners))

    def plane(yy, zz):
        return part(((yy % NY) * NZ + zz % NZ) * 128, 128)

    def piece(xx, cc):
        return part(p * 128 + xx * 64 + cc * 32, 32)

    pieces = [
        push(pw.at[1 - c], w.at[piece(x, c)], p_s, p_r.at[0], other),
        push(pw.at[c], w.at[piece(x, c)], p_s, p_r.at[1], mate),
        push(pw.at[1 - c], w.at[piece(x, c)], p_s, p_r.at[2], diag),
    ]
    w[piece(x, c), :] = pw[c]
    trades = [
        push(q.at[:, theirs], qx, o_s.at[0], o_r.at[0], other),
        push(do.at[:, theirs], dx, o_s.at[1], o_r.at[1], other),
        push(hid, hs.at[toks], o_s.at[2], o_r.at[2], other),
    ]
    for copy in pieces:
        copy.wait_recv()

    def plane_sem(yy, zz):
        return g_r.at[(yy % NY) * NZ + zz % NZ]

    def wait_plane(yy, zz):
        ref = w.at[plane(yy, zz)]
        remote(ref, ref, g_s, plane_sem(yy, zz), other).wait_recv()

    @pl.when(c == 0)
    def _():
        def go(yy, zz, to):
            ref = w.at[plane(yy, zz)]
            push(ref, ref, g_s, plane_sem(yy, zz), to)

        for n in range(4):
            go(y, z, zs[n])
        for to in ys:
            go(y, z, to)
        for d in DZ:
            wait_plane(y, z + d)
            if d == 2:
                go(y, z + 2, zs[1])
            if d == -2:
                go(y, z - 2, zs[0])
                go(y, z - 2, zs[2])
            for to in ys:
                go(y, z + d, to)
        for d in (0,) + DZ:
            for e in DY:
                wait_plane(y + e, z + d)
        all_sent(w.at[pl.ds(0, 31 * 128)], g_s, other)

    @pl.when(c == 1)
    def _():
        def half(yy, zz):
            return w.at[part(((yy % NY) * NZ + zz % NZ) * 128 + x * 64, 64)]

        def go(yy, zz, to):
            ref = half(yy, zz)
            push(ref, ref, g_s, plane_sem(yy, zz), to)

        def wait_half(yy, zz):
            ref = half(yy, zz)
            remote(ref, ref, g_s, plane_sem(yy, zz), other).wait_recv()

        def share(yy, zz):
            ref = half(yy, zz)
            push(ref, ref, v_s, v_r, mate)

        for to in ys:
            go(y, z, to)
        up, down = zs[0], zs[1]
        for d in range(4):
            for n, e in enumerate((0,) + DY):
                if d == 0:
                    if e:
                        wait_half(y + e, z)
                    go(y + e, z, up)
                    go(y + e, z, down)
                    if e:
                        share(y + e, z)
                    continue
                wait_half(y + e, z - d)
                if d < 3 or n < 2:
                    go(y + e, z - d, up)
                share(y + e, z - d)
                wait_half(y + e, z + d)
                if d < 3 or n >= 2:
                    go(y + e, z + d, down)
                share(y + e, z + d)
        for e in (0,) + DY:
            wait_half(y + e, z + 4)
            share(y + e, z + 4)
        ref = w.at[pl.ds(0, 31 * 64)]
        remote(ref, ref, v_s, v_r, mate).wait()
        all_sent(ref, g_s, other)

    for copy in trades:
        copy.wait_recv()
    for copy in staged:
        copy.wait()
    weights = push(w, wo, wo_s, wo_r, other)

    def project(n, sums):
        span = part(n * 1024, 1024)
        return sums + dot(hs[:, span], w[span, :])

    raw = lax.fori_loop(0, 4, project, jnp.zeros((256, 256), F32))

    def win_rows(k, xx):
        return part((k * 2 + xx) * 256, 256)

    def win_piece(k, xx, n):
        return win.at[n // 2, part((k * 2 + xx) * 256 + (n % 2) * 128, 128)]

    keys = raw[:, 0:HD]
    win[0, win_rows(4, x), :] = (keys * cos[...] - pltpu.roll(keys, 64, 1) * sin[...]).astype(BF)
    win[1, win_rows(4, x), :] = raw[:, HD : 2 * HD].astype(BF)

    def window_up(k, n):
        return remote(
            win_piece(k, x, n), win_piece(k - 1, x, n),
            wz_s, wz_r.at[(k - 1) * 4 + n], up1,
        )

    def window_across(k, n):
        ref = win_piece(k, x, n)
        return remote(ref, ref, wx_s, wx_r.at[4 - x - k], mate)

    for n in range(4):
        window_up(4, n).start()

    @pl.when(x == 0)
    def _():
        for n in range(4):
            window_across(4, n).start()

    for t in range(2):
        @pl.when(c == t)
        def _():
            for g in range(4):
                cols = pl.ds(g * HD, HD)
                rows = pl.ds((t * 4 + g) * HD, HD)
                qa[rows, :] = q_own[:, cols]
                da[rows, :] = d_own[:, cols]

        @pl.when(c != t)
        def _():
            for g in range(4):
                rows = pl.ds((t * 4 + g) * HD, HD)
                qa[rows, :] = qx[:, g * HD : (g + 1) * HD]
                da[rows, :] = dx[:, g * HD : (g + 1) * HD]

    for n in range(8):
        block = slice(n * HD, (n + 1) * HD)
        qt[:, block] = qa[block, :].T
        dt[:, block] = da[block, :].T
    base = x * 256
    row = lax.broadcasted_iota(jnp.int32, (256, 128), 0)
    col = lax.broadcasted_iota(jnp.int32, (256, 128), 1)
    tilt = col - row

    def key_rows(b):
        return part(base + b * 256, 256)

    def forward(b, carry):
        best, sums, out = carry
        seg_k = []
        for n in range(2):
            index = chip * 2 - 16 + b * 2 + n
            line = seg[pl.ds(jnp.maximum(index, 0), 1), :].astype(F32)
            line = jnp.where(index >= 0, line, -1.0)
            seg_k.append(jnp.broadcast_to(line, (128, 128)).T)
        seg_k = jnp.concatenate(seg_k, axis=0)
        bias = []
        for t in range(2):
            seg_q = seg[pl.ds(chip * 2 + t, 1), :].astype(F32)
            gap = tilt + (WINDOW + t * 128 - b * 256)
            ok = (seg_k == seg_q) & (gap >= 0) & (gap < WINDOW)
            bias += [jnp.where(ok, 0.0, NEG)] * 4
        values = dot(win[0, key_rows(b), :], qt[...]) * TO_EXP2 + jnp.concatenate(bias, axis=1)
        higher = jnp.maximum(best, jnp.max(values, axis=0, keepdims=True))
        e = jnp.exp2(values - higher)
        s[part(b * 256, 256), :] = e
        top[pl.ds(b, 1), :] = higher
        shrink = jnp.exp2(best - higher)
        mixed = lax.dot_general(
            win[1, key_rows(b), :], e.astype(BF), LEFT, preferred_element_type=F32
        )
        return higher, sums * shrink + jnp.sum(e, axis=0, keepdims=True), out * shrink + mixed

    def turn_over(n, _):
        cols = part(n * 512, 512)
        hst[cols, :] = hs[:, cols].T
        return 0

    lax.fori_loop(0, 8, turn_over, 0)

    def wait_mate(d):
        ref = win.at[:, win_rows(4 + x - d, 1 - x)]
        remote(ref, ref, wx_s, wx_r.at[d - 1], mate).wait_recv()

    def inward(d, carry):
        k = 4 - d
        for n in range(4):
            ref = win_piece(k, x, n)
            remote(ref, ref, wz_s, wz_r.at[k * 4 + n], up1).wait_recv()

            @pl.when(d < 4)
            def _():
                window_up(k, n).start()

            @pl.when((k >= 1) | (x == 1))
            def _():
                window_across(k, n).start()

        @pl.when(d > 1)
        def _():
            wait_mate(d - 1)

        carry = forward(jnp.where(d == 1, 8, 11 - 2 * d), carry)
        return forward(2 * k, carry)

    carry = (
        jnp.full((1, 1024), NEG, F32), jnp.zeros((1, 1024), F32), jnp.zeros((HD, 1024), F32)
    )
    carry = lax.fori_loop(1, 5, inward, carry)
    wait_mate(4)
    best, sums, out = forward(1, carry)
    inverse = 1.0 / sums
    low = (out * inverse).astype(BF)
    delta = jnp.sum(low.astype(F32) * dt[...].astype(F32), axis=0, keepdims=True)
    for t in range(2):
        for g in range(4):
            n = t * 4 + g
            att2[t, :, g * HD : (g + 1) * HD] = low[:, n * HD : (n + 1) * HD].T
    trades.append(push(att2.at[1 - c], att.at[:, mine], o_s.at[3], o_r.at[3], other))
    keep_att = pltpu.make_async_copy(att2.at[c], att.at[:, mine], out_sem.at[0])
    keep_att.start()

    def rows_of_piece(n):
        return pl.ds(n * 64, 64)

    def give(b, n):
        j = (7 - b) // 2
        return remote(
            dkv.at[b, rows_of_piece(n)], x_in.at[j, rows_of_piece(n)],
            bx_s, bx_r.at[j * 4 + n], mate,
        )

    def pass_on(k, n):
        return remote(
            own.at[k, rows_of_piece(n)], z_in.at[k + 1, rows_of_piece(n)],
            bz_s, bz_r.at[k * 4 + n], down1,
        )


    def merge(k, j, n, chain):
        rows = rows_of_piece(n)
        value = dkv[2 * k, rows, :].astype(F32)
        if j is not None:
            ref = x_in.at[j, rows]
            remote(ref, ref, bx_s, bx_r.at[j * 4 + n], mate).wait_recv()
            value = value + x_in[j, rows, :].astype(F32)
        if chain:
            ref = z_in.at[k, rows]
            remote(ref, ref, bz_s, bz_r.at[(k - 1) * 4 + n], down1).wait_recv()
            value = value + z_in[k, rows, :].astype(F32)
        own[k, rows, :] = value.astype(BF)

    def back(n, query_sum):
        odd = n % 2
        b = jnp.where(n == 8, 8, n + 1 - 2 * odd)
        rows = part(b * 256, 256)
        k = win[0, key_rows(b), :]
        v = win[1, key_rows(b), :]
        probs = s[rows, :] * (inverse * jnp.exp2(top[pl.ds(b, 1), :] - best))
        dscores = probs * (dot(v, dt[...]) - delta)
        probs = probs.astype(BF)
        dscores = dscores.astype(BF)
        dkv[b, :, 0:HD] = (dot(dscores, qa[...]) * SCALING).astype(BF)
        dkv[b, :, HD : 2 * HD] = dot(probs, da[...]).astype(BF)

        @pl.when((odd == 0) & (n < 8))
        def _():
            for piece in range(4):
                give(b, piece).start()

        @pl.when((n == 1) & (x == 0))
        def _():
            for piece in range(4):
                merge(0, None, piece, False)
                pass_on(0, piece).start()

        @pl.when((n == 6) & (x == 1))
        def _():
            for piece in range(4):
                merge(0, 3, piece, False)
                pass_on(0, piece).start()

        @pl.when((n == 6) & (x == 0))
        def _():
            for piece in range(4):
                merge(1, 3, piece, True)
                pass_on(1, piece).start()

        return query_sum + lax.dot_general(k, dscores, LEFT, preferred_element_type=F32)

    query_sum = lax.fori_loop(0, 9, back, jnp.zeros((HD, 1024), F32))

    @pl.when(x == 1)
    def _():
        for n in range(4):
            merge(1, 2, n, True)
            pass_on(1, n).start()

    for k in (2, 3):
        for n in range(4):
            merge(k, 4 - x - k, n, True)
            pass_on(k, n).start()
    query_low = (query_sum * SCALING).astype(BF)
    for t in range(2):
        for g in range(4):
            n = t * 4 + g
            gq2[t, :, g * HD : (g + 1) * HD] = query_low[:, n * HD : (n + 1) * HD].T
    trades.append(push(gq2.at[1 - c], gq.at[:, mine], o_s.at[4], o_r.at[4], other))
    keep_gq = pltpu.make_async_copy(gq2.at[c], gq.at[:, mine], out_sem.at[1])
    keep_gq.start()

    all_sent(win.at[0, pl.ds(0, 2048)], wz_s, up1)
    all_sent(win.at[0, pl.ds(0, 2048)], wx_s, mate)
    all_sent(w.at[pl.ds(0, 96)], p_s, other)
    for copy in trades[:3] + [weights]:
        copy.wait_send()
    for copy in trades[3:]:
        copy.wait()
    keep_att.wait()
    keep_gq.wait()
    for n in range(4):
        @pl.when(x == 0)
        def _():
            merge(4, 0, n, True)

        @pl.when(x == 1)
        def _():
            merge(4, None, n, True)

    grads = own[4].astype(F32)
    keys = grads[:, 0:HD]
    kvg[:, 0:HD] = (keys * cos[...] + pltpu.roll(keys, 64, 1) * sin[...]).astype(BF)
    kvg[:, HD : 2 * HD] = grads[:, HD : 2 * HD].astype(BF)
    crossing = push(kvg.at[part((1 - c) * 128, 128)], kvo, k_s, k_r, other)

    def outer(n, _):
        rows = part(n * 512, 512)
        wg[rows, :] = dot(hst[rows, :], kvg[...]).astype(BF)
        return 0

    lax.fori_loop(0, 8, outer, 0)

    @pl.when(c == 0)
    def _():
        for i, d in enumerate(FAR + (0,)):
            push(wg.at[plane(y + 2, z + d)], relay.at[i], a_s, l_r.at[i], ys[i % 2])
        for i, d in enumerate(FAR + (0,)):
            n = 1 - i % 2
            push(wg.at[plane(y + DY[n], z + d)], buf0.at[i, n], a_s, a_r.at[i * 2 + n], ys[n])

    @pl.when(c == 1)
    def _():
        for n, e in enumerate((2, 1, -1, 0)):
            top = 4 if n < 2 else 3
            low = 3 if n < 2 else 4
            push(
                wg.at[plane(y + e, z + top)], plus.at[n, top - 1],
                a_s, a_r.at[n * 4 + top - 1], zs[0],
            )
            push(
                wg.at[plane(y + e, z - low)], minus.at[n, low - 1],
                b_s, b_r.at[n * 4 + low - 1], zs[1],
            )

    crossing.wait_recv()
    weights.wait_recv()

    def hidden(n, _):
        for m in range(2):
            span = part(n * 1024 + m * 512, 512)
            ph[n, :, m * 512 : (m + 1) * 512] = (
                lax.dot_general(kvg[toks, :], w[span, :], RIGHT, preferred_element_type=F32)
                + lax.dot_general(kvo[...], wo[span, :], RIGHT, preferred_element_type=F32)
            ).astype(BF)
        remote(ph.at[n], h_in.at[n], h_s.at[n], h_r.at[n], peer).start()
        pltpu.make_async_copy(ph.at[n], ph_out.at[n], out_sem.at[2 + n]).start()
        return 0

    lax.fori_loop(0, 4, hidden, 0)

    @pl.when(c == 0)
    def _():
        for i, d in enumerate(FAR + (0,)):
            n = i % 2
            remote(relay.at[i], relay.at[i], a_s, l_r.at[i], other).wait_recv()
            relay[i] = (
                relay[i].astype(F32) + wg[plane(y + DY[n], z + d), :].astype(F32)
            ).astype(BF)
            push(relay.at[i], buf0.at[i, n], a_s, a_r.at[i * 2 + n], ys[n])
        ready = {4: (0, 1, 2, 3, 4), 5: (5,), 6: (6,)}
        for i, d in enumerate(FAR + (0,)):
            for n in range(2):
                ref = buf0.at[i, n]
                remote(ref, ref, a_s, a_r.at[i * 2 + n], other).wait_recv()
            value = (
                wg[plane(y, z + d), :].astype(F32)
                + buf0[i, 0].astype(F32)
                + buf0[i, 1].astype(F32)
            )
            if d:
                acc0[i] = value.astype(BF)
                for m in ready.get(i, ()):
                    push(acc0.at[m], zin0.at[m], b_s, b_r.at[m], zs[DZ.index(FAR[m])])
            else:
                total[...] = value
        for i in range(7):
            remote(zin0.at[i], zin0.at[i], b_s, b_r.at[i], other).wait_recv()
            total[...] += zin0[i].astype(F32)

    @pl.when(c == 1)
    def _():
        def step(ref, send, recv, n, m, e, sign, to):
            remote(ref.at[n, m], ref.at[n, m], send, recv.at[n * 4 + m], other).wait_recv()
            if m:
                ref[n, m] = (
                    ref[n, m].astype(F32) + wg[plane(y + e, z + sign * m), :].astype(F32)
                ).astype(BF)
                push(
                    ref.at[n, m], ref.at[n, m - 1],
                    send, recv.at[n * 4 + m - 1], to,
                )

        for m in (3, 2, 1, 0):
            for n, e in enumerate((2, 1, -1, 0)):
                top = 4 if n < 2 else 3
                low = 3 if n < 2 else 4
                if m < top:
                    step(plus, a_s, a_r, n, m, e, 1, zs[0])
                if m < low:
                    step(minus, b_s, b_r, n, m, e, -1, zs[1])
                if m == 0:
                    value = (
                        wg[plane(y + e, z), :].astype(F32)
                        + plus[n, 0].astype(F32)
                        + minus[n, 0].astype(F32)
                    )
                    if e:
                        acc1[n] = value.astype(BF)
                        to = DY.index(e)
                        push(acc1.at[n], yin1.at[n], m_s, m_r.at[n], ys[to])
                    else:
                        total[...] = value
        for n in range(3):
            remote(yin1.at[n], yin1.at[n], m_s, m_r.at[n], other).wait_recv()
            total[...] += yin1[n].astype(F32)

    def rows_of(xx, cc):
        return part(xx * 64 + cc * 32, 32)

    finals = [
        push(total.at[rows_of(x, 1 - c)], f_in.at[0], f_s.at[0], f_r.at[0], other),
        push(total.at[rows_of(1 - x, c)], f_in.at[1], f_s.at[1], f_r.at[1], mate),
        push(total.at[rows_of(1 - x, 1 - c)], f_in.at[2], f_s.at[2], f_r.at[2], diag),
    ]

    keep_own = pltpu.make_async_copy(total.at[rows_of(x, c)], own_out, out_sem.at[6])
    keep_own.start()
    crossing.wait_send()
    all_sent(x_in, bx_s, mate)
    all_sent(x_in, bz_s, down1)

    @pl.when(c == 0)
    def _():
        all_sent(wg.at[pl.ds(0, 24 * 128)], a_s, other)
        all_sent(zin0, b_s, other)

    @pl.when(c == 1)
    def _():
        all_sent(wg.at[pl.ds(0, 14 * 128)], a_s, other)
        all_sent(wg.at[pl.ds(0, 14 * 128)], b_s, other)
        all_sent(yin1, m_s, other)

    for copy in finals:
        copy.wait()
    keep_own.wait()
    for n in range(4):
        remote(ph.at[n], h_in.at[n], h_s.at[n], h_r.at[n], peer).wait()
        pltpu.make_async_copy(ph.at[n], ph_out.at[n], out_sem.at[2 + n]).wait()


def run(wk, wv, hid, q, do, seg, table):
    dma = pltpu.SemaphoreType.DMA
    shape = jax.ShapeDtypeStruct

    def bf(*dims):
        return pltpu.VMEM(dims, BF)

    def f32(*dims):
        return pltpu.VMEM(dims, F32)

    buffers = [
        f32(256, 128), f32(256, 128), f32(16, 1024),
        bf(2, 32, 256), bf(4096, 256), bf(4096, 256), bf(256, 4096), bf(4096, 256),
        bf(128, 512), bf(128, 512), bf(128, 512), bf(128, 512), bf(2, 2560, 128),
        bf(1024, 128), bf(1024, 128), bf(128, 1024), bf(128, 1024), f32(2304, 1024),
        bf(9, 256, 256), bf(2, 128, 512), bf(2, 128, 512),
        bf(4, 256, 256), bf(5, 256, 256), bf(5, 256, 256), bf(256, 256), bf(128, 256),
        bf(4096, 256), bf(4, 128, 1024),
        bf(8, 128, 256), bf(8, 2, 128, 256), bf(7, 128, 256), bf(7, 128, 256),
        bf(4, 4, 128, 256), bf(4, 4, 128, 256), bf(3, 128, 256), bf(3, 128, 256),
        f32(128, 256),
    ]
    counts = [
        0, 3, 0, 32, 0, 0, 5, 5, 0, 0, 0, 16, 0, 4, 0, 16,
        0, 16, 0, 0, 4, 4, 8, 0, 16, 0, 16, 0, 3, 3, 3, 3, 7,
    ]
    return pl.pallas_call(
        kernel,
        out_shape=(
            shape((128, 1024), BF),
            shape((128, 1024), BF),
            shape((4, 128, 1024), BF),
            shape((4, 128, 1024), BF),
            shape((32, 256), F32),
            shape((3, 32, 256), F32),
        ),
        in_specs=[VM, VM, ANY, ANY, ANY, VM, VM],
        out_specs=(ANY,) * 6,
        scratch_shapes=buffers + [dma((n,)) if n else dma for n in counts],
        compiler_params=pltpu.CompilerParams(
            collective_id=0, has_side_effects=True, vmem_limit_bytes=60 * 2**20
        ),
        name="layer",
    )(wk, wv, hid, q, do, seg, table)


def last_kernel(
    att_in, gq_in, ph_in, h_in, own_in, f_in, att, gq, gh, gk, gv,
    ph, hb, at, qt, own, f, gsum, gkb, gvb, sem_in, sem_out
):
    def load(src, dst, n):
        copy = pltpu.make_async_copy(src, dst, sem_in.at[n])
        copy.start()
        return copy

    def store(src, dst, n):
        copy = pltpu.make_async_copy(src, dst, sem_out.at[n])
        copy.start()
        return copy

    parts = [
        (load(ph_in.at[n], ph.at[n], n), load(h_in.at[n], hb.at[n], 4 + n)) for n in range(4)
    ]
    small = [load(own_in, own, 8), load(f_in, f, 9)]
    whole = [load(att_in, at, 10), load(gq_in, qt, 11)]
    stores = []
    for n in range(4):
        for copy in parts[n]:
            copy.wait()
        gsum[:, n * 1024 : (n + 1) * 1024] = (ph[n].astype(F32) + hb[n].astype(F32)).astype(BF)
        cols = pl.ds(n * 1024, 1024)
        stores.append(store(gsum.at[:, cols], gh.at[:, cols], n))
    for n, (copy, src, dst) in enumerate(((whole[0], at, att), (whole[1], qt, gq))):
        copy.wait()
        stores.append(store(src, dst, 4 + n))
    for copy in small:
        copy.wait()
    c = lax.axis_index("ctx") % 2
    here = own[...] + f[1]
    there = f[0] + f[2]
    for n in range(2):
        @pl.when(c == n)
        def _():
            for first, value in ((n, here), (1 - n, there)):
                gkb[:, first * HD : (first + 1) * HD] = value[:, 0:HD]
                gvb[:, first * HD : (first + 1) * HD] = value[:, HD : 2 * HD]

    stores += [store(gkb, gk, 6), store(gvb, gv, 7)]
    for copy in stores:
        copy.wait()


def last(*parts):
    dma = pltpu.SemaphoreType.DMA
    results = (
        jax.ShapeDtypeStruct((128, 1024), BF),
        jax.ShapeDtypeStruct((128, 1024), BF),
        jax.ShapeDtypeStruct((128, 4096), BF),
        jax.ShapeDtypeStruct((32, 256), F32),
        jax.ShapeDtypeStruct((32, 256), F32),
    )
    return pl.pallas_call(
        last_kernel,
        out_shape=results,
        in_specs=[ANY] * 6,
        out_specs=(ANY,) * 5,
        scratch_shapes=[
            pltpu.VMEM((4, 128, 1024), BF),
            pltpu.VMEM((4, 128, 1024), BF),
            pltpu.VMEM((128, 1024), BF),
            pltpu.VMEM((128, 1024), BF),
            pltpu.VMEM((32, 256), F32),
            pltpu.VMEM((3, 32, 256), F32),
            pltpu.VMEM((128, 4096), BF),
            pltpu.VMEM((32, 256), F32),
            pltpu.VMEM((32, 256), F32),
            dma((12,)),
            dma((8,)),
        ],
        compiler_params=pltpu.CompilerParams(vmem_limit_bytes=60 * 2**20),
        name="last",
    )(*parts)


def tables():
    frequency = 10000.0 ** (-(np.arange(64) * 2.0 / HD))
    first = (np.arange(64) * 256)[:, None] * frequency[None, :]
    within = np.arange(256)[:, None] * frequency[None, :]
    both = np.concatenate([np.cos(first), np.sin(first), np.cos(within), np.sin(within)])
    return jnp.asarray(np.concatenate([both, both], axis=1), F32)


def body(hidden_in, queries, key_weight, value_weight, seg_ids, grad_out):
    seg = seg_ids.reshape(128, 128)
    return last(*run(key_weight, value_weight, hidden_in, queries, grad_out, seg, tables()))


def solution(mesh):
    placed = (
        P("ctx", None),
        P("ctx", "head"),
        P("ctx", "head"),
        P("ctx", "head"),
        P(),
        P("ctx", "head"),
    )
    return jax.shard_map(
        body,
        mesh=mesh,
        in_specs=placed,
        out_specs=(
            P("ctx", "head"),
            P("ctx", "head"),
            P("ctx", None),
            P("ctx", "head"),
            P("ctx", "head"),
        ),
        check_vma=False,
    )
```

```python
import math

import jax
import jax.numpy as jnp
import numpy as np
from jax import lax
from jax.experimental import pallas as pl
from jax.experimental.pallas import tpu as pltpu
from jax.sharding import PartitionSpec as P

HD = 128
WINDOW = 2048
NEG = -1e30
MESH = pl.DeviceIdType.MESH
VM = pl.BlockSpec(memory_space=pltpu.VMEM)
ANY = pl.BlockSpec(memory_space=pl.ANY)
BF = jnp.bfloat16
F32 = jnp.float32
NY, NZ = 4, 8
DZ = (1, -1, 2, -2, 3, -3, 4)
DY = (1, -1, 2)
FAR = (4, -3, 3, -2, 2, -1, 1)
READY = {4: (0, 1, 2, 3, 4), 5: (5,), 6: (6,)}
LAG = 2
AHEAD = 4
SCALING = 1.0 / math.sqrt(HD)
TO_EXP2 = SCALING * math.log2(math.e)
LEFT = (((0,), (0,)), ((), ()))
RIGHT = (((1,), (1,)), ((), ()))


def coords():
    i = lax.axis_index("ctx")
    return i // 32, (i // 4) % 8, (i // 2) % 2, i % 2, lax.axis_index("head")


def dev(y, z, x, c, h):
    return (((y % NY) * NZ + z % NZ) * 4 + x * 2 + c, h)


def plane_dev(p, x, c, h):
    return ((p % 32) * 4 + x * 2 + c, h)


def remote(src, dst, send, recv, to):
    return pltpu.make_async_remote_copy(
        src_ref=src, dst_ref=dst, send_sem=send, recv_sem=recv, device_id=to, device_id_type=MESH
    )


def push(src, dst, send, recv, to):
    copy = remote(src, dst, send, recv, to)
    copy.start()
    return copy


def all_sent(ref, sem, to):
    remote(ref, ref, sem, sem, to).wait_send()


def dot(a, b):
    return jnp.dot(a, b, preferred_element_type=F32)


def part(start, size):
    return pl.ds(pl.multiple_of(start, size), size)


def kernel(
    wk, wv, hid, q, do, seg_in, table_in,
    att, gq, ph_out, h_in, own_out, f_in,
    seg, table, cos, sin, top, pw, w, wo, hs, hst, q_own, d_own, qx, dx, win, qa, da, qt, dt, s, dkv, att2, gq2,
    x_in, own, z_in, kvg, kvo, wg, ph,
    relay, buf0, acc0, zin0, plus, minus, acc1, yin1, total,
    p_s, p_r, g_s, g_r, v_s, v_r, o_s, o_r, wo_s, wo_r, wz_s, wz_r, wx_s, wx_r,
    bx_s, bx_r, bz_s, bz_r, k_s, k_r, h_s, h_r, l_r, a_s, a_r, b_s, b_r, m_s, m_r, f_s, f_r, loc, out_sem, in_sem,
):
    y, z, x, c, h = coords()
    p = y * NZ + z
    chip = p * 2 + x
    other = dev(y, z, x, 1 - c, h)
    mate = dev(y, z, 1 - x, c, h)
    diag = dev(y, z, 1 - x, 1 - c, h)
    peer = dev(y, z, x, c, 1 - h)
    ys = [dev(y + d, z, x, c, h) for d in DY]
    zs = [dev(y, z + d, x, c, h) for d in DZ]
    up1, down1 = plane_dev(p + 1, x, c, h), plane_dev(p - 1, x, c, h)
    partners = [other, mate, diag, peer, up1, down1] + ys + zs
    barrier = pltpu.get_barrier_semaphore()
    for partner in partners:
        pl.semaphore_signal(barrier, inc=1, device_id=partner, device_id_type=MESH)
    theirs = part((1 - c) * 512, 512)
    mine = part(c * 512, 512)
    toks = part(c * 128, 128)
    own_weights = []
    for n in range(2):
        for m, ref in enumerate((wk, wv)):
            own_weights.append(
                pltpu.make_async_copy(
                    ref.at[:, pl.ds(n * HD, HD)], pw.at[n, :, pl.ds(m * HD, HD)], in_sem.at[n * 2 + m]
                )
            )
    small = [
        pltpu.make_async_copy(seg_in, seg, in_sem.at[4]),
        pltpu.make_async_copy(table_in, table, in_sem.at[5]),
    ]
    for copy in own_weights + small:
        copy.start()
    staged = [
        pltpu.make_async_copy(q.at[:, mine], q_own, loc.at[0]),
        pltpu.make_async_copy(do.at[:, mine], d_own, loc.at[1]),
        pltpu.make_async_copy(hid, hs.at[toks], loc.at[2]),
    ]
    for copy in staged:
        copy.start()
    for copy in small:
        copy.wait()
    cos_a, sin_a = table[pl.ds(chip, 1), :], table[pl.ds(64 + chip, 1), :]
    cos_b, sin_b = table[128:384, :], table[384:640, :]
    cos[...] = cos_a * cos_b - sin_a * sin_b
    lane = lax.broadcasted_iota(jnp.int32, (256, HD), 1)
    angle_sin = sin_a * cos_b + cos_a * sin_b
    sin[...] = jnp.where(lane < 64, angle_sin, -angle_sin)
    for copy in own_weights:
        copy.wait()
    pl.semaphore_wait(barrier, len(partners))

    def plane(yy, zz):
        return part(((yy % NY) * NZ + zz % NZ) * 128, 128)

    def piece(xx, cc):
        return part(p * 128 + xx * 64 + cc * 32, 32)

    pieces = [
        push(pw.at[1 - c], w.at[piece(x, c)], p_s, p_r.at[0], other),
        push(pw.at[c], w.at[piece(x, c)], p_s, p_r.at[1], mate),
        push(pw.at[1 - c], w.at[piece(x, c)], p_s, p_r.at[2], diag),
    ]
    w[piece(x, c), :] = pw[c]
    trades = [
        push(q.at[:, theirs], qx, o_s.at[0], o_r.at[0], other),
        push(do.at[:, theirs], dx, o_s.at[1], o_r.at[1], other),
        push(hid, hs.at[toks], o_s.at[2], o_r.at[2], other),
    ]
    for copy in pieces:
        copy.wait_recv()

    def plane_sem(yy, zz):
        return g_r.at[(yy % NY) * NZ + zz % NZ]

    def wait_plane(yy, zz):
        ref = w.at[plane(yy, zz)]
        remote(ref, ref, g_s, plane_sem(yy, zz), other).wait_recv()

    @pl.when(c == 0)
    def _():
        def go(yy, zz, to):
            ref = w.at[plane(yy, zz)]
            push(ref, ref, g_s, plane_sem(yy, zz), to)

        for n in range(4):
            go(y, z, zs[n])
        for to in ys:
            go(y, z, to)
        for d in DZ:
            wait_plane(y, z + d)
            if d == 2:
                go(y, z + 2, zs[1])
            if d == -2:
                go(y, z - 2, zs[0])
                go(y, z - 2, zs[2])
            for to in ys:
                go(y, z + d, to)
        for d in (0,) + DZ:
            for e in DY:
                wait_plane(y + e, z + d)
        all_sent(w.at[pl.ds(0, 31 * 128)], g_s, other)

    @pl.when(c == 1)
    def _():
        def half(yy, zz):
            return w.at[part(((yy % NY) * NZ + zz % NZ) * 128 + x * 64, 64)]

        def go(yy, zz, to):
            ref = half(yy, zz)
            push(ref, ref, g_s, plane_sem(yy, zz), to)

        def wait_half(yy, zz):
            ref = half(yy, zz)
            remote(ref, ref, g_s, plane_sem(yy, zz), other).wait_recv()

        def share(yy, zz):
            ref = half(yy, zz)
            push(ref, ref, v_s, v_r, mate)

        for to in ys:
            go(y, z, to)
        up, down = zs[0], zs[1]
        for d in range(4):
            for n, e in enumerate((0,) + DY):
                if d == 0:
                    if e:
                        wait_half(y + e, z)
                    go(y + e, z, up)
                    go(y + e, z, down)
                    if e:
                        share(y + e, z)
                    continue
                wait_half(y + e, z - d)
                if d < 3 or n < 2:
                    go(y + e, z - d, up)
                share(y + e, z - d)
                wait_half(y + e, z + d)
                if d < 3 or n >= 2:
                    go(y + e, z + d, down)
                share(y + e, z + d)
        for e in (0,) + DY:
            wait_half(y + e, z + 4)
            share(y + e, z + 4)
        ref = w.at[pl.ds(0, 31 * 64)]
        remote(ref, ref, v_s, v_r, mate).wait()
        all_sent(ref, g_s, other)

    for copy in trades:
        copy.wait_recv()
    for copy in staged:
        copy.wait()
    weights = push(w, wo, wo_s, wo_r, other)

    def project(n, sums):
        span = part(n * 1024, 1024)
        return sums + dot(hs[:, span], w[span, :])

    raw = lax.fori_loop(0, 4, project, jnp.zeros((256, 256), F32))

    def win_rows(k, xx):
        return part((k * 2 + xx) * 256, 256)

    def win_piece(k, xx, n):
        return win.at[n // 2, part((k * 2 + xx) * 256 + (n % 2) * 128, 128)]

    keys = raw[:, 0:HD]
    win[0, win_rows(4, x), :] = (keys * cos[...] - pltpu.roll(keys, 64, 1) * sin[...]).astype(BF)
    win[1, win_rows(4, x), :] = raw[:, HD : 2 * HD].astype(BF)

    def window_up(k, n):
        return remote(
            win_piece(k, x, n), win_piece(k - 1, x, n),
            wz_s, wz_r.at[(k - 1) * 4 + n], up1,
        )

    def window_across(k, n):
        ref = win_piece(k, x, n)
        return remote(ref, ref, wx_s, wx_r.at[4 - x - k], mate)

    for n in range(4):
        window_up(4, n).start()

    @pl.when(x == 0)
    def _():
        for n in range(4):
            window_across(4, n).start()

    for t in range(2):
        @pl.when(c == t)
        def _():
            for g in range(4):
                cols = pl.ds(g * HD, HD)
                rows = pl.ds((t * 4 + g) * HD, HD)
                qa[rows, :] = q_own[:, cols]
                da[rows, :] = d_own[:, cols]

        @pl.when(c != t)
        def _():
            for g in range(4):
                rows = pl.ds((t * 4 + g) * HD, HD)
                qa[rows, :] = qx[:, g * HD : (g + 1) * HD]
                da[rows, :] = dx[:, g * HD : (g + 1) * HD]

    for n in range(8):
        block = slice(n * HD, (n + 1) * HD)
        qt[:, block] = qa[block, :].T
        dt[:, block] = da[block, :].T
    base = x * 256
    row = lax.broadcasted_iota(jnp.int32, (256, 128), 0)
    col = lax.broadcasted_iota(jnp.int32, (256, 128), 1)
    tilt = col - row

    def key_rows(b):
        return part(base + b * 256, 256)

    def forward(b, carry):
        best, sums, out = carry
        seg_k = []
        for n in range(2):
            index = chip * 2 - 16 + b * 2 + n
            line = seg[pl.ds(jnp.maximum(index, 0), 1), :].astype(F32)
            line = jnp.where(index >= 0, line, -1.0)
            seg_k.append(jnp.broadcast_to(line, (128, 128)).T)
        seg_k = jnp.concatenate(seg_k, axis=0)
        bias = []
        for t in range(2):
            seg_q = seg[pl.ds(chip * 2 + t, 1), :].astype(F32)
            gap = tilt + (WINDOW + t * 128 - b * 256)
            ok = (seg_k == seg_q) & (gap >= 0) & (gap < WINDOW)
            bias += [jnp.where(ok, 0.0, NEG)] * 4
        values = dot(win[0, key_rows(b), :], qt[...]) * TO_EXP2 + jnp.concatenate(bias, axis=1)
        higher = jnp.maximum(best, jnp.max(values, axis=0, keepdims=True))
        e = jnp.exp2(values - higher)
        s[part(b * 256, 256), :] = e
        top[pl.ds(b, 1), :] = higher
        shrink = jnp.exp2(best - higher)
        mixed = lax.dot_general(
            win[1, key_rows(b), :], e.astype(BF), LEFT, preferred_element_type=F32
        )
        return higher, sums * shrink + jnp.sum(e, axis=0, keepdims=True), out * shrink + mixed

    def turn_over(n, _):
        cols = part(n * 512, 512)
        hst[cols, :] = hs[:, cols].T
        return 0

    lax.fori_loop(0, 8, turn_over, 0)

    def wait_mate(d):
        ref = win.at[:, win_rows(4 + x - d, 1 - x)]
        remote(ref, ref, wx_s, wx_r.at[d - 1], mate).wait_recv()

    def inward(d, carry):
        k = 4 - d
        for n in range(4):
            ref = win_piece(k, x, n)
            remote(ref, ref, wz_s, wz_r.at[k * 4 + n], up1).wait_recv()

            @pl.when(d < 4)
            def _():
                window_up(k, n).start()

            @pl.when((k >= 1) | (x == 1))
            def _():
                window_across(k, n).start()

        @pl.when(d > 1)
        def _():
            wait_mate(d - 1)

        carry = forward(jnp.where(d == 1, 8, 11 - 2 * d), carry)
        return forward(2 * k, carry)

    carry = (
        jnp.full((1, 1024), NEG, F32), jnp.zeros((1, 1024), F32), jnp.zeros((HD, 1024), F32)
    )
    carry = lax.fori_loop(1, 5, inward, carry)
    wait_mate(4)
    best, sums, out = forward(1, carry)
    inverse = 1.0 / sums
    low = (out * inverse).astype(BF)
    delta = jnp.sum(low.astype(F32) * dt[...].astype(F32), axis=0, keepdims=True)
    for t in range(2):
        for g in range(4):
            n = t * 4 + g
            att2[t, :, g * HD : (g + 1) * HD] = low[:, n * HD : (n + 1) * HD].T
    trades.append(push(att2.at[1 - c], att.at[:, mine], o_s.at[3], o_r.at[3], other))
    keep_att = pltpu.make_async_copy(att2.at[c], att.at[:, mine], out_sem.at[0])
    keep_att.start()

    def rows_of_piece(n):
        return pl.ds(n * 64, 64)

    def give(b, n):
        j = (7 - b) // 2
        return remote(
            dkv.at[b, rows_of_piece(n)], x_in.at[j, rows_of_piece(n)],
            bx_s, bx_r.at[j * 4 + n], mate,
        )

    def pass_on(k, n):
        return remote(
            own.at[k, rows_of_piece(n)], z_in.at[k + 1, rows_of_piece(n)],
            bz_s, bz_r.at[k * 4 + n], down1,
        )


    def merge(k, j, n, chain):
        rows = rows_of_piece(n)
        value = dkv[2 * k, rows, :].astype(F32)
        if j is not None:
            ref = x_in.at[j, rows]
            remote(ref, ref, bx_s, bx_r.at[j * 4 + n], mate).wait_recv()
            value = value + x_in[j, rows, :].astype(F32)
        if chain:
            ref = z_in.at[k, rows]
            remote(ref, ref, bz_s, bz_r.at[(k - 1) * 4 + n], down1).wait_recv()
            value = value + z_in[k, rows, :].astype(F32)
        own[k, rows, :] = value.astype(BF)

    def back(n, query_sum):
        odd = n % 2
        b = jnp.where(n == 8, 8, n + 1 - 2 * odd)
        rows = part(b * 256, 256)
        k = win[0, key_rows(b), :]
        v = win[1, key_rows(b), :]
        probs = s[rows, :] * (inverse * jnp.exp2(top[pl.ds(b, 1), :] - best))
        dscores = probs * (dot(v, dt[...]) - delta)
        probs = probs.astype(BF)
        dscores = dscores.astype(BF)
        dkv[b, :, 0:HD] = (dot(dscores, qa[...]) * SCALING).astype(BF)
        dkv[b, :, HD : 2 * HD] = dot(probs, da[...]).astype(BF)

        @pl.when((odd == 0) & (n < 8))
        def _():
            for piece in range(4):
                give(b, piece).start()

        @pl.when((n == 1) & (x == 0))
        def _():
            for piece in range(4):
                merge(0, None, piece, False)
                pass_on(0, piece).start()

        @pl.when((n == 6) & (x == 1))
        def _():
            for piece in range(4):
                merge(0, 3, piece, False)
                pass_on(0, piece).start()

        @pl.when((n == 6) & (x == 0))
        def _():
            for piece in range(4):
                merge(1, 3, piece, True)
                pass_on(1, piece).start()

        return query_sum + lax.dot_general(k, dscores, LEFT, preferred_element_type=F32)

    query_sum = lax.fori_loop(0, 9, back, jnp.zeros((HD, 1024), F32))

    @pl.when(x == 1)
    def _():
        for n in range(4):
            merge(1, 2, n, True)
            pass_on(1, n).start()

    for k in (2, 3):
        for n in range(4):
            merge(k, 4 - x - k, n, True)
            pass_on(k, n).start()
    query_low = (query_sum * SCALING).astype(BF)
    for t in range(2):
        for g in range(4):
            n = t * 4 + g
            gq2[t, :, g * HD : (g + 1) * HD] = query_low[:, n * HD : (n + 1) * HD].T
    trades.append(push(gq2.at[1 - c], gq.at[:, mine], o_s.at[4], o_r.at[4], other))
    keep_gq = pltpu.make_async_copy(gq2.at[c], gq.at[:, mine], out_sem.at[1])
    keep_gq.start()

    all_sent(win.at[0, pl.ds(0, 2048)], wz_s, up1)
    all_sent(win.at[0, pl.ds(0, 2048)], wx_s, mate)
    all_sent(w.at[pl.ds(0, 96)], p_s, other)
    for copy in trades[:3] + [weights]:
        copy.wait_send()
    for copy in trades[3:]:
        copy.wait()
    keep_att.wait()
    keep_gq.wait()
    for n in range(4):
        @pl.when(x == 0)
        def _():
            merge(4, 0, n, True)

        @pl.when(x == 1)
        def _():
            merge(4, None, n, True)

    grads = own[4].astype(F32)
    keys = grads[:, 0:HD]
    kvg[:, 0:HD] = (keys * cos[...] + pltpu.roll(keys, 64, 1) * sin[...]).astype(BF)
    kvg[:, HD : 2 * HD] = grads[:, HD : 2 * HD].astype(BF)
    crossing = push(kvg.at[part((1 - c) * 128, 128)], kvo, k_s, k_r, other)

    def outer(n, _):
        rows = part(n * 512, 512)
        wg[rows, :] = dot(hst[rows, :], kvg[...]).astype(BF)
        return 0

    lax.fori_loop(0, 8, outer, 0)

    order = FAR + (0,)

    def leave(i):
        n = i % 2
        push(wg.at[plane(y + 2, z + order[i])], relay.at[i], a_s, l_r.at[i], ys[n])
        push(
            wg.at[plane(y + DY[1 - n], z + order[i])], buf0.at[i, 1 - n],
            a_s, a_r.at[i * 2 + 1 - n], ys[1 - n],
        )

    @pl.when(c == 0)
    def _():
        for i in range(AHEAD):
            leave(i)

    @pl.when(c == 1)
    def _():
        for n, e in enumerate((2, 1, -1, 0)):
            top = 4 if n < 2 else 3
            low = 3 if n < 2 else 4
            push(
                wg.at[plane(y + e, z + top)], plus.at[n, top - 1],
                a_s, a_r.at[n * 4 + top - 1], zs[0],
            )
            push(
                wg.at[plane(y + e, z - low)], minus.at[n, low - 1],
                b_s, b_r.at[n * 4 + low - 1], zs[1],
            )

    crossing.wait_recv()
    weights.wait_recv()

    def hidden(n, _):
        for m in range(2):
            span = part(n * 1024 + m * 512, 512)
            ph[n, :, m * 512 : (m + 1) * 512] = (
                lax.dot_general(kvg[toks, :], w[span, :], RIGHT, preferred_element_type=F32)
                + lax.dot_general(kvo[...], wo[span, :], RIGHT, preferred_element_type=F32)
            ).astype(BF)
        remote(ph.at[n], h_in.at[n], h_s.at[n], h_r.at[n], peer).start()
        pltpu.make_async_copy(ph.at[n], ph_out.at[n], out_sem.at[2 + n]).start()
        return 0

    lax.fori_loop(0, 4, hidden, 0)

    @pl.when(c == 0)
    def _():
        def pass_row(i, d):
            n = i % 2
            remote(relay.at[i], relay.at[i], a_s, l_r.at[i], other).wait_recv()
            relay[i] = (
                relay[i].astype(F32) + wg[plane(y + DY[n], z + d), :].astype(F32)
            ).astype(BF)
            push(relay.at[i], buf0.at[i, n], a_s, a_r.at[i * 2 + n], ys[n])

        def pass_plane(i, d):
            for n in range(2):
                ref = buf0.at[i, n]
                remote(ref, ref, a_s, a_r.at[i * 2 + n], other).wait_recv()
            value = (
                wg[plane(y, z + d), :].astype(F32)
                + buf0[i, 0].astype(F32)
                + buf0[i, 1].astype(F32)
            )
            if d:
                acc0[i] = value.astype(BF)
                for m in READY.get(i, ()):
                    push(acc0.at[m], zin0.at[m], b_s, b_r.at[m], zs[DZ.index(FAR[m])])
            else:
                total[...] = value

        for i in range(8 + LAG):
            if i < 8:
                pass_row(i, order[i])
            if i + AHEAD < 8:
                leave(i + AHEAD)
            if i >= LAG:
                pass_plane(i - LAG, order[i - LAG])
        for i in range(7):
            remote(zin0.at[i], zin0.at[i], b_s, b_r.at[i], other).wait_recv()
            total[...] += zin0[i].astype(F32)

    @pl.when(c == 1)
    def _():
        def step(ref, send, recv, n, m, e, sign, to):
            remote(ref.at[n, m], ref.at[n, m], send, recv.at[n * 4 + m], other).wait_recv()
            if m:
                ref[n, m] = (
                    ref[n, m].astype(F32) + wg[plane(y + e, z + sign * m), :].astype(F32)
                ).astype(BF)
                push(
                    ref.at[n, m], ref.at[n, m - 1],
                    send, recv.at[n * 4 + m - 1], to,
                )

        for m in (3, 2, 1, 0):
            for n, e in enumerate((2, 1, -1, 0)):
                top = 4 if n < 2 else 3
                low = 3 if n < 2 else 4
                if m < top:
                    step(plus, a_s, a_r, n, m, e, 1, zs[0])
                if m < low:
                    step(minus, b_s, b_r, n, m, e, -1, zs[1])
                if m == 0:
                    value = (
                        wg[plane(y + e, z), :].astype(F32)
                        + plus[n, 0].astype(F32)
                        + minus[n, 0].astype(F32)
                    )
                    if e:
                        acc1[n] = value.astype(BF)
                        to = DY.index(e)
                        push(acc1.at[n], yin1.at[n], m_s, m_r.at[n], ys[to])
                    else:
                        total[...] = value
        for n in range(3):
            remote(yin1.at[n], yin1.at[n], m_s, m_r.at[n], other).wait_recv()
            total[...] += yin1[n].astype(F32)

    def rows_of(xx, cc):
        return part(xx * 64 + cc * 32, 32)

    finals = [
        push(total.at[rows_of(x, 1 - c)], f_in.at[0], f_s.at[0], f_r.at[0], other),
        push(total.at[rows_of(1 - x, c)], f_in.at[1], f_s.at[1], f_r.at[1], mate),
        push(total.at[rows_of(1 - x, 1 - c)], f_in.at[2], f_s.at[2], f_r.at[2], diag),
    ]

    keep_own = pltpu.make_async_copy(total.at[rows_of(x, c)], own_out, out_sem.at[6])
    keep_own.start()
    crossing.wait_send()
    all_sent(x_in, bx_s, mate)
    all_sent(x_in, bz_s, down1)

    @pl.when(c == 0)
    def _():
        all_sent(wg.at[pl.ds(0, 24 * 128)], a_s, other)
        all_sent(zin0, b_s, other)

    @pl.when(c == 1)
    def _():
        all_sent(wg.at[pl.ds(0, 14 * 128)], a_s, other)
        all_sent(wg.at[pl.ds(0, 14 * 128)], b_s, other)
        all_sent(yin1, m_s, other)

    for copy in finals:
        copy.wait()
    keep_own.wait()
    for n in range(4):
        remote(ph.at[n], h_in.at[n], h_s.at[n], h_r.at[n], peer).wait()
        pltpu.make_async_copy(ph.at[n], ph_out.at[n], out_sem.at[2 + n]).wait()


def run(wk, wv, hid, q, do, seg, table):
    dma = pltpu.SemaphoreType.DMA
    shape = jax.ShapeDtypeStruct

    def bf(*dims):
        return pltpu.VMEM(dims, BF)

    def f32(*dims):
        return pltpu.VMEM(dims, F32)

    buffers = [
        pltpu.VMEM((128, 128), jnp.int32), f32(640, 128),
        f32(256, 128), f32(256, 128), f32(16, 1024),
        bf(2, 32, 256), bf(4096, 256), bf(4096, 256), bf(256, 4096), bf(4096, 256),
        bf(128, 512), bf(128, 512), bf(128, 512), bf(128, 512), bf(2, 2560, 128),
        bf(1024, 128), bf(1024, 128), bf(128, 1024), bf(128, 1024), f32(2304, 1024),
        bf(9, 256, 256), bf(2, 128, 512), bf(2, 128, 512),
        bf(4, 256, 256), bf(5, 256, 256), bf(5, 256, 256), bf(256, 256), bf(128, 256),
        bf(4096, 256), bf(4, 128, 1024),
        bf(8, 128, 256), bf(8, 2, 128, 256), bf(7, 128, 256), bf(7, 128, 256),
        bf(4, 4, 128, 256), bf(4, 4, 128, 256), bf(3, 128, 256), bf(3, 128, 256),
        f32(128, 256),
    ]
    counts = [
        0, 3, 0, 32, 0, 0, 5, 5, 0, 0, 0, 16, 0, 4, 0, 16,
        0, 16, 0, 0, 4, 4, 8, 0, 16, 0, 16, 0, 3, 3, 3, 3, 7, 6,
    ]
    return pl.pallas_call(
        kernel,
        out_shape=(
            shape((128, 1024), BF),
            shape((128, 1024), BF),
            shape((4, 128, 1024), BF),
            shape((4, 128, 1024), BF),
            shape((32, 256), F32),
            shape((3, 32, 256), F32),
        ),
        in_specs=[ANY] * 7,
        out_specs=(ANY,) * 6,
        scratch_shapes=buffers + [dma((n,)) if n else dma for n in counts],
        compiler_params=pltpu.CompilerParams(
            collective_id=0, has_side_effects=True, vmem_limit_bytes=60 * 2**20
        ),
        name="layer",
    )(wk, wv, hid, q, do, seg, table)


def last_kernel(
    att_in, gq_in, ph_in, h_in, own_in, f_in, att, gq, gh, gk, gv,
    ph, hb, at, qt, own, f, gsum, gkb, gvb, sem_in, sem_out
):
    def load(src, dst, n):
        copy = pltpu.make_async_copy(src, dst, sem_in.at[n])
        copy.start()
        return copy

    def store(src, dst, n):
        copy = pltpu.make_async_copy(src, dst, sem_out.at[n])
        copy.start()
        return copy

    parts = [
        (load(ph_in.at[n], ph.at[n], n), load(h_in.at[n], hb.at[n], 4 + n)) for n in range(4)
    ]
    small = [load(own_in, own, 8), load(f_in, f, 9)]
    whole = [load(att_in, at, 10), load(gq_in, qt, 11)]
    stores = []
    for n in range(4):
        for copy in parts[n]:
            copy.wait()
        gsum[:, n * 1024 : (n + 1) * 1024] = (ph[n].astype(F32) + hb[n].astype(F32)).astype(BF)
        cols = pl.ds(n * 1024, 1024)
        stores.append(store(gsum.at[:, cols], gh.at[:, cols], n))
    for n, (copy, src, dst) in enumerate(((whole[0], at, att), (whole[1], qt, gq))):
        copy.wait()
        stores.append(store(src, dst, 4 + n))
    for copy in small:
        copy.wait()
    c = lax.axis_index("ctx") % 2
    here = own[...] + f[1]
    there = f[0] + f[2]
    for n in range(2):
        @pl.when(c == n)
        def _():
            for first, value in ((n, here), (1 - n, there)):
                gkb[:, first * HD : (first + 1) * HD] = value[:, 0:HD]
                gvb[:, first * HD : (first + 1) * HD] = value[:, HD : 2 * HD]

    stores += [store(gkb, gk, 6), store(gvb, gv, 7)]
    for copy in stores:
        copy.wait()


def last(*parts):
    dma = pltpu.SemaphoreType.DMA
    results = (
        jax.ShapeDtypeStruct((128, 1024), BF),
        jax.ShapeDtypeStruct((128, 1024), BF),
        jax.ShapeDtypeStruct((128, 4096), BF),
        jax.ShapeDtypeStruct((32, 256), F32),
        jax.ShapeDtypeStruct((32, 256), F32),
    )
    return pl.pallas_call(
        last_kernel,
        out_shape=results,
        in_specs=[ANY] * 6,
        out_specs=(ANY,) * 5,
        scratch_shapes=[
            pltpu.VMEM((4, 128, 1024), BF),
            pltpu.VMEM((4, 128, 1024), BF),
            pltpu.VMEM((128, 1024), BF),
            pltpu.VMEM((128, 1024), BF),
            pltpu.VMEM((32, 256), F32),
            pltpu.VMEM((3, 32, 256), F32),
            pltpu.VMEM((128, 4096), BF),
            pltpu.VMEM((32, 256), F32),
            pltpu.VMEM((32, 256), F32),
            dma((12,)),
            dma((8,)),
        ],
        compiler_params=pltpu.CompilerParams(vmem_limit_bytes=60 * 2**20),
        name="last",
    )(*parts)


def tables():
    frequency = 10000.0 ** (-(np.arange(64) * 2.0 / HD))
    first = (np.arange(64) * 256)[:, None] * frequency[None, :]
    within = np.arange(256)[:, None] * frequency[None, :]
    both = np.concatenate([np.cos(first), np.sin(first), np.cos(within), np.sin(within)])
    return jnp.asarray(np.concatenate([both, both], axis=1), F32)


def body(hidden_in, queries, key_weight, value_weight, seg_ids, grad_out):
    seg = seg_ids.reshape(128, 128)
    return last(*run(key_weight, value_weight, hidden_in, queries, grad_out, seg, tables()))


def solution(mesh):
    placed = (
        P("ctx", None),
        P("ctx", "head"),
        P("ctx", "head"),
        P("ctx", "head"),
        P(),
        P("ctx", "head"),
    )
    return jax.shard_map(
        body,
        mesh=mesh,
        in_specs=placed,
        out_specs=(
            P("ctx", "head"),
            P("ctx", "head"),
            P("ctx", None),
            P("ctx", "head"),
            P("ctx", "head"),
        ),
        check_vma=False,
    )
```

```python
import math

import jax
import jax.numpy as jnp
import numpy as np
from jax import lax
from jax.experimental import pallas as pl
from jax.experimental.pallas import tpu as pltpu
from jax.sharding import PartitionSpec as P

HD = 128
WINDOW = 2048
NEG = -1e30
MESH = pl.DeviceIdType.MESH
VM = pl.BlockSpec(memory_space=pltpu.VMEM)
ANY = pl.BlockSpec(memory_space=pl.ANY)
BF = jnp.bfloat16
F32 = jnp.float32
NY, NZ = 4, 8
DZ = (1, -1, 2, -2, 3, -3, 4)
DY = (1, -1, 2)
FAR = (4, -3, 3, -2, 2, -1, 1)
READY = {2: (0, 1, 2), 3: (3,), 4: (4,), 5: (5,), 6: (6,)}
LAG = 2
AHEAD = 4
SCALING = 1.0 / math.sqrt(HD)
TO_EXP2 = SCALING * math.log2(math.e)
LEFT = (((0,), (0,)), ((), ()))
RIGHT = (((1,), (1,)), ((), ()))


def coords():
    i = lax.axis_index("ctx")
    return i // 32, (i // 4) % 8, (i // 2) % 2, i % 2, lax.axis_index("head")


def dev(y, z, x, c, h):
    return (((y % NY) * NZ + z % NZ) * 4 + x * 2 + c, h)


def plane_dev(p, x, c, h):
    return ((p % 32) * 4 + x * 2 + c, h)


def remote(src, dst, send, recv, to):
    return pltpu.make_async_remote_copy(
        src_ref=src, dst_ref=dst, send_sem=send, recv_sem=recv, device_id=to, device_id_type=MESH
    )


def push(src, dst, send, recv, to):
    copy = remote(src, dst, send, recv, to)
    copy.start()
    return copy


def all_sent(ref, sem, to):
    remote(ref, ref, sem, sem, to).wait_send()


def dot(a, b):
    return jnp.dot(a, b, preferred_element_type=F32)


def part(start, size):
    return pl.ds(pl.multiple_of(start, size), size)


def kernel(
    wk, wv, hid, q, do, seg_in, table_in,
    att, gq, gh, h_in, own_out, f_in,
    seg, table, cos, sin, top, pw, w, wo, wp, wpo, hs, hst, q_own, d_own, qx, dx, win, qa, da, qt, dt, s, dkv, att2, gq2,
    x_in, own, z_in, kvg, kvo, kvp, wg, ph,
    relay, buf0, acc0, zin0, plus, minus, acc1, yin1, total,
    p_s, p_r, g_s, g_r, v_s, v_r, q_s, q_r, o_s, o_r, wo_s, wo_r, wz_s, wz_r, wx_s, wx_r,
    bx_s, bx_r, bz_s, bz_r, k_s, k_r, h_s, h_r, l_r, a_s, a_r, b_s, b_r, m_s, m_r, f_s, f_r, loc, out_sem, in_sem,
):
    y, z, x, c, h = coords()
    p = y * NZ + z
    chip = p * 2 + x
    other = dev(y, z, x, 1 - c, h)
    mate = dev(y, z, 1 - x, c, h)
    diag = dev(y, z, 1 - x, 1 - c, h)
    peer = dev(y, z, x, c, 1 - h)
    peer_other = dev(y, z, x, 1 - c, 1 - h)
    ys = [dev(y + d, z, x, c, h) for d in DY]
    zs = [dev(y, z + d, x, c, h) for d in DZ]
    up1, down1 = plane_dev(p + 1, x, c, h), plane_dev(p - 1, x, c, h)
    partners = [other, mate, diag, peer, peer_other, up1, down1] + ys + zs
    barrier = pltpu.get_barrier_semaphore()
    for partner in partners:
        pl.semaphore_signal(barrier, inc=1, device_id=partner, device_id_type=MESH)
    theirs = part((1 - c) * 512, 512)
    mine = part(c * 512, 512)
    toks = part(c * 128, 128)
    own_weights = []
    for n in range(2):
        for m, ref in enumerate((wk, wv)):
            own_weights.append(
                pltpu.make_async_copy(
                    ref.at[:, pl.ds(n * HD, HD)], pw.at[n, :, pl.ds(m * HD, HD)], in_sem.at[n * 2 + m]
                )
            )
    small = [
        pltpu.make_async_copy(seg_in, seg, in_sem.at[4]),
        pltpu.make_async_copy(table_in, table, in_sem.at[5]),
    ]
    for copy in own_weights + small:
        copy.start()
    staged = [
        pltpu.make_async_copy(q.at[:, mine], q_own, loc.at[0]),
        pltpu.make_async_copy(do.at[:, mine], d_own, loc.at[1]),
        pltpu.make_async_copy(hid, hs.at[toks], loc.at[2]),
    ]
    for copy in staged:
        copy.start()
    for copy in small:
        copy.wait()
    cos_a, sin_a = table[pl.ds(chip, 1), :], table[pl.ds(64 + chip, 1), :]
    cos_b, sin_b = table[128:384, :], table[384:640, :]
    cos[...] = cos_a * cos_b - sin_a * sin_b
    lane = lax.broadcasted_iota(jnp.int32, (256, HD), 1)
    angle_sin = sin_a * cos_b + cos_a * sin_b
    sin[...] = jnp.where(lane < 64, angle_sin, -angle_sin)
    for copy in own_weights:
        copy.wait()
    pl.semaphore_wait(barrier, len(partners))

    def plane(yy, zz):
        return part(((yy % NY) * NZ + zz % NZ) * 128, 128)

    def piece(xx, cc):
        return part(p * 128 + xx * 64 + cc * 32, 32)

    pieces = [
        push(pw.at[1 - c], w.at[piece(x, c)], p_s, p_r.at[0], other),
        push(pw.at[c], w.at[piece(x, c)], p_s, p_r.at[1], mate),
        push(pw.at[1 - c], w.at[piece(x, c)], p_s, p_r.at[2], diag),
    ]
    w[piece(x, c), :] = pw[c]
    trades = [
        push(q.at[:, theirs], qx, o_s.at[0], o_r.at[0], other),
        push(do.at[:, theirs], dx, o_s.at[1], o_r.at[1], other),
        push(hid, hs.at[toks], o_s.at[2], o_r.at[2], other),
    ]
    for copy in pieces:
        copy.wait_recv()

    def plane_sem(yy, zz):
        return g_r.at[(yy % NY) * NZ + zz % NZ]

    def wait_plane(yy, zz):
        ref = w.at[plane(yy, zz)]
        remote(ref, ref, g_s, plane_sem(yy, zz), other).wait_recv()

    @pl.when(c == 0)
    def _():
        def go(yy, zz, to):
            ref = w.at[plane(yy, zz)]
            push(ref, ref, g_s, plane_sem(yy, zz), to)

        for n in range(4):
            go(y, z, zs[n])
        for to in ys:
            go(y, z, to)
        for d in DZ:
            wait_plane(y, z + d)
            if d == 2:
                go(y, z + 2, zs[1])
            if d == -2:
                go(y, z - 2, zs[0])
                go(y, z - 2, zs[2])
            for to in ys:
                go(y, z + d, to)
        for d in (0,) + DZ:
            for e in DY:
                wait_plane(y + e, z + d)
        all_sent(w.at[pl.ds(0, 31 * 128)], g_s, other)

    @pl.when(c == 1)
    def _():
        def half(yy, zz):
            return w.at[part(((yy % NY) * NZ + zz % NZ) * 128 + x * 64, 64)]

        def go(yy, zz, to):
            ref = half(yy, zz)
            push(ref, ref, g_s, plane_sem(yy, zz), to)

        def wait_half(yy, zz):
            ref = half(yy, zz)
            remote(ref, ref, g_s, plane_sem(yy, zz), other).wait_recv()

        def share(yy, zz):
            ref = half(yy, zz)
            push(ref, ref, v_s, v_r, mate)

        for to in ys:
            go(y, z, to)
        up, down = zs[0], zs[1]
        for d in range(4):
            for n, e in enumerate((0,) + DY):
                if d == 0:
                    if e:
                        wait_half(y + e, z)
                    go(y + e, z, up)
                    go(y + e, z, down)
                    if e:
                        share(y + e, z)
                    continue
                wait_half(y + e, z - d)
                if d < 3 or n < 2:
                    go(y + e, z - d, up)
                share(y + e, z - d)
                wait_half(y + e, z + d)
                if d < 3 or n >= 2:
                    go(y + e, z + d, down)
                share(y + e, z + d)
        for e in (0,) + DY:
            wait_half(y + e, z + 4)
            share(y + e, z + 4)
        ref = w.at[pl.ds(0, 31 * 64)]
        remote(ref, ref, v_s, v_r, mate).wait()
        all_sent(ref, g_s, other)

    for copy in trades:
        copy.wait_recv()
    for copy in staged:
        copy.wait()
    weights = push(w, wo, wo_s.at[0], wo_r.at[0], other)

    def lend(n):
        return remote(
            w.at[part((1 - h) * 1024 + n * 512, 512)], wp.at[pl.ds(n * 512, 512)],
            q_s.at[n], q_r.at[n], peer,
        )

    lend(0).start()

    def project(n, sums):
        span = part(n * 1024, 1024)
        return sums + dot(hs[:, span], w[span, :])

    raw = lax.fori_loop(0, 4, project, jnp.zeros((256, 256), F32))

    def win_rows(k, xx):
        return part((k * 2 + xx) * 256, 256)

    def win_piece(k, xx, n):
        return win.at[n // 2, part((k * 2 + xx) * 256 + (n % 2) * 128, 128)]

    keys = raw[:, 0:HD]
    win[0, win_rows(4, x), :] = (keys * cos[...] - pltpu.roll(keys, 64, 1) * sin[...]).astype(BF)
    win[1, win_rows(4, x), :] = raw[:, HD : 2 * HD].astype(BF)

    def window_up(k, n):
        return remote(
            win_piece(k, x, n), win_piece(k - 1, x, n),
            wz_s, wz_r.at[(k - 1) * 4 + n], up1,
        )

    def window_across(k, n):
        ref = win_piece(k, x, n)
        return remote(ref, ref, wx_s, wx_r.at[4 - x - k], mate)

    for n in range(4):
        window_up(4, n).start()

    @pl.when(x == 0)
    def _():
        for n in range(4):
            window_across(4, n).start()

    for t in range(2):
        @pl.when(c == t)
        def _():
            for g in range(4):
                cols = pl.ds(g * HD, HD)
                rows = pl.ds((t * 4 + g) * HD, HD)
                qa[rows, :] = q_own[:, cols]
                da[rows, :] = d_own[:, cols]

        @pl.when(c != t)
        def _():
            for g in range(4):
                rows = pl.ds((t * 4 + g) * HD, HD)
                qa[rows, :] = qx[:, g * HD : (g + 1) * HD]
                da[rows, :] = dx[:, g * HD : (g + 1) * HD]

    for n in range(8):
        block = slice(n * HD, (n + 1) * HD)
        qt[:, block] = qa[block, :].T
        dt[:, block] = da[block, :].T
    base = x * 256
    row = lax.broadcasted_iota(jnp.int32, (256, 128), 0)
    col = lax.broadcasted_iota(jnp.int32, (256, 128), 1)
    tilt = col - row

    def key_rows(b):
        return part(base + b * 256, 256)

    def forward(b, carry):
        best, sums, out = carry
        seg_k = []
        for n in range(2):
            index = chip * 2 - 16 + b * 2 + n
            line = seg[pl.ds(jnp.maximum(index, 0), 1), :].astype(F32)
            line = jnp.where(index >= 0, line, -1.0)
            seg_k.append(jnp.broadcast_to(line, (128, 128)).T)
        seg_k = jnp.concatenate(seg_k, axis=0)
        bias = []
        for t in range(2):
            seg_q = seg[pl.ds(chip * 2 + t, 1), :].astype(F32)
            gap = tilt + (WINDOW + t * 128 - b * 256)
            ok = (seg_k == seg_q) & (gap >= 0) & (gap < WINDOW)
            bias += [jnp.where(ok, 0.0, NEG)] * 4
        values = dot(win[0, key_rows(b), :], qt[...]) * TO_EXP2 + jnp.concatenate(bias, axis=1)
        higher = jnp.maximum(best, jnp.max(values, axis=0, keepdims=True))
        e = jnp.exp2(values - higher)
        s[part(b * 256, 256), :] = e
        top[pl.ds(b, 1), :] = higher
        shrink = jnp.exp2(best - higher)
        mixed = lax.dot_general(
            win[1, key_rows(b), :], e.astype(BF), LEFT, preferred_element_type=F32
        )
        return higher, sums * shrink + jnp.sum(e, axis=0, keepdims=True), out * shrink + mixed

    def turn_over(n, _):
        cols = part(n * 512, 512)
        hst[cols, :] = hs[:, cols].T
        return 0

    lax.fori_loop(0, 8, turn_over, 0)

    def wait_mate(d):
        ref = win.at[:, win_rows(4 + x - d, 1 - x)]
        remote(ref, ref, wx_s, wx_r.at[d - 1], mate).wait_recv()

    def inward(d, carry):
        k = 4 - d
        for n in range(4):
            ref = win_piece(k, x, n)
            remote(ref, ref, wz_s, wz_r.at[k * 4 + n], up1).wait_recv()

            @pl.when(d < 4)
            def _():
                window_up(k, n).start()

            @pl.when((k >= 1) | (x == 1))
            def _():
                window_across(k, n).start()

        @pl.when(d > 1)
        def _():
            wait_mate(d - 1)

        carry = forward(jnp.where(d == 1, 8, 11 - 2 * d), carry)
        return forward(2 * k, carry)

    carry = (
        jnp.full((1, 1024), NEG, F32), jnp.zeros((1, 1024), F32), jnp.zeros((HD, 1024), F32)
    )
    carry = lax.fori_loop(1, 5, inward, carry)
    wait_mate(4)
    best, sums, out = forward(1, carry)
    inverse = 1.0 / sums
    low = (out * inverse).astype(BF)
    delta = jnp.sum(low.astype(F32) * dt[...].astype(F32), axis=0, keepdims=True)
    for t in range(2):
        for g in range(4):
            n = t * 4 + g
            att2[t, :, g * HD : (g + 1) * HD] = low[:, n * HD : (n + 1) * HD].T
    trades.append(push(att2.at[1 - c], att.at[:, mine], o_s.at[3], o_r.at[3], other))
    keep_att = pltpu.make_async_copy(att2.at[c], att.at[:, mine], out_sem.at[0])
    keep_att.start()

    def rows_of_piece(n):
        return pl.ds(n * 64, 64)

    def give(b, n):
        j = (7 - b) // 2
        return remote(
            dkv.at[b, rows_of_piece(n)], x_in.at[j, rows_of_piece(n)],
            bx_s, bx_r.at[j * 4 + n], mate,
        )

    def pass_on(k, n):
        return remote(
            own.at[k, rows_of_piece(n)], z_in.at[k + 1, rows_of_piece(n)],
            bz_s, bz_r.at[k * 4 + n], down1,
        )


    def merge(k, j, n, chain):
        rows = rows_of_piece(n)
        value = dkv[2 * k, rows, :].astype(F32)
        if j is not None:
            ref = x_in.at[j, rows]
            remote(ref, ref, bx_s, bx_r.at[j * 4 + n], mate).wait_recv()
            value = value + x_in[j, rows, :].astype(F32)
        if chain:
            ref = z_in.at[k, rows]
            remote(ref, ref, bz_s, bz_r.at[(k - 1) * 4 + n], down1).wait_recv()
            value = value + z_in[k, rows, :].astype(F32)
        own[k, rows, :] = value.astype(BF)

    def back(n, query_sum):
        odd = n % 2
        b = jnp.where(n == 8, 8, n + 1 - 2 * odd)
        rows = part(b * 256, 256)
        k = win[0, key_rows(b), :]
        v = win[1, key_rows(b), :]
        probs = s[rows, :] * (inverse * jnp.exp2(top[pl.ds(b, 1), :] - best))
        dscores = probs * (dot(v, dt[...]) - delta)
        probs = probs.astype(BF)
        dscores = dscores.astype(BF)
        dkv[b, :, 0:HD] = (dot(dscores, qa[...]) * SCALING).astype(BF)
        dkv[b, :, HD : 2 * HD] = dot(probs, da[...]).astype(BF)

        @pl.when((odd == 0) & (n < 8))
        def _():
            for piece in range(4):
                give(b, piece).start()

        @pl.when(n == 6)
        def _():
            lend(1).start()

        @pl.when((n == 1) & (x == 0))
        def _():
            for piece in range(4):
                merge(0, None, piece, False)
                pass_on(0, piece).start()

        @pl.when((n == 6) & (x == 1))
        def _():
            for piece in range(4):
                merge(0, 3, piece, False)
                pass_on(0, piece).start()

        @pl.when((n == 6) & (x == 0))
        def _():
            for piece in range(4):
                merge(1, 3, piece, True)
                pass_on(1, piece).start()

        return query_sum + lax.dot_general(k, dscores, LEFT, preferred_element_type=F32)

    query_sum = lax.fori_loop(0, 9, back, jnp.zeros((HD, 1024), F32))

    @pl.when(x == 1)
    def _():
        for n in range(4):
            merge(1, 2, n, True)
            pass_on(1, n).start()

    for k in (2, 3):
        for n in range(4):
            merge(k, 4 - x - k, n, True)
            pass_on(k, n).start()
    query_low = (query_sum * SCALING).astype(BF)
    for t in range(2):
        for g in range(4):
            n = t * 4 + g
            gq2[t, :, g * HD : (g + 1) * HD] = query_low[:, n * HD : (n + 1) * HD].T
    trades.append(push(gq2.at[1 - c], gq.at[:, mine], o_s.at[4], o_r.at[4], other))
    keep_gq = pltpu.make_async_copy(gq2.at[c], gq.at[:, mine], out_sem.at[1])
    keep_gq.start()

    all_sent(win.at[0, pl.ds(0, 2048)], wz_s, up1)
    all_sent(win.at[0, pl.ds(0, 2048)], wx_s, mate)
    all_sent(w.at[pl.ds(0, 96)], p_s, other)
    for copy in trades[:3] + [weights]:
        copy.wait_send()
    for copy in trades[3:]:
        copy.wait()
    keep_att.wait()
    keep_gq.wait()
    for n in range(4):
        @pl.when(x == 0)
        def _():
            merge(4, 0, n, True)

        @pl.when(x == 1)
        def _():
            merge(4, None, n, True)

    grads = own[4].astype(F32)
    keys = grads[:, 0:HD]
    kvg[:, 0:HD] = (keys * cos[...] + pltpu.roll(keys, 64, 1) * sin[...]).astype(BF)
    kvg[:, HD : 2 * HD] = grads[:, HD : 2 * HD].astype(BF)
    away = kvg.at[part((1 - c) * 128, 128)]
    crossing = push(away, kvo, k_s.at[0], k_r.at[0], other)
    across = [
        push(kvg.at[toks], kvp.at[0], k_s.at[1], k_r.at[1], peer),
        push(away, kvp.at[1], k_s.at[2], k_r.at[2], peer_other),
    ]

    def outer(n, _):
        rows = part(n * 512, 512)
        wg[rows, :] = dot(hst[rows, :], kvg[...]).astype(BF)
        return 0

    lax.fori_loop(0, 8, outer, 0)

    order = FAR + (0,)

    def leave(i):
        n = i % 2
        push(wg.at[plane(y + 2, z + order[i])], relay.at[i], a_s, l_r.at[i], ys[n])
        push(
            wg.at[plane(y + DY[1 - n], z + order[i])], buf0.at[i, 1 - n],
            a_s, a_r.at[i * 2 + 1 - n], ys[1 - n],
        )

    @pl.when(c == 0)
    def _():
        for i in range(AHEAD):
            leave(i)

    @pl.when(c == 1)
    def _():
        for n, e in enumerate((2, 1, -1, 0)):
            top = 4 if n < 2 else 3
            low = 3 if n < 2 else 4
            push(
                wg.at[plane(y + e, z + top)], plus.at[n, top - 1],
                a_s, a_r.at[n * 4 + top - 1], zs[0],
            )
            push(
                wg.at[plane(y + e, z - low)], minus.at[n, low - 1],
                b_s, b_r.at[n * 4 + low - 1], zs[1],
            )

    crossing.wait_recv()
    weights.wait_recv()

    def hidden(n, _):
        for m in range(2):
            span = part(2048 + n * 1024 + m * 512, 512)
            ph[n, :, m * 512 : (m + 1) * 512] = (
                lax.dot_general(kvg[toks, :], w[span, :], RIGHT, preferred_element_type=F32)
                + lax.dot_general(kvo[...], wo[span, :], RIGHT, preferred_element_type=F32)
            ).astype(BF)
        remote(ph.at[n], h_in.at[n], h_s.at[n], h_r.at[n], peer).start()
        pltpu.make_async_copy(ph.at[n], gh.at[2 + n], out_sem.at[2 + n]).start()
        return 0

    lax.fori_loop(0, 2, hidden, 0)
    for n in range(2):
        lend(n).wait()
    borrowed = push(wp, wpo, wo_s.at[1], wo_r.at[1], other)

    def quarter_to(n):
        return remote(ph.at[2], gh.at[n], h_s.at[2], h_r.at[2], peer)

    keep_quarter = pltpu.make_async_copy(ph.at[2], gh.at[h], out_sem.at[4])

    def quarter():
        borrowed.wait_recv()
        for copy in across:
            copy.wait_recv()
        for m in range(2):
            span = part(h * 1024 + m * 512, 512)
            near = pl.ds(m * 512, 512)
            value = 0.0
            for left, right in (
                (kvg[toks, :], w[span, :]),
                (kvo[...], wo[span, :]),
                (kvp[0], wp[near, :]),
                (kvp[1], wpo[near, :]),
            ):
                value = value + lax.dot_general(left, right, RIGHT, preferred_element_type=F32)
            ph[2, :, m * 512 : (m + 1) * 512] = value.astype(BF)
        quarter_to(h).start()
        keep_quarter.start()


    @pl.when(c == 0)
    def _():
        def pass_row(i, d):
            n = i % 2
            remote(relay.at[i], relay.at[i], a_s, l_r.at[i], other).wait_recv()
            relay[i] = (
                relay[i].astype(F32) + wg[plane(y + DY[n], z + d), :].astype(F32)
            ).astype(BF)
            push(relay.at[i], buf0.at[i, n], a_s, a_r.at[i * 2 + n], ys[n])

        def pass_plane(i, d):
            for n in range(2):
                ref = buf0.at[i, n]
                remote(ref, ref, a_s, a_r.at[i * 2 + n], other).wait_recv()
            value = (
                wg[plane(y, z + d), :].astype(F32)
                + buf0[i, 0].astype(F32)
                + buf0[i, 1].astype(F32)
            )
            if d:
                acc0[i] = value.astype(BF)
                for m in READY.get(i, ()):
                    push(acc0.at[m], zin0.at[m], b_s, b_r.at[m], zs[DZ.index(FAR[m])])
            else:
                total[...] = value

        for i in range(8 + LAG):
            if i < 8:
                pass_row(i, order[i])
            if i + AHEAD < 8:
                leave(i + AHEAD)
            if i >= LAG:
                pass_plane(i - LAG, order[i - LAG])
            if i == 4:
                quarter()
        for i in range(7):
            remote(zin0.at[i], zin0.at[i], b_s, b_r.at[i], other).wait_recv()
            total[...] += zin0[i].astype(F32)

    @pl.when(c == 1)
    def _():
        def step(ref, send, recv, n, m, e, sign, to):
            remote(ref.at[n, m], ref.at[n, m], send, recv.at[n * 4 + m], other).wait_recv()
            if m:
                ref[n, m] = (
                    ref[n, m].astype(F32) + wg[plane(y + e, z + sign * m), :].astype(F32)
                ).astype(BF)
                push(
                    ref.at[n, m], ref.at[n, m - 1],
                    send, recv.at[n * 4 + m - 1], to,
                )

        for m in (3, 2, 1, 0):
            if m == 1:
                quarter()
            for n, e in enumerate((2, 1, -1, 0)):
                top = 4 if n < 2 else 3
                low = 3 if n < 2 else 4
                if m < top:
                    step(plus, a_s, a_r, n, m, e, 1, zs[0])
                if m < low:
                    step(minus, b_s, b_r, n, m, e, -1, zs[1])
                if m == 0:
                    value = (
                        wg[plane(y + e, z), :].astype(F32)
                        + plus[n, 0].astype(F32)
                        + minus[n, 0].astype(F32)
                    )
                    if e:
                        acc1[n] = value.astype(BF)
                        to = DY.index(e)
                        push(acc1.at[n], yin1.at[n], m_s, m_r.at[n], ys[to])
                    else:
                        total[...] = value
        for n in range(3):
            remote(yin1.at[n], yin1.at[n], m_s, m_r.at[n], other).wait_recv()
            total[...] += yin1[n].astype(F32)

    def rows_of(xx, cc):
        return part(xx * 64 + cc * 32, 32)

    finals = [
        push(total.at[rows_of(x, 1 - c)], f_in.at[0], f_s.at[0], f_r.at[0], other),
        push(total.at[rows_of(1 - x, c)], f_in.at[1], f_s.at[1], f_r.at[1], mate),
        push(total.at[rows_of(1 - x, 1 - c)], f_in.at[2], f_s.at[2], f_r.at[2], diag),
    ]

    keep_own = pltpu.make_async_copy(total.at[rows_of(x, c)], own_out, out_sem.at[6])
    keep_own.start()
    crossing.wait_send()
    borrowed.wait_send()
    for copy in across:
        copy.wait_send()
    all_sent(x_in, bx_s, mate)
    all_sent(x_in, bz_s, down1)

    @pl.when(c == 0)
    def _():
        all_sent(wg.at[pl.ds(0, 24 * 128)], a_s, other)
        all_sent(zin0, b_s, other)

    @pl.when(c == 1)
    def _():
        all_sent(wg.at[pl.ds(0, 14 * 128)], a_s, other)
        all_sent(wg.at[pl.ds(0, 14 * 128)], b_s, other)
        all_sent(yin1, m_s, other)

    for copy in finals:
        copy.wait()
    keep_own.wait()
    for n in range(2):
        remote(ph.at[n], h_in.at[n], h_s.at[n], h_r.at[n], peer).wait()
        pltpu.make_async_copy(ph.at[n], gh.at[2 + n], out_sem.at[2 + n]).wait()
    quarter_to(h).wait_send()
    quarter_to(1 - h).wait_recv()
    keep_quarter.wait()


def run(wk, wv, hid, q, do, seg, table):
    dma = pltpu.SemaphoreType.DMA
    shape = jax.ShapeDtypeStruct

    def bf(*dims):
        return pltpu.VMEM(dims, BF)

    def f32(*dims):
        return pltpu.VMEM(dims, F32)

    buffers = [
        pltpu.VMEM((128, 128), jnp.int32), f32(640, 128),
        f32(256, 128), f32(256, 128), f32(16, 1024),
        bf(2, 32, 256), bf(4096, 256), bf(4096, 256), bf(1024, 256), bf(1024, 256), bf(256, 4096), bf(4096, 256),
        bf(128, 512), bf(128, 512), bf(128, 512), bf(128, 512), bf(2, 2560, 128),
        bf(1024, 128), bf(1024, 128), bf(128, 1024), bf(128, 1024), f32(2304, 1024),
        bf(9, 256, 256), bf(2, 128, 512), bf(2, 128, 512),
        bf(4, 256, 256), bf(5, 256, 256), bf(5, 256, 256), bf(256, 256), bf(128, 256), bf(2, 128, 256),
        bf(4096, 256), bf(3, 128, 1024),
        bf(8, 128, 256), bf(8, 2, 128, 256), bf(7, 128, 256), bf(7, 128, 256),
        bf(4, 4, 128, 256), bf(4, 4, 128, 256), bf(3, 128, 256), bf(3, 128, 256),
        f32(128, 256),
    ]
    counts = [
        0, 3, 0, 32, 0, 0, 2, 2, 5, 5, 2, 2, 0, 16, 0, 4, 0, 16,
        0, 16, 3, 3, 3, 3, 8, 0, 16, 0, 16, 0, 3, 3, 3, 3, 7, 6,
    ]
    return pl.pallas_call(
        kernel,
        out_shape=(
            shape((128, 1024), BF),
            shape((128, 1024), BF),
            shape((4, 128, 1024), BF),
            shape((2, 128, 1024), BF),
            shape((32, 256), F32),
            shape((3, 32, 256), F32),
        ),
        in_specs=[ANY] * 7,
        out_specs=(ANY,) * 6,
        scratch_shapes=buffers + [dma((n,)) if n else dma for n in counts],
        compiler_params=pltpu.CompilerParams(
            collective_id=0, has_side_effects=True, vmem_limit_bytes=60 * 2**20
        ),
        name="layer",
    )(wk, wv, hid, q, do, seg, table)


def last_kernel(
    att_in, gq_in, ph_in, h_in, own_in, f_in, att, gq, gh, gk, gv,
    ph, hb, at, qt, own, f, gkb, gvb, sem_in, sem_out
):
    def load(src, dst, n):
        copy = pltpu.make_async_copy(src, dst, sem_in.at[n])
        copy.start()
        return copy

    def store(src, dst, n):
        copy = pltpu.make_async_copy(src, dst, sem_out.at[n])
        copy.start()
        return copy

    parts = [
        (load(ph_in.at[n], ph.at[n], n),) + ((load(h_in.at[n - 2], hb.at[n - 2], 4 + n),) if n > 1 else ())
        for n in range(4)
    ]
    small = [load(own_in, own, 8), load(f_in, f, 9)]
    whole = [load(att_in, at, 10), load(gq_in, qt, 11)]
    stores = []
    for n in range(4):
        for copy in parts[n]:
            copy.wait()
        if n > 1:
            ph[n] = (ph[n].astype(F32) + hb[n - 2].astype(F32)).astype(BF)
        stores.append(store(ph.at[n], gh.at[:, pl.ds(n * 1024, 1024)], n))
    for n, (copy, src, dst) in enumerate(((whole[0], at, att), (whole[1], qt, gq))):
        copy.wait()
        stores.append(store(src, dst, 4 + n))
    for copy in small:
        copy.wait()
    c = lax.axis_index("ctx") % 2
    here = own[...] + f[1]
    there = f[0] + f[2]
    for n in range(2):
        @pl.when(c == n)
        def _():
            for first, value in ((n, here), (1 - n, there)):
                gkb[:, first * HD : (first + 1) * HD] = value[:, 0:HD]
                gvb[:, first * HD : (first + 1) * HD] = value[:, HD : 2 * HD]

    stores += [store(gkb, gk, 6), store(gvb, gv, 7)]
    for copy in stores:
        copy.wait()


def last(*parts):
    dma = pltpu.SemaphoreType.DMA
    results = (
        jax.ShapeDtypeStruct((128, 1024), BF),
        jax.ShapeDtypeStruct((128, 1024), BF),
        jax.ShapeDtypeStruct((128, 4096), BF),
        jax.ShapeDtypeStruct((32, 256), F32),
        jax.ShapeDtypeStruct((32, 256), F32),
    )
    return pl.pallas_call(
        last_kernel,
        out_shape=results,
        in_specs=[ANY] * 6,
        out_specs=(ANY,) * 5,
        scratch_shapes=[
            pltpu.VMEM((4, 128, 1024), BF),
            pltpu.VMEM((2, 128, 1024), BF),
            pltpu.VMEM((128, 1024), BF),
            pltpu.VMEM((128, 1024), BF),
            pltpu.VMEM((32, 256), F32),
            pltpu.VMEM((3, 32, 256), F32),
            pltpu.VMEM((32, 256), F32),
            pltpu.VMEM((32, 256), F32),
            dma((12,)),
            dma((8,)),
        ],
        compiler_params=pltpu.CompilerParams(vmem_limit_bytes=60 * 2**20),
        name="last",
    )(*parts)


def tables():
    frequency = 10000.0 ** (-(np.arange(64) * 2.0 / HD))
    first = (np.arange(64) * 256)[:, None] * frequency[None, :]
    within = np.arange(256)[:, None] * frequency[None, :]
    both = np.concatenate([np.cos(first), np.sin(first), np.cos(within), np.sin(within)])
    return jnp.asarray(np.concatenate([both, both], axis=1), F32)


def body(hidden_in, queries, key_weight, value_weight, seg_ids, grad_out):
    seg = seg_ids.reshape(128, 128)
    return last(*run(key_weight, value_weight, hidden_in, queries, grad_out, seg, tables()))


def solution(mesh):
    placed = (
        P("ctx", None),
        P("ctx", "head"),
        P("ctx", "head"),
        P("ctx", "head"),
        P(),
        P("ctx", "head"),
    )
    return jax.shard_map(
        body,
        mesh=mesh,
        in_specs=placed,
        out_specs=(
            P("ctx", "head"),
            P("ctx", "head"),
            P("ctx", None),
            P("ctx", "head"),
            P("ctx", "head"),
        ),
        check_vma=False,
    )
```

```python
import math

import jax
import jax.numpy as jnp
import numpy as np
from jax import lax
from jax.experimental import pallas as pl
from jax.experimental.pallas import tpu as pltpu
from jax.sharding import PartitionSpec as P

HD = 128
WINDOW = 2048
NEG = -1e30
MESH = pl.DeviceIdType.MESH
VM = pl.BlockSpec(memory_space=pltpu.VMEM)
ANY = pl.BlockSpec(memory_space=pl.ANY)
BF = jnp.bfloat16
F32 = jnp.float32
NY, NZ = 4, 8
DZ = (1, -1, 2, -2, 3, -3, 4)
DY = (1, -1, 2)
FAR = (4, -3, 3, -2, 2, -1, 1)
READY = {2: (0, 1, 2), 3: (3,), 4: (4,), 5: (5,), 6: (6,)}
LAG = 2
AHEAD = 4
SCALING = 1.0 / math.sqrt(HD)
TO_EXP2 = SCALING * math.log2(math.e)
LEFT = (((0,), (0,)), ((), ()))
RIGHT = (((1,), (1,)), ((), ()))


def coords():
    i = lax.axis_index("ctx")
    return i // 32, (i // 4) % 8, (i // 2) % 2, i % 2, lax.axis_index("head")


def dev(y, z, x, c, h):
    return (((y % NY) * NZ + z % NZ) * 4 + x * 2 + c, h)


def plane_dev(p, x, c, h):
    return ((p % 32) * 4 + x * 2 + c, h)


def remote(src, dst, send, recv, to):
    return pltpu.make_async_remote_copy(
        src_ref=src, dst_ref=dst, send_sem=send, recv_sem=recv, device_id=to, device_id_type=MESH
    )


def push(src, dst, send, recv, to):
    copy = remote(src, dst, send, recv, to)
    copy.start()
    return copy


def all_sent(ref, sem, to):
    remote(ref, ref, sem, sem, to).wait_send()


def dot(a, b):
    return jnp.dot(a, b, preferred_element_type=F32)


def part(start, size):
    return pl.ds(pl.multiple_of(start, size), size)


def kernel(
    wk, wv, hid, q, do, seg_in, table_in,
    att, gq, gh, h_in, own_out, f_in,
    seg, table, cos, sin, top, pw, w, wo, wp, wpo, hs, hst, q_own, d_own, qx, dx, win, qa, da, qt, dt, s, dkv, att2, gq2,
    x_in, own, z_in, kvg, kvo, kvp, wg, ph,
    relay, buf0, acc0, zin0, plus, minus, acc1, yin1, total,
    p_s, p_r, g_s, g_r, v_s, v_r, q_s, q_r, o_s, o_r, wo_s, wo_r, wz_s, wz_r, wx_s, wx_r,
    bx_s, bx_r, bz_s, bz_r, k_s, k_r, h_s, h_r, l_r, a_s, a_r, b_s, b_r, m_s, m_r, f_s, f_r, loc, out_sem, in_sem,
):
    y, z, x, c, h = coords()
    p = y * NZ + z
    chip = p * 2 + x
    other = dev(y, z, x, 1 - c, h)
    mate = dev(y, z, 1 - x, c, h)
    diag = dev(y, z, 1 - x, 1 - c, h)
    peer = dev(y, z, x, c, 1 - h)
    peer_other = dev(y, z, x, 1 - c, 1 - h)
    ys = [dev(y + d, z, x, c, h) for d in DY]
    zs = [dev(y, z + d, x, c, h) for d in DZ]
    up1, down1 = plane_dev(p + 1, x, c, h), plane_dev(p - 1, x, c, h)
    partners = [other, mate, diag, peer, peer_other, up1, down1] + ys + zs
    barrier = pltpu.get_barrier_semaphore()
    for partner in partners:
        pl.semaphore_signal(barrier, inc=1, device_id=partner, device_id_type=MESH)
    theirs = part((1 - c) * 512, 512)
    mine = part(c * 512, 512)
    toks = part(c * 128, 128)
    own_weights = []
    for n in range(2):
        for m, ref in enumerate((wk, wv)):
            own_weights.append(
                pltpu.make_async_copy(
                    ref.at[:, pl.ds(n * HD, HD)], pw.at[n, :, pl.ds(m * HD, HD)], in_sem.at[n * 2 + m]
                )
            )
    small = [
        pltpu.make_async_copy(seg_in, seg, in_sem.at[4]),
        pltpu.make_async_copy(table_in, table, in_sem.at[5]),
    ]
    for copy in own_weights + small:
        copy.start()
    staged = [
        pltpu.make_async_copy(q.at[:, mine], q_own, loc.at[0]),
        pltpu.make_async_copy(do.at[:, mine], d_own, loc.at[1]),
        pltpu.make_async_copy(hid, hs.at[toks], loc.at[2]),
    ]
    for copy in staged:
        copy.start()
    for copy in small:
        copy.wait()
    cos_a, sin_a = table[pl.ds(chip, 1), :], table[pl.ds(64 + chip, 1), :]
    cos_b, sin_b = table[128:384, :], table[384:640, :]
    cos[...] = cos_a * cos_b - sin_a * sin_b
    lane = lax.broadcasted_iota(jnp.int32, (256, HD), 1)
    angle_sin = sin_a * cos_b + cos_a * sin_b
    sin[...] = jnp.where(lane < 64, angle_sin, -angle_sin)
    for copy in own_weights:
        copy.wait()
    pl.semaphore_wait(barrier, len(partners))

    def plane(yy, zz):
        return part(((yy % NY) * NZ + zz % NZ) * 128, 128)

    def piece(xx, cc):
        return part(p * 128 + xx * 64 + cc * 32, 32)

    pieces = [
        push(pw.at[1 - c], w.at[piece(x, c)], p_s, p_r.at[0], other),
        push(pw.at[c], w.at[piece(x, c)], p_s, p_r.at[1], mate),
        push(pw.at[1 - c], w.at[piece(x, c)], p_s, p_r.at[2], diag),
    ]
    w[piece(x, c), :] = pw[c]
    trades = [
        push(q.at[:, theirs], qx, o_s.at[0], o_r.at[0], other),
        push(do.at[:, theirs], dx, o_s.at[1], o_r.at[1], other),
        push(hid, hs.at[toks], o_s.at[2], o_r.at[2], other),
    ]
    for copy in pieces:
        copy.wait_recv()

    def plane_sem(yy, zz):
        return g_r.at[(yy % NY) * NZ + zz % NZ]

    def wait_plane(yy, zz):
        ref = w.at[plane(yy, zz)]
        remote(ref, ref, g_s, plane_sem(yy, zz), other).wait_recv()

    @pl.when(c == 0)
    def _():
        def go(yy, zz, to):
            ref = w.at[plane(yy, zz)]
            push(ref, ref, g_s, plane_sem(yy, zz), to)

        for n in range(4):
            go(y, z, zs[n])
        for to in ys:
            go(y, z, to)
        for d in DZ:
            wait_plane(y, z + d)
            if d == 2:
                go(y, z + 2, zs[1])
            if d == -2:
                go(y, z - 2, zs[0])
                go(y, z - 2, zs[2])
            for to in ys:
                go(y, z + d, to)
        for d in (0,) + DZ:
            for e in DY:
                wait_plane(y + e, z + d)
        all_sent(w.at[pl.ds(0, 31 * 128)], g_s, other)

    @pl.when(c == 1)
    def _():
        def half(yy, zz):
            return w.at[part(((yy % NY) * NZ + zz % NZ) * 128 + x * 64, 64)]

        def go(yy, zz, to):
            ref = half(yy, zz)
            push(ref, ref, g_s, plane_sem(yy, zz), to)

        def wait_half(yy, zz):
            ref = half(yy, zz)
            remote(ref, ref, g_s, plane_sem(yy, zz), other).wait_recv()

        def share(yy, zz):
            ref = half(yy, zz)
            push(ref, ref, v_s, v_r, mate)

        for to in ys:
            go(y, z, to)
        up, down = zs[0], zs[1]
        for d in range(4):
            for n, e in enumerate((0,) + DY):
                if d == 0:
                    if e:
                        wait_half(y + e, z)
                    go(y + e, z, up)
                    go(y + e, z, down)
                    if e:
                        share(y + e, z)
                    continue
                wait_half(y + e, z - d)
                if d < 3 or n < 2:
                    go(y + e, z - d, up)
                share(y + e, z - d)
                wait_half(y + e, z + d)
                if d < 3 or n >= 2:
                    go(y + e, z + d, down)
                share(y + e, z + d)
        for e in (0,) + DY:
            wait_half(y + e, z + 4)
            share(y + e, z + 4)
        ref = w.at[pl.ds(0, 31 * 64)]
        remote(ref, ref, v_s, v_r, mate).wait()
        all_sent(ref, g_s, other)

    for copy in trades:
        copy.wait_recv()
    for copy in staged:
        copy.wait()
    weights = push(w, wo, wo_s.at[0], wo_r.at[0], other)

    def lend(n):
        return remote(
            w.at[part((1 - h) * 1024 + n * 512, 512)], wp.at[pl.ds(n * 512, 512)],
            q_s.at[n], q_r.at[n], peer,
        )


    def project(n, sums):
        span = part(n * 1024, 1024)
        return sums + dot(hs[:, span], w[span, :])

    raw = lax.fori_loop(0, 4, project, jnp.zeros((256, 256), F32))

    def win_rows(k, xx):
        return part((k * 2 + xx) * 256, 256)

    def win_piece(k, xx, n):
        return win.at[n // 2, part((k * 2 + xx) * 256 + (n % 2) * 128, 128)]

    keys = raw[:, 0:HD]
    win[0, win_rows(4, x), :] = (keys * cos[...] - pltpu.roll(keys, 64, 1) * sin[...]).astype(BF)
    win[1, win_rows(4, x), :] = raw[:, HD : 2 * HD].astype(BF)

    def window_up(k, n):
        return remote(
            win_piece(k, x, n), win_piece(k - 1, x, n),
            wz_s, wz_r.at[(k - 1) * 4 + n], up1,
        )

    def window_across(k, n):
        ref = win_piece(k, x, n)
        return remote(ref, ref, wx_s, wx_r.at[4 - x - k], mate)

    for n in range(4):
        window_up(4, n).start()

    @pl.when(x == 0)
    def _():
        for n in range(4):
            window_across(4, n).start()

    lend(0).start()

    for t in range(2):
        @pl.when(c == t)
        def _():
            for g in range(4):
                cols = pl.ds(g * HD, HD)
                rows = pl.ds((t * 4 + g) * HD, HD)
                qa[rows, :] = q_own[:, cols]
                da[rows, :] = d_own[:, cols]

        @pl.when(c != t)
        def _():
            for g in range(4):
                rows = pl.ds((t * 4 + g) * HD, HD)
                qa[rows, :] = qx[:, g * HD : (g + 1) * HD]
                da[rows, :] = dx[:, g * HD : (g + 1) * HD]

    for n in range(8):
        block = slice(n * HD, (n + 1) * HD)
        qt[:, block] = qa[block, :].T
        dt[:, block] = da[block, :].T
    base = x * 256
    row = lax.broadcasted_iota(jnp.int32, (256, 128), 0)
    col = lax.broadcasted_iota(jnp.int32, (256, 128), 1)
    tilt = col - row

    def key_rows(b):
        return part(base + b * 256, 256)

    def forward(b, carry):
        best, sums, out = carry
        seg_k = []
        for n in range(2):
            index = chip * 2 - 16 + b * 2 + n
            line = seg[pl.ds(jnp.maximum(index, 0), 1), :].astype(F32)
            line = jnp.where(index >= 0, line, -1.0)
            seg_k.append(jnp.broadcast_to(line, (128, 128)).T)
        seg_k = jnp.concatenate(seg_k, axis=0)
        bias = []
        for t in range(2):
            seg_q = seg[pl.ds(chip * 2 + t, 1), :].astype(F32)
            gap = tilt + (WINDOW + t * 128 - b * 256)
            ok = (seg_k == seg_q) & (gap >= 0) & (gap < WINDOW)
            bias += [jnp.where(ok, 0.0, NEG)] * 4
        values = dot(win[0, key_rows(b), :], qt[...]) * TO_EXP2 + jnp.concatenate(bias, axis=1)
        higher = jnp.maximum(best, jnp.max(values, axis=0, keepdims=True))
        e = jnp.exp2(values - higher)
        s[part(b * 256, 256), :] = e
        top[pl.ds(b, 1), :] = higher
        shrink = jnp.exp2(best - higher)
        mixed = lax.dot_general(
            win[1, key_rows(b), :], e.astype(BF), LEFT, preferred_element_type=F32
        )
        return higher, sums * shrink + jnp.sum(e, axis=0, keepdims=True), out * shrink + mixed

    def turn_over(n, _):
        cols = part(n * 512, 512)
        hst[cols, :] = hs[:, cols].T
        return 0

    lax.fori_loop(0, 8, turn_over, 0)

    def wait_mate(d):
        ref = win.at[:, win_rows(4 + x - d, 1 - x)]
        remote(ref, ref, wx_s, wx_r.at[d - 1], mate).wait_recv()

    def inward(d, carry):
        k = 4 - d
        for n in range(4):
            ref = win_piece(k, x, n)
            remote(ref, ref, wz_s, wz_r.at[k * 4 + n], up1).wait_recv()

            @pl.when(d < 4)
            def _():
                window_up(k, n).start()

            @pl.when((k >= 1) | (x == 1))
            def _():
                window_across(k, n).start()

        @pl.when(d > 1)
        def _():
            wait_mate(d - 1)

        carry = forward(jnp.where(d == 1, 8, 11 - 2 * d), carry)
        return forward(2 * k, carry)

    carry = (
        jnp.full((1, 1024), NEG, F32), jnp.zeros((1, 1024), F32), jnp.zeros((HD, 1024), F32)
    )
    carry = lax.fori_loop(1, 5, inward, carry)
    wait_mate(4)
    best, sums, out = forward(1, carry)
    inverse = 1.0 / sums
    low = (out * inverse).astype(BF)
    delta = jnp.sum(low.astype(F32) * dt[...].astype(F32), axis=0, keepdims=True)
    for t in range(2):
        for g in range(4):
            n = t * 4 + g
            att2[t, :, g * HD : (g + 1) * HD] = low[:, n * HD : (n + 1) * HD].T
    trades.append(push(att2.at[1 - c], att.at[:, mine], o_s.at[3], o_r.at[3], other))
    keep_att = pltpu.make_async_copy(att2.at[c], att.at[:, mine], out_sem.at[0])
    keep_att.start()

    def rows_of_piece(n):
        return pl.ds(n * 64, 64)

    def give(b, n):
        j = (7 - b) // 2
        return remote(
            dkv.at[b, rows_of_piece(n)], x_in.at[j, rows_of_piece(n)],
            bx_s, bx_r.at[j * 4 + n], mate,
        )

    def pass_on(k, n):
        return remote(
            own.at[k, rows_of_piece(n)], z_in.at[k + 1, rows_of_piece(n)],
            bz_s, bz_r.at[k * 4 + n], down1,
        )


    def merge(k, j, n, chain):
        rows = rows_of_piece(n)
        value = dkv[2 * k, rows, :].astype(F32)
        if j is not None:
            ref = x_in.at[j, rows]
            remote(ref, ref, bx_s, bx_r.at[j * 4 + n], mate).wait_recv()
            value = value + x_in[j, rows, :].astype(F32)
        if chain:
            ref = z_in.at[k, rows]
            remote(ref, ref, bz_s, bz_r.at[(k - 1) * 4 + n], down1).wait_recv()
            value = value + z_in[k, rows, :].astype(F32)
        own[k, rows, :] = value.astype(BF)

    def back(n, query_sum):
        odd = n % 2
        b = jnp.where(n == 8, 8, n + 1 - 2 * odd)
        rows = part(b * 256, 256)
        k = win[0, key_rows(b), :]
        v = win[1, key_rows(b), :]
        probs = s[rows, :] * (inverse * jnp.exp2(top[pl.ds(b, 1), :] - best))
        dscores = probs * (dot(v, dt[...]) - delta)
        probs = probs.astype(BF)
        dscores = dscores.astype(BF)
        dkv[b, :, 0:HD] = (dot(dscores, qa[...]) * SCALING).astype(BF)
        dkv[b, :, HD : 2 * HD] = dot(probs, da[...]).astype(BF)

        @pl.when((odd == 0) & (n < 8))
        def _():
            for piece in range(4):
                give(b, piece).start()

        @pl.when(n == 6)
        def _():
            lend(1).start()

        @pl.when((n == 1) & (x == 0))
        def _():
            for piece in range(4):
                merge(0, None, piece, False)
                pass_on(0, piece).start()

        @pl.when((n == 6) & (x == 1))
        def _():
            for piece in range(4):
                merge(0, 3, piece, False)
                pass_on(0, piece).start()

        @pl.when((n == 6) & (x == 0))
        def _():
            for piece in range(4):
                merge(1, 3, piece, True)
                pass_on(1, piece).start()

        return query_sum + lax.dot_general(k, dscores, LEFT, preferred_element_type=F32)

    query_sum = lax.fori_loop(0, 9, back, jnp.zeros((HD, 1024), F32))

    @pl.when(x == 1)
    def _():
        for n in range(4):
            merge(1, 2, n, True)
            pass_on(1, n).start()

    for k in (2, 3):
        for n in range(4):
            merge(k, 4 - x - k, n, True)
            pass_on(k, n).start()
    query_low = (query_sum * SCALING).astype(BF)
    for t in range(2):
        for g in range(4):
            n = t * 4 + g
            gq2[t, :, g * HD : (g + 1) * HD] = query_low[:, n * HD : (n + 1) * HD].T
    trades.append(push(gq2.at[1 - c], gq.at[:, mine], o_s.at[4], o_r.at[4], other))
    keep_gq = pltpu.make_async_copy(gq2.at[c], gq.at[:, mine], out_sem.at[1])
    keep_gq.start()

    all_sent(win.at[0, pl.ds(0, 2048)], wz_s, up1)
    all_sent(win.at[0, pl.ds(0, 2048)], wx_s, mate)
    all_sent(w.at[pl.ds(0, 96)], p_s, other)
    for copy in trades[:3] + [weights]:
        copy.wait_send()
    for copy in trades[3:]:
        copy.wait()
    keep_att.wait()
    keep_gq.wait()
    for n in range(4):
        @pl.when(x == 0)
        def _():
            merge(4, 0, n, True)

        @pl.when(x == 1)
        def _():
            merge(4, None, n, True)

    grads = own[4].astype(F32)
    keys = grads[:, 0:HD]
    kvg[:, 0:HD] = (keys * cos[...] + pltpu.roll(keys, 64, 1) * sin[...]).astype(BF)
    kvg[:, HD : 2 * HD] = grads[:, HD : 2 * HD].astype(BF)
    away = kvg.at[part((1 - c) * 128, 128)]
    crossing = push(away, kvo, k_s.at[0], k_r.at[0], other)
    across = [
        push(kvg.at[toks], kvp.at[0], k_s.at[1], k_r.at[1], peer),
        push(away, kvp.at[1], k_s.at[2], k_r.at[2], peer_other),
    ]

    def outer(n, _):
        rows = part(n * 512, 512)
        wg[rows, :] = dot(hst[rows, :], kvg[...]).astype(BF)
        return 0

    lax.fori_loop(0, 8, outer, 0)

    order = FAR + (0,)

    def leave(i):
        n = i % 2
        push(wg.at[plane(y + 2, z + order[i])], relay.at[i], a_s, l_r.at[i], ys[n])
        push(
            wg.at[plane(y + DY[1 - n], z + order[i])], buf0.at[i, 1 - n],
            a_s, a_r.at[i * 2 + 1 - n], ys[1 - n],
        )

    @pl.when(c == 0)
    def _():
        for i in range(AHEAD):
            leave(i)

    @pl.when(c == 1)
    def _():
        for n, e in enumerate((2, 1, -1, 0)):
            top = 4 if n < 2 else 3
            low = 3 if n < 2 else 4
            push(
                wg.at[plane(y + e, z + top)], plus.at[n, top - 1],
                a_s, a_r.at[n * 4 + top - 1], zs[0],
            )
            push(
                wg.at[plane(y + e, z - low)], minus.at[n, low - 1],
                b_s, b_r.at[n * 4 + low - 1], zs[1],
            )

    crossing.wait_recv()
    weights.wait_recv()

    def hidden(n, _):
        for m in range(2):
            span = part(2048 + n * 1024 + m * 512, 512)
            ph[n, :, m * 512 : (m + 1) * 512] = (
                lax.dot_general(kvg[toks, :], w[span, :], RIGHT, preferred_element_type=F32)
                + lax.dot_general(kvo[...], wo[span, :], RIGHT, preferred_element_type=F32)
            ).astype(BF)
        remote(ph.at[n], h_in.at[n], h_s.at[n], h_r.at[n], peer).start()
        pltpu.make_async_copy(ph.at[n], gh.at[2 + n], out_sem.at[2 + n]).start()
        return 0

    lax.fori_loop(0, 2, hidden, 0)
    for n in range(2):
        lend(n).wait()
    borrowed = push(wp, wpo, wo_s.at[1], wo_r.at[1], other)

    def quarter_to(n):
        return remote(ph.at[2], gh.at[n], h_s.at[2], h_r.at[2], peer)

    keep_quarter = pltpu.make_async_copy(ph.at[2], gh.at[h], out_sem.at[4])

    def quarter():
        borrowed.wait_recv()
        for copy in across:
            copy.wait_recv()
        for m in range(2):
            span = part(h * 1024 + m * 512, 512)
            near = pl.ds(m * 512, 512)
            value = 0.0
            for left, right in (
                (kvg[toks, :], w[span, :]),
                (kvo[...], wo[span, :]),
                (kvp[0], wp[near, :]),
                (kvp[1], wpo[near, :]),
            ):
                value = value + lax.dot_general(left, right, RIGHT, preferred_element_type=F32)
            ph[2, :, m * 512 : (m + 1) * 512] = value.astype(BF)
        quarter_to(h).start()
        keep_quarter.start()


    @pl.when(c == 0)
    def _():
        def pass_row(i, d):
            n = i % 2
            remote(relay.at[i], relay.at[i], a_s, l_r.at[i], other).wait_recv()
            relay[i] = (
                relay[i].astype(F32) + wg[plane(y + DY[n], z + d), :].astype(F32)
            ).astype(BF)
            push(relay.at[i], buf0.at[i, n], a_s, a_r.at[i * 2 + n], ys[n])

        def pass_plane(i, d):
            for n in range(2):
                ref = buf0.at[i, n]
                remote(ref, ref, a_s, a_r.at[i * 2 + n], other).wait_recv()
            value = (
                wg[plane(y, z + d), :].astype(F32)
                + buf0[i, 0].astype(F32)
                + buf0[i, 1].astype(F32)
            )
            if d:
                acc0[i] = value.astype(BF)
                for m in READY.get(i, ()):
                    push(acc0.at[m], zin0.at[m], b_s, b_r.at[m], zs[DZ.index(FAR[m])])
            else:
                total[...] = value

        for i in range(8 + LAG):
            if i < 8:
                pass_row(i, order[i])
            if i + AHEAD < 8:
                leave(i + AHEAD)
            if i >= LAG:
                pass_plane(i - LAG, order[i - LAG])
            if i == 4:
                quarter()
        for i in range(7):
            remote(zin0.at[i], zin0.at[i], b_s, b_r.at[i], other).wait_recv()
            total[...] += zin0[i].astype(F32)

    @pl.when(c == 1)
    def _():
        def step(ref, send, recv, n, m, e, sign, to):
            remote(ref.at[n, m], ref.at[n, m], send, recv.at[n * 4 + m], other).wait_recv()
            if m:
                ref[n, m] = (
                    ref[n, m].astype(F32) + wg[plane(y + e, z + sign * m), :].astype(F32)
                ).astype(BF)
                push(
                    ref.at[n, m], ref.at[n, m - 1],
                    send, recv.at[n * 4 + m - 1], to,
                )

        for m in (3, 2, 1, 0):
            if m == 1:
                quarter()
            for n, e in enumerate((2, 1, -1, 0)):
                top = 4 if n < 2 else 3
                low = 3 if n < 2 else 4
                if m < top:
                    step(plus, a_s, a_r, n, m, e, 1, zs[0])
                if m < low:
                    step(minus, b_s, b_r, n, m, e, -1, zs[1])
                if m == 0:
                    value = (
                        wg[plane(y + e, z), :].astype(F32)
                        + plus[n, 0].astype(F32)
                        + minus[n, 0].astype(F32)
                    )
                    if e:
                        acc1[n] = value.astype(BF)
                        to = DY.index(e)
                        push(acc1.at[n], yin1.at[n], m_s, m_r.at[n], ys[to])
                    else:
                        total[...] = value
        for n in range(3):
            remote(yin1.at[n], yin1.at[n], m_s, m_r.at[n], other).wait_recv()
            total[...] += yin1[n].astype(F32)

    def rows_of(xx, cc):
        return part(xx * 64 + cc * 32, 32)

    finals = [
        push(total.at[rows_of(x, 1 - c)], f_in.at[0], f_s.at[0], f_r.at[0], other),
        push(total.at[rows_of(1 - x, c)], f_in.at[1], f_s.at[1], f_r.at[1], mate),
        push(total.at[rows_of(1 - x, 1 - c)], f_in.at[2], f_s.at[2], f_r.at[2], diag),
    ]

    keep_own = pltpu.make_async_copy(total.at[rows_of(x, c)], own_out, out_sem.at[6])
    keep_own.start()
    crossing.wait_send()
    borrowed.wait_send()
    for copy in across:
        copy.wait_send()
    all_sent(x_in, bx_s, mate)
    all_sent(x_in, bz_s, down1)

    @pl.when(c == 0)
    def _():
        all_sent(wg.at[pl.ds(0, 24 * 128)], a_s, other)
        all_sent(zin0, b_s, other)

    @pl.when(c == 1)
    def _():
        all_sent(wg.at[pl.ds(0, 14 * 128)], a_s, other)
        all_sent(wg.at[pl.ds(0, 14 * 128)], b_s, other)
        all_sent(yin1, m_s, other)

    for copy in finals:
        copy.wait()
    keep_own.wait()
    for n in range(2):
        remote(ph.at[n], h_in.at[n], h_s.at[n], h_r.at[n], peer).wait()
        pltpu.make_async_copy(ph.at[n], gh.at[2 + n], out_sem.at[2 + n]).wait()
    quarter_to(h).wait_send()
    quarter_to(1 - h).wait_recv()
    keep_quarter.wait()


def run(wk, wv, hid, q, do, seg, table):
    dma = pltpu.SemaphoreType.DMA
    shape = jax.ShapeDtypeStruct

    def bf(*dims):
        return pltpu.VMEM(dims, BF)

    def f32(*dims):
        return pltpu.VMEM(dims, F32)

    buffers = [
        pltpu.VMEM((128, 128), jnp.int32), f32(640, 128),
        f32(256, 128), f32(256, 128), f32(16, 1024),
        bf(2, 32, 256), bf(4096, 256), bf(4096, 256), bf(1024, 256), bf(1024, 256), bf(256, 4096), bf(4096, 256),
        bf(128, 512), bf(128, 512), bf(128, 512), bf(128, 512), bf(2, 2560, 128),
        bf(1024, 128), bf(1024, 128), bf(128, 1024), bf(128, 1024), f32(2304, 1024),
        bf(9, 256, 256), bf(2, 128, 512), bf(2, 128, 512),
        bf(4, 256, 256), bf(5, 256, 256), bf(5, 256, 256), bf(256, 256), bf(128, 256), bf(2, 128, 256),
        bf(4096, 256), bf(3, 128, 1024),
        bf(8, 128, 256), bf(8, 2, 128, 256), bf(7, 128, 256), bf(7, 128, 256),
        bf(4, 4, 128, 256), bf(4, 4, 128, 256), bf(3, 128, 256), bf(3, 128, 256),
        f32(128, 256),
    ]
    counts = [
        0, 3, 0, 32, 0, 0, 2, 2, 5, 5, 2, 2, 0, 16, 0, 4, 0, 16,
        0, 16, 3, 3, 3, 3, 8, 0, 16, 0, 16, 0, 3, 3, 3, 3, 7, 6,
    ]
    return pl.pallas_call(
        kernel,
        out_shape=(
            shape((128, 1024), BF),
            shape((128, 1024), BF),
            shape((4, 128, 1024), BF),
            shape((2, 128, 1024), BF),
            shape((32, 256), F32),
            shape((3, 32, 256), F32),
        ),
        in_specs=[ANY] * 7,
        out_specs=(ANY,) * 6,
        scratch_shapes=buffers + [dma((n,)) if n else dma for n in counts],
        compiler_params=pltpu.CompilerParams(
            collective_id=0, has_side_effects=True, vmem_limit_bytes=60 * 2**20
        ),
        name="layer",
    )(wk, wv, hid, q, do, seg, table)


def last_kernel(
    att_in, gq_in, ph_in, h_in, own_in, f_in, att, gq, gh, gk, gv,
    ph, hb, at, qt, own, f, gkb, gvb, sem_in, sem_out
):
    def load(src, dst, n):
        copy = pltpu.make_async_copy(src, dst, sem_in.at[n])
        copy.start()
        return copy

    def store(src, dst, n):
        copy = pltpu.make_async_copy(src, dst, sem_out.at[n])
        copy.start()
        return copy

    parts = [
        (load(ph_in.at[n], ph.at[n], n),) + ((load(h_in.at[n - 2], hb.at[n - 2], 4 + n),) if n > 1 else ())
        for n in range(4)
    ]
    small = [load(own_in, own, 8), load(f_in, f, 9)]
    whole = [load(att_in, at, 10), load(gq_in, qt, 11)]
    stores = []
    for n in range(4):
        for copy in parts[n]:
            copy.wait()
        if n > 1:
            ph[n] = (ph[n].astype(F32) + hb[n - 2].astype(F32)).astype(BF)
        stores.append(store(ph.at[n], gh.at[:, pl.ds(n * 1024, 1024)], n))
    for n, (copy, src, dst) in enumerate(((whole[0], at, att), (whole[1], qt, gq))):
        copy.wait()
        stores.append(store(src, dst, 4 + n))
    for copy in small:
        copy.wait()
    c = lax.axis_index("ctx") % 2
    here = own[...] + f[1]
    there = f[0] + f[2]
    for n in range(2):
        @pl.when(c == n)
        def _():
            for first, value in ((n, here), (1 - n, there)):
                gkb[:, first * HD : (first + 1) * HD] = value[:, 0:HD]
                gvb[:, first * HD : (first + 1) * HD] = value[:, HD : 2 * HD]

    stores += [store(gkb, gk, 6), store(gvb, gv, 7)]
    for copy in stores:
        copy.wait()


def last(*parts):
    dma = pltpu.SemaphoreType.DMA
    results = (
        jax.ShapeDtypeStruct((128, 1024), BF),
        jax.ShapeDtypeStruct((128, 1024), BF),
        jax.ShapeDtypeStruct((128, 4096), BF),
        jax.ShapeDtypeStruct((32, 256), F32),
        jax.ShapeDtypeStruct((32, 256), F32),
    )
    return pl.pallas_call(
        last_kernel,
        out_shape=results,
        in_specs=[ANY] * 6,
        out_specs=(ANY,) * 5,
        scratch_shapes=[
            pltpu.VMEM((4, 128, 1024), BF),
            pltpu.VMEM((2, 128, 1024), BF),
            pltpu.VMEM((128, 1024), BF),
            pltpu.VMEM((128, 1024), BF),
            pltpu.VMEM((32, 256), F32),
            pltpu.VMEM((3, 32, 256), F32),
            pltpu.VMEM((32, 256), F32),
            pltpu.VMEM((32, 256), F32),
            dma((12,)),
            dma((8,)),
        ],
        compiler_params=pltpu.CompilerParams(vmem_limit_bytes=60 * 2**20),
        name="last",
    )(*parts)


def tables():
    frequency = 10000.0 ** (-(np.arange(64) * 2.0 / HD))
    first = (np.arange(64) * 256)[:, None] * frequency[None, :]
    within = np.arange(256)[:, None] * frequency[None, :]
    both = np.concatenate([np.cos(first), np.sin(first), np.cos(within), np.sin(within)])
    return jnp.asarray(np.concatenate([both, both], axis=1), F32)


def body(hidden_in, queries, key_weight, value_weight, seg_ids, grad_out):
    seg = seg_ids.reshape(128, 128)
    return last(*run(key_weight, value_weight, hidden_in, queries, grad_out, seg, tables()))


def solution(mesh):
    placed = (
        P("ctx", None),
        P("ctx", "head"),
        P("ctx", "head"),
        P("ctx", "head"),
        P(),
        P("ctx", "head"),
    )
    return jax.shard_map(
        body,
        mesh=mesh,
        in_specs=placed,
        out_specs=(
            P("ctx", "head"),
            P("ctx", "head"),
            P("ctx", None),
            P("ctx", "head"),
            P("ctx", "head"),
        ),
        check_vma=False,
    )
```
